128 devices in a mesh: cp: 32 (over z, y_hi, x), tp: 4 (over y_lo, core).
Axes of the slice: x: 4, y: 4 (y_hi: 2, y_lo: 2; y = y_hi * 2 + y_lo), z: 4, core: 2. Of those that a mesh axis runs over, the one named last changes fastest.
Arguments:
- queries: bfloat16 [256, 128, 128], P('cp', 'tp'), may hold values from -32 to 32
- keys: bfloat16 [65536, 8, 128], P('cp', 'tp'), may hold values from -24 to 24
- values: bfloat16 [65536, 8, 128], P('cp', 'tp'), may hold values from -12 to 12
- lengths: int32 [32], P('cp'), may hold values from 1024 to 2048
- start: int32 [1], replicated, may hold values from 32512 to 65280
- out_weight: bfloat16 [16384, 16384], P('tp', 'cp'), may hold values from -0.046875 to 0.046875
Outputs:
- projected: bfloat16 [256, 16384], P('tp', 'cp')
The draws below stay inside these ranges and needn't reach their ends.
All inputs are finite; a program needn't handle non-finite values.
Results may differ from the reference program's by a relative error of at most 0.0065.
Values may be sent and summed in bfloat16 or wider, within the bound.
No kernel may reach another device: no remote copies, remote signals or barrier semaphores. Data moves between devices by JAX's collectives and lax.ppermute only.
A program may use at most 64 MiB of HBM per device.

```python
import math
import jax
import jax.numpy as jnp
from jax import lax

D = 16384
H = 128
KVH = 8
DH = 128
S_DEV = 2048
QROWS = 256
KV = 65536
SHARDS = 32


def draw_queries(key, part):
    key = jax.random.fold_in(key, 11)
    drawn = 3.0 * jax.random.normal(key, (QROWS, H, DH), jnp.float32)
    return jnp.clip(drawn, -32.0, 32.0).astype(jnp.bfloat16)


def draw_keys(key, part):
    key = jax.random.fold_in(key, 23)
    drawn = jax.random.normal(key, (KV, KVH, DH), jnp.float32)
    return jnp.clip(drawn, -24.0, 24.0).astype(jnp.bfloat16)


def touch_ends(result, own_key, least, top_value):
    place = [jax.random.randint(jax.random.fold_in(own_key, axis), (), 0, length) for axis, length in enumerate(result.shape)]
    longest = result.shape.index(max(result.shape))
    neighbour = place[:longest] + [(place[longest] + 1) % result.shape[longest]] + place[longest + 1:]
    return result.at[tuple(place)].set(least).at[tuple(neighbour)].set(top_value)


def block_scale(own_key, shape, split, least, high):
    gain, own = 1.0, jax.random.fold_in(own_key, 6)
    for axis_at, shards_of in split:
        heights = jnp.exp(jax.random.uniform(jax.random.fold_in(own, axis_at), (shards_of,), jnp.float32, least / len(split), high / len(split)))
        gain = gain * jnp.repeat(heights, shape[axis_at] // shards_of).reshape([-1 if axis == axis_at else 1 for axis in range(len(shape))])
    return gain


def noise(own_key, extent, width, limit, shards=(), held_as=jnp.bfloat16):
    values = jax.random.normal(own_key, extent, jnp.float32) * width
    if len(shards) > 0:
        values = block_scale(own_key, extent, shards, -0.22, 0.18) * values
    return jnp.clip(values, min=-limit, max=limit).astype(held_as)


def setup_inputs(seed: int = 0) -> dict:
    key_of = jax.random.split(jax.random.key(seed), 7)
    return {
        "queries": draw_queries(jax.random.fold_in(key_of[6], 71), 0),
        "keys": draw_keys(jax.random.fold_in(key_of[6], 71), 0),
        "values": noise(key_of[2], (KV, KVH, DH), 2.0, 12.0, ((0, 32), (1, 4))),
        "lengths": touch_ends(jax.random.randint(key_of[3], (SHARDS,), S_DEV // 2, S_DEV + 1), jax.random.fold_in(key_of[3], 1), S_DEV // 2, S_DEV).astype(jnp.int32),
        "start": jax.random.randint(key_of[4], (1,), KV // 2 - QROWS, KV - QROWS + 1).astype(jnp.int32),
        "out_weight": noise(key_of[5], (H * DH, D), (H * DH) ** -0.5, 0.046875, ((0, 4), (1, 32))),
    }


NEG = -1e+30

def combine(earlier, later):
    numer_a, peak_a, total_a = earlier
    numer_b, peak_b, total_b = later
    joined = jnp.maximum(peak_a, peak_b)
    rescale_a = jnp.exp(peak_a - joined)
    rescale_b = jnp.exp(peak_b - joined)
    return (numer_a * rescale_a[..., None] + numer_b * rescale_b[..., None], joined, total_a * rescale_a + total_b * rescale_b)

def shard_partial(grouped, keys_here, values_here, visible, score_scale):

    def per_head(triple):
        query_head, key_head, value_head = triple
        scores = jnp.einsum('rgd,sd->rgs', query_head, key_head) * score_scale
        masked = visible[:, None, :]
        scores = jnp.where(masked, scores, NEG)
        row_max = lax.optimization_barrier(jnp.max(scores, axis=-1))
        exp_terms = jnp.where(masked, jnp.exp(scores - row_max[..., None]), 0.0)
        exp_total = lax.optimization_barrier(jnp.sum(exp_terms, axis=-1))
        weights = exp_terms.astype(jnp.bfloat16).astype(jnp.float32)
        numer = jnp.einsum('rgs,sd->rgd', weights, value_head)
        return (numer, row_max, exp_total)
    numer, row_max, exp_total = lax.map(per_head, (grouped.transpose(1, 0, 2, 3), keys_here.transpose(1, 0, 2), values_here.transpose(1, 0, 2)))
    return (numer.transpose(1, 0, 2, 3), row_max.transpose(1, 0, 2), exp_total.transpose(1, 0, 2))

def reference(queries, keys, values, lengths, start, out_weight):
    row_len, head_count, head_dim = queries.shape
    kv_heads = keys.shape[1]
    group_size = head_count // kv_heads
    shard_count = lengths.shape[0]
    key_span = keys.shape[0] // shard_count
    score_scale = 1.0 / math.sqrt(head_dim)
    grouped = queries.astype(jnp.float32).reshape(row_len, kv_heads, group_size, head_dim)
    query_pos = start[0] + jnp.arange(row_len, dtype=jnp.int32)
    slot_ids = jnp.arange(key_span, dtype=jnp.int32)

    def absorb(running, shard_index):
        first_slot = (shard_index * key_span).astype(jnp.int32)
        keys_here = lax.dynamic_slice_in_dim(keys, first_slot, key_span, 0).astype(jnp.float32)
        values_here = lax.dynamic_slice_in_dim(values, first_slot, key_span, 0).astype(jnp.float32)
        key_pos = first_slot + slot_ids
        visible = (slot_ids < lengths[shard_index])[None, :] & (key_pos[None, :] <= query_pos[:, None])
        fresh = shard_partial(grouped, keys_here, values_here, visible, score_scale)
        return (combine(running, fresh), None)
    initial = (jnp.zeros((row_len, kv_heads, group_size, head_dim), jnp.float32), jnp.full((row_len, kv_heads, group_size), NEG, jnp.float32), jnp.zeros((row_len, kv_heads, group_size), jnp.float32))
    merged, _ = lax.scan(absorb, initial, jnp.arange(shard_count, dtype=jnp.int32))
    numer, peak_vals, totals = merged
    attn = (numer / totals[..., None]).astype(jnp.bfloat16).reshape(row_len, head_count * head_dim)
    return jnp.dot(attn, out_weight, preferred_element_type=jnp.float32).astype(jnp.bfloat16)
```

```python
import functools
import itertools
import math

import jax
import jax.numpy as jnp
from jax import lax
from jax.experimental import pallas as pl
from jax.experimental.pallas import tpu as pltpu
from jax.sharding import PartitionSpec as P

NEG = -1e30
BIG = 2.0**100
RING = 4
MIB = 2**20


def coords(cp, tp):
    z, yh, x = cp // 8, (cp // 4) % 2, cp % 4
    yl, core = tp // 2, tp % 2
    return z, yh, x, yl, core


def moved(x, a=0, b=0, yh=0, yl=0, core=0):
    pairs = []
    for cp, tp in itertools.product(range(32), range(4)):
        zi, yhi, xi, yli, ci = coords(cp, tp)
        dz, dx = (a, b) if ci == 0 else (b, a)
        zo, xo = (zi + dz) % RING, (xi + dx) % RING
        yho, ylo, co = yhi ^ yh, yli ^ yl, ci ^ core
        pairs.append((cp * 4 + tp, ((zo * 2 + yho) * 4 + xo) * 4 + ylo * 2 + co))
    return lax.ppermute(x, ("cp", "tp"), pairs)


def source(me, da, db, dy):
    z, yh, x, _, core = me
    dz = jnp.where(core == 0, da, db)
    dx = jnp.where(core == 0, db, da)
    return (z - dz + RING) % RING, yh ^ dy, (x - dx + RING) % RING


def spread(row, eye):
    return jnp.sum(jnp.where(eye, row, 0.0), axis=1, keepdims=True)


def gathered_row(column, eye):
    return jnp.sum(jnp.where(eye, column, 0.0), axis=0, keepdims=True)


def diagonal():
    shape = (128, 128)
    return lax.broadcasted_iota(jnp.int32, shape, 0) == lax.broadcasted_iota(jnp.int32, shape, 1)


def stat_rows(m, l):
    high = l.astype(jnp.bfloat16).astype(jnp.float32)
    return jnp.concatenate([m, high, l - high, jnp.zeros((5, 128), jnp.float32)], axis=0)


def attend_kernel(me_ref, len_ref, start_ref, q_ref, k_ref, v_ref, o_ref, vx, *, db, nb, nkv, span, tile, scale):
    step = pl.program_id(0)
    rows = nb * 128
    length = len_ref[0]
    me = tuple(me_ref[i] for i in range(5))
    shard = (me[0] * 2 + me[1]) * 4 + me[2]

    @pl.when(step == 0)
    def _():
        live = lax.broadcasted_iota(jnp.int32, (span, 128), 0) < length
        for kv in range(nkv):
            vx[kv, :, :128] = jnp.where(live, v_ref[kv], jnp.zeros((), jnp.bfloat16))
            vx[kv, :, 128:] = jnp.where(live, 1.0, 0.0).astype(jnp.bfloat16)

    lims = []
    for b in range(nb):
        blk = step * nb + b
        z, yh, x = source(me, blk // 2, db, blk % 2)
        lims.append(start_ref[0] + z * 64 + yh * 32 + x * 8 + 1 - shard * span)
    lo = functools.reduce(jnp.minimum, lims)
    hi = functools.reduce(jnp.maximum, lims) + 7
    eye = diagonal()
    tok = lax.broadcasted_iota(jnp.int32, (128, 1), 0) & 7

    def limit():
        return jnp.concatenate([lims[b] + tok for b in range(nb)], axis=0)

    def scores(kv, t, width):
        q = q_ref[:, kv].reshape(rows, 128)
        return lax.dot_general(
            q, k_ref[kv, pl.ds(t, width), :], (((1,), (1,)), ((), ())), preferred_element_type=jnp.float32
        )

    def weigh(p, kv, t, width):
        return jnp.dot(p.astype(jnp.bfloat16), vx[kv, pl.ds(t, width), :], preferred_element_type=jnp.float32)

    def put(results):
        for b in range(nb):
            r = slice(b * 128, (b + 1) * 128)
            stats = []
            for kv, (m, acc) in enumerate(results):
                o_ref[b, kv * 128 : (kv + 1) * 128, :] = acc[r, :128].astype(jnp.bfloat16)
                stats.append(stat_rows(gathered_row(m[r], eye), gathered_row(acc[r, 128:], eye)))
            o_ref[b, nkv * 128 :, :] = jnp.concatenate(stats, axis=0).astype(jnp.bfloat16)

    def rounded(m):
        return m.astype(jnp.bfloat16).astype(jnp.float32)

    def quick(masked):
        ok = []
        results = []
        lim = limit() if masked else None
        col = lax.broadcasted_iota(jnp.int32, (1, tile), 1)
        for kv in range(nkv):
            first = scores(kv, 0, tile)
            if masked:
                m = jnp.max(jnp.where(col < lim, first, NEG), axis=1, keepdims=True)
                m = jnp.where(lim > 0, m * scale, NEG)
            else:
                m = jnp.max(first, axis=1, keepdims=True) * scale
            m = rounded(m)
            acc = None
            for t in range(0, span, tile):
                s = first if t == 0 else scores(kv, t, tile)
                p = jnp.exp2(s * scale - m)
                if masked:
                    p = jnp.where(col + t < lim, p, 0.0)
                d = weigh(p, kv, t, tile)
                acc = d if acc is None else acc + d
            ok.append(jnp.min(jnp.where(acc[:, 128:] < BIG, 1.0, 0.0)))
            results.append((m, acc))
        put(results)
        return functools.reduce(jnp.minimum, ok) > 0.5

    def careful():
        lim = jnp.minimum(limit(), length)
        col = lax.broadcasted_iota(jnp.int32, (1, tile), 1)
        results = []
        for kv in range(nkv):

            def top(i, m):
                t = pl.multiple_of(i * tile, tile)
                s = jnp.where(col + t < lim, scores(kv, t, tile) * scale, NEG)
                return jnp.maximum(m, jnp.max(s, axis=1, keepdims=True))

            m = rounded(lax.fori_loop(0, span // tile, top, jnp.full((rows, 1), NEG, jnp.float32)))

            def add(i, acc):
                t = pl.multiple_of(i * tile, tile)
                p = jnp.where(col + t < lim, jnp.exp2(scores(kv, t, tile) * scale - m), 0.0)
                return acc + weigh(p, kv, t, tile)

            acc = lax.fori_loop(0, span // tile, add, jnp.zeros((rows, 256), jnp.float32))
            results.append((m, acc))
        put(results)

    def run(masked):
        ok = quick(masked)

        @pl.when(jnp.logical_not(ok))
        def _():
            careful()

    pl.when(lo >= length)(lambda: run(False))
    pl.when((lo < length) & (hi > 0))(lambda: run(True))

    @pl.when((lo < length) & (hi <= 0))
    def _():
        o_ref[:, : nkv * 128, :] = jnp.zeros((nb, nkv * 128, 128), jnp.bfloat16)
        row = lax.broadcasted_iota(jnp.int32, (nb, nkv * 8, 128), 1)
        o_ref[:, nkv * 128 :, :] = jnp.where((row & 7) == 0, NEG, 0.0).astype(jnp.bfloat16)


def attend(me, lengths, start, q, k, v, db):
    blocks, nkv = q.shape[:2]
    span = v.shape[1]
    nb, tile = 4, 256
    out_rows = nkv * 136
    smem = pl.BlockSpec(memory_space=pltpu.SMEM)
    return pl.pallas_call(
        functools.partial(
            attend_kernel, db=db, nb=nb, nkv=nkv, span=span, tile=tile, scale=math.log2(math.e) / math.sqrt(128)
        ),
        grid=(blocks // nb,),
        in_specs=[
            smem,
            smem,
            smem,
            pl.BlockSpec((nb, nkv, 128, 128), lambda i: (i, 0, 0, 0)),
            pl.BlockSpec(k.shape, lambda i: (0, 0, 0)),
            pl.BlockSpec(v.shape, lambda i: (0, 0, 0)),
        ],
        out_specs=pl.BlockSpec((nb, out_rows, 128), lambda i: (i, 0, 0)),
        out_shape=jax.ShapeDtypeStruct((blocks, out_rows, 128), jnp.bfloat16),
        scratch_shapes=[pltpu.VMEM((nkv, span, 256), jnp.bfloat16)],
        compiler_params=pltpu.CompilerParams(vmem_limit_bytes=24 * MIB, dimension_semantics=("arbitrary",)),
        cost_estimate=pl.CostEstimate(
            flops=8 * blocks * nkv * 128 * span * 128, bytes_accessed=4 * MIB, transcendentals=blocks * nkv * 128 * span
        ),
        name="attend_plane",
    )(me, lengths, start, q, k, v)


def merged(parts, b, kv, nkv, eye):
    base = nkv * 128 + kv * 8
    stats = [p[b, nkv * 128 :, :].astype(jnp.float32)[kv * 8 : kv * 8 + 8] for p in parts]
    m = functools.reduce(jnp.maximum, [s[0:1] for s in stats])
    total = jnp.zeros((1, 128), jnp.float32)
    out = jnp.zeros((128, 128), jnp.float32)
    for p, s in zip(parts, stats):
        factor = jnp.exp2(s[0:1] - m)
        total = total + factor * (s[1:2] + s[2:3])
        out = out + spread(factor, eye) * p[b, kv * 128 : (kv + 1) * 128, :].astype(jnp.float32)
    return out, m, total


def combine_kernel(*refs, nkv):
    parts, o_ref = refs[:-1], refs[-1]
    eye = diagonal()
    for b in range(o_ref.shape[0]):
        stats = []
        for kv in range(nkv):
            out, m, total = merged(parts, b, kv, nkv, eye)
            o_ref[b, kv * 128 : (kv + 1) * 128, :] = out.astype(jnp.bfloat16)
            stats.append(stat_rows(m, total))
        o_ref[b, nkv * 128 :, :] = jnp.concatenate(stats, axis=0).astype(jnp.bfloat16)


def combine(parts, nkv):
    return pl.pallas_call(
        functools.partial(combine_kernel, nkv=nkv),
        out_shape=jax.ShapeDtypeStruct(parts[0].shape, jnp.bfloat16),
        compiler_params=pltpu.CompilerParams(vmem_limit_bytes=16 * MIB),
        name="combine",
    )(*parts)


def finish_kernel(*refs, nkv):
    parts, o_ref = refs[:-1], refs[-1]
    eye = diagonal()
    for kv in range(nkv):
        out, _, total = merged(parts, 0, kv, nkv, eye)
        attn = (out * spread(1.0 / total, eye)).astype(jnp.bfloat16)
        for h in range(16):
            c = (kv * 16 + h) * 128
            o_ref[:, c : c + 128] = attn[h * 8 : (h + 1) * 8, :]


def finish(parts, nkv):
    return pl.pallas_call(
        functools.partial(finish_kernel, nkv=nkv),
        out_shape=jax.ShapeDtypeStruct((8, nkv * 2048), jnp.bfloat16),
        name="finish",
    )(*parts)


def project_kernel(me_ref, x0, x1, x2, x3, w_ref, o_ref):
    me = tuple(me_ref[i] for i in range(5))
    yl, core = me[3], me[4]
    x = jnp.concatenate([r[...] for r in (x0, x1, x2, x3)], axis=0)
    y = jnp.dot(x, w_ref[...], preferred_element_type=jnp.float32)
    for db, da, dy in itertools.product(range(RING), range(RING), range(2)):
        z, yh, xx = source(me, da, db, dy)
        row = (((z % 2) ^ core) * 2 + ((z // 2) ^ yl)) * 64 + yh * 32 + xx * 8
        at = (db * RING + da) * 16 + dy * 8
        o_ref[pl.ds(pl.multiple_of(row, 8), 8), :] = y[at : at + 8, :]


def project(me, planes, w):
    rows = sum(p.shape[0] for p in planes)
    vmem = pl.BlockSpec(memory_space=pltpu.VMEM)
    return pl.pallas_call(
        project_kernel,
        in_specs=[pl.BlockSpec(memory_space=pltpu.SMEM)] + [vmem] * 5,
        out_specs=vmem,
        out_shape=jax.ShapeDtypeStruct((rows, w.shape[1]), jnp.float32),
        compiler_params=pltpu.CompilerParams(vmem_limit_bytes=24 * MIB),
        name="project",
    )(me, *planes, w)


def on_device(queries, keys, values, lengths, start, out_weight):
    nkv = keys.shape[1]
    me = jnp.stack(coords(lax.axis_index("cp"), lax.axis_index("tp"))).astype(jnp.int32)
    k = keys.transpose(1, 0, 2)
    v = values.transpose(1, 0, 2)
    q = queries.reshape(8, nkv, 16, 128).transpose(1, 2, 0, 3).reshape(1, nkv, 128, 128)

    def gather_plane(x):
        x = jnp.concatenate([x, moved(x, yh=1)], axis=0)
        return jnp.concatenate([x] + [moved(x, a=d) for d in (1, 2, 3)], axis=0)

    q = gather_plane(q)
    planes = {0: q}
    for d in (1, 3, 2):
        planes[d] = moved(q, b=d)
    parts = []
    for d in (0, 1, 3, 2):
        part = attend(me, lengths, start, planes[d], k, v, d)
        parts.append(moved(part, b=-d) if d else part)
    c = combine(parts, nkv)
    c = combine([c[:2]] + [moved(c[2 * d : 2 * d + 2], a=-d) for d in (1, 3, 2)], nkv)
    attn = finish([c[:1], moved(c[1:], yh=1)], nkv)
    attn = gather_plane(attn)
    rows = [attn] + [moved(attn, b=d) for d in (1, 2, 3)]
    y = project(me, rows, out_weight)
    y = y[:128] + moved(y[128:], core=1)
    y = y[:64] + moved(y[64:], yl=1)
    return y.astype(jnp.bfloat16)


def solution(mesh):
    in_specs = (
        P("cp", "tp", None),
        P("cp", "tp", None),
        P("cp", "tp", None),
        P("cp"),
        P(),
        P("tp", "cp"),
    )
    return jax.shard_map(on_device, mesh=mesh, in_specs=in_specs, out_specs=P("tp", "cp"), check_vma=False)
```

```python
import functools
import itertools
import math

import jax
import jax.numpy as jnp
from jax import lax
from jax.experimental import pallas as pl
from jax.experimental.pallas import tpu as pltpu
from jax.sharding import PartitionSpec as P

NEG = -1e30
BIG = 2.0**100
RING = 4
MIB = 2**20


def coords(cp, tp):
    z, yh, x = cp // 8, (cp // 4) % 2, cp % 4
    yl, core = tp // 2, tp % 2
    return z, yh, x, yl, core


def moved(x, a=0, b=0, yh=0, yl=0, core=0):
    pairs = []
    for cp, tp in itertools.product(range(32), range(4)):
        zi, yhi, xi, yli, ci = coords(cp, tp)
        dz, dx = (a, b) if ci == 0 else (b, a)
        zo, xo = (zi + dz) % RING, (xi + dx) % RING
        yho, ylo, co = yhi ^ yh, yli ^ yl, ci ^ core
        pairs.append((cp * 4 + tp, ((zo * 2 + yho) * 4 + xo) * 4 + ylo * 2 + co))
    return lax.ppermute(x, ("cp", "tp"), pairs)


def after(x, *earlier):
    return lax.optimization_barrier((x, *earlier))[0]


def source(me, da, db, dy):
    z, yh, x, _, core = me
    dz = jnp.where(core == 0, da, db)
    dx = jnp.where(core == 0, db, da)
    return (z - dz) & (RING - 1), yh ^ dy, (x - dx) & (RING - 1)


def spread(row, eye):
    return jnp.sum(jnp.where(eye, row, 0.0), axis=1, keepdims=True)


def gathered_row(column, eye):
    return jnp.sum(jnp.where(eye, column, 0.0), axis=0, keepdims=True)


def diagonal():
    shape = (128, 128)
    return lax.broadcasted_iota(jnp.int32, shape, 0) == lax.broadcasted_iota(jnp.int32, shape, 1)


def stat_rows(m, l):
    high = l.astype(jnp.bfloat16).astype(jnp.float32)
    return jnp.concatenate([m, high, l - high, jnp.zeros((13, 128), jnp.float32)], axis=0).astype(jnp.bfloat16)


def attend_kernel(me_ref, len_ref, start_ref, q_ref, k_ref, v_ref, o_ref, vx, kx, *, db, kvs, nb, span, tile, scale):
    step = pl.program_id(0)
    rows = nb * 128

    @pl.when(step == 0)
    def _():
        me = tuple(me_ref[i] for i in range(5))
        shard = (me[0] * 2 + me[1]) * 4 + me[2]
        lane = lax.broadcasted_iota(jnp.int32, (1, 128), 1)
        z, yh, x = source(me, lane >> 4, db, (lane >> 3) & 1)
        seen = start_ref[0] + z * 64 + yh * 32 + x * 8 + (lane & 7) + 1 - shard * span
        seen = jnp.minimum(seen, len_ref[0])
        slot = lax.broadcasted_iota(jnp.int32, (span, 128), 0)
        mask = jnp.where((slot >= seen) & (lane < 64), NEG, 0.0).astype(jnp.bfloat16)
        for i, kv in enumerate(kvs):
            kx[i, :, :128] = k_ref[kv]
            kx[i, :, 128:] = mask
            vx[i, :, :128] = v_ref[kv]
            vx[i, :, 128:] = jnp.ones((span, 128), jnp.bfloat16)

    eye = diagonal()
    row = lax.broadcasted_iota(jnp.int32, (rows, 128), 0)
    lane = lax.broadcasted_iota(jnp.int32, (rows, 128), 1)
    hot = jnp.where(lane == (step * nb + (row >> 7)) * 8 + (row & 7), 1.0, 0.0).astype(jnp.bfloat16)

    def scores(i, t):
        q = jnp.concatenate([q_ref[:, kvs[i]].reshape(rows, 128), hot], axis=1)
        return lax.dot_general(
            q, kx[i, pl.ds(t, tile), :], (((1,), (1,)), ((), ())), preferred_element_type=jnp.float32
        )

    def point(m):
        return jnp.maximum(m * scale, 0.01 * NEG).astype(jnp.bfloat16).astype(jnp.float32)

    def put(i, m, acc):
        for b in range(nb):
            r = slice(b * 128, (b + 1) * 128)
            o_ref[b, i, :128, :] = acc[r, :128].astype(jnp.bfloat16)
            o_ref[b, i, 128:, :] = stat_rows(gathered_row(m[r], eye), gathered_row(acc[r, 128:], eye))

    ok = []
    for i in range(len(kvs)):
        first = scores(i, 0)
        m = point(jnp.max(first, axis=1, keepdims=True))
        p = []
        for t in range(0, span, tile):
            s = first if t == 0 else scores(i, t)
            p.append(jnp.exp2(s * scale - m).astype(jnp.bfloat16))
        acc = jnp.dot(jnp.concatenate(p, axis=1), vx[i], preferred_element_type=jnp.float32)
        ok.append(jnp.min(jnp.where(acc[:, 128:] < BIG, 1.0, 0.0)))
        put(i, m, acc)

    @pl.when(functools.reduce(jnp.minimum, ok) < 0.5)
    def _():
        for i in range(len(kvs)):

            def top(n, m):
                s = scores(i, pl.multiple_of(n * tile, tile))
                return jnp.maximum(m, jnp.max(s, axis=1, keepdims=True))

            m = point(lax.fori_loop(0, span // tile, top, jnp.full((rows, 1), NEG, jnp.float32)))

            def add(n, acc):
                t = pl.multiple_of(n * tile, tile)
                p = jnp.exp2(scores(i, t) * scale - m).astype(jnp.bfloat16)
                return acc + jnp.dot(p, vx[i, pl.ds(t, tile), :], preferred_element_type=jnp.float32)

            put(i, m, lax.fori_loop(0, span // tile, add, jnp.zeros((rows, 256), jnp.float32)))


def attend(me, lengths, start, q, k, v, db, kvs):
    blocks = q.shape[0]
    span = v.shape[1]
    nb, tile = 8 // len(kvs), 256
    smem, vmem = pl.BlockSpec(memory_space=pltpu.SMEM), pl.BlockSpec(memory_space=pltpu.VMEM)
    return pl.pallas_call(
        functools.partial(
            attend_kernel, db=db, kvs=kvs, nb=nb, span=span, tile=tile, scale=math.log2(math.e) / math.sqrt(128)
        ),
        grid=(blocks // nb,),
        in_specs=[smem, smem, smem, pl.BlockSpec((nb, *q.shape[1:]), lambda i: (i, 0, 0, 0)), vmem, vmem],
        out_specs=pl.BlockSpec((nb, len(kvs), 144, 128), lambda i: (i, 0, 0, 0)),
        out_shape=jax.ShapeDtypeStruct((blocks, len(kvs), 144, 128), jnp.bfloat16),
        scratch_shapes=[pltpu.VMEM((len(kvs), span, 256), jnp.bfloat16)] * 2,
        compiler_params=pltpu.CompilerParams(vmem_limit_bytes=28 * MIB, dimension_semantics=("arbitrary",)),
        cost_estimate=pl.CostEstimate(
            flops=8 * blocks * len(kvs) * 128 * span * 128,
            bytes_accessed=4 * MIB,
            transcendentals=blocks * len(kvs) * 128 * span,
        ),
        name="attend_plane",
    )(me, lengths, start, q, k, v)


def merged(parts, eye):
    stats = [p[128:, :].astype(jnp.float32) for p in parts]
    m = functools.reduce(jnp.maximum, [s[0:1] for s in stats])
    total = jnp.zeros((1, 128), jnp.float32)
    out = jnp.zeros((128, 128), jnp.float32)
    for p, s in zip(parts, stats):
        factor = jnp.exp2(s[0:1] - m)
        total = total + factor * (s[1:2] + s[2:3])
        out = out + spread(factor, eye) * p[:128, :].astype(jnp.float32)
    return out, m, total


def combine_kernel(*refs):
    parts, o_ref = refs[:-1], refs[-1]
    eye = diagonal()
    for b, kv in itertools.product(range(o_ref.shape[0]), range(o_ref.shape[1])):
        out, m, total = merged([p[b, kv] for p in parts], eye)
        o_ref[b, kv, :128, :] = out.astype(jnp.bfloat16)
        o_ref[b, kv, 128:, :] = stat_rows(m, total)


def combine(parts):
    return pl.pallas_call(
        combine_kernel,
        out_shape=jax.ShapeDtypeStruct(parts[0].shape, jnp.bfloat16),
        compiler_params=pltpu.CompilerParams(vmem_limit_bytes=16 * MIB),
        name="combine",
    )(*parts)


def finish_kernel(mine, theirs, o_ref):
    eye = diagonal()
    for kv in range(mine.shape[1]):
        attn = []
        for dy in range(2):
            out, _, total = merged([mine[dy, kv], theirs[1 - dy, kv]], eye)
            attn.append((out * spread(1.0 / total, eye)).astype(jnp.bfloat16))
        for h in range(16):
            c = (kv * 16 + h) * 128
            o_ref[:, c : c + 128] = jnp.concatenate([a[h * 8 : (h + 1) * 8, :] for a in attn], axis=0)


def finish(mine, theirs):
    return pl.pallas_call(
        finish_kernel,
        out_shape=jax.ShapeDtypeStruct((16, mine.shape[1] * 2048), jnp.bfloat16),
        name="finish",
    )(mine, theirs)


def project_kernel(me_ref, x0, x1, x2, x3, w_ref, o_ref, acc):
    step = pl.program_id(0)
    x = jnp.concatenate([r[...] for r in (x0, x1, x2, x3)], axis=0)
    y = jnp.dot(x, w_ref[...], preferred_element_type=jnp.float32)

    @pl.when(step == 0)
    def _():
        acc[...] = y

    @pl.when(step > 0)
    def _():
        acc[...] += y

    @pl.when(step == pl.num_programs(0) - 1)
    def _():
        me = tuple(me_ref[i] for i in range(5))
        yl, core = me[3], me[4]
        for db, da, dy in itertools.product(range(RING), range(RING), range(2)):
            z, yh, xx = source(me, da, db, dy)
            row = (((z & 1) ^ core) * 2 + ((z >> 1) ^ yl)) * 64 + yh * 32 + xx * 8
            at = (db * RING + da) * 16 + dy * 8
            o_ref[pl.ds(pl.multiple_of(row, 8), 8), :] = acc[at : at + 8, :]


def project(me, planes, w):
    rows = sum(p.shape[0] for p in planes)
    steps = 4
    depth = w.shape[0] // steps
    return pl.pallas_call(
        project_kernel,
        grid=(steps,),
        in_specs=[pl.BlockSpec(memory_space=pltpu.SMEM)]
        + [pl.BlockSpec((p.shape[0], depth), lambda i: (0, i)) for p in planes]
        + [pl.BlockSpec((depth, w.shape[1]), lambda i: (i, 0))],
        out_specs=pl.BlockSpec((rows, w.shape[1]), lambda i: (0, 0)),
        out_shape=jax.ShapeDtypeStruct((rows, w.shape[1]), jnp.float32),
        scratch_shapes=[pltpu.VMEM((rows, w.shape[1]), jnp.float32)],
        compiler_params=pltpu.CompilerParams(vmem_limit_bytes=56 * MIB, dimension_semantics=("arbitrary",)),
        name="project",
    )(me, *planes, w)


def on_device(queries, keys, values, lengths, start, out_weight):
    nkv = keys.shape[1]
    me = jnp.stack(coords(lax.axis_index("cp"), lax.axis_index("tp"))).astype(jnp.int32)
    k = keys.transpose(1, 0, 2)
    v = values.transpose(1, 0, 2)
    q = queries.reshape(8, nkv, 16, 128).transpose(1, 2, 0, 3).reshape(1, nkv, 128, 128)
    q = jnp.concatenate([q, moved(q, yh=1)], axis=0)
    q = jnp.concatenate([q] + [moved(q, a=d) for d in (1, 2, 3)], axis=0)
    planes = {0: q}
    for d in (1, 3, 2):
        planes[d] = moved(q, b=d)

    kvs = tuple(range(nkv))
    parts = []
    for d in (0, 1, 3, 2):
        x = after(planes[d], parts[-1]) if parts else planes[d]
        parts.append(attend(me, lengths, start, x, k, v, d, kvs))
    c = combine([parts[0]] + [moved(p, b=-d) for p, d in zip(parts[1:], (1, 3, 2))])
    c = combine([c[:2]] + [moved(c[2 * d : 2 * d + 2], a=-d) for d in (1, 3, 2)])
    attn = finish(c, moved(c, yh=1))
    attn = jnp.concatenate([attn] + [moved(attn, a=d) for d in (1, 2, 3)], axis=0)
    rows = [attn] + [moved(attn, b=d) for d in (1, 2, 3)]
    y = project(me, rows, out_weight)
    y = y[:128] + moved(y[128:], core=1)
    y = y[:64] + moved(y[64:], yl=1)
    return y.astype(jnp.bfloat16)


def solution(mesh):
    in_specs = (
        P("cp", "tp", None),
        P("cp", "tp", None),
        P("cp", "tp", None),
        P("cp"),
        P(),
        P("tp", "cp"),
    )
    return jax.shard_map(on_device, mesh=mesh, in_specs=in_specs, out_specs=P("tp", "cp"), check_vma=False)
```

```python
import functools
import itertools
import math

import jax
import jax.numpy as jnp
from jax import lax
from jax.experimental import pallas as pl
from jax.experimental.pallas import tpu as pltpu
from jax.sharding import PartitionSpec as P

NEG = -1e30
BIG = 2.0**100
RING = 4
MIB = 2**20


def coords(cp, tp):
    z, yh, x = cp // 8, (cp // 4) % 2, cp % 4
    yl, core = tp // 2, tp % 2
    return z, yh, x, yl, core


def moved(x, a=0, b=0, yh=0, yl=0, core=0):
    pairs = []
    for cp, tp in itertools.product(range(32), range(4)):
        zi, yhi, xi, yli, ci = coords(cp, tp)
        dz, dx = (a, b) if ci == 0 else (b, a)
        zo, xo = (zi + dz) % RING, (xi + dx) % RING
        yho, ylo, co = yhi ^ yh, yli ^ yl, ci ^ core
        pairs.append((cp * 4 + tp, ((zo * 2 + yho) * 4 + xo) * 4 + ylo * 2 + co))
    return lax.ppermute(x, ("cp", "tp"), pairs)


def together(*arrays):
    return lax.optimization_barrier(arrays)


def source(me, da, db, dy):
    z, yh, x, _, core = me
    dz = jnp.where(core == 0, da, db)
    dx = jnp.where(core == 0, db, da)
    return (z - dz) & (RING - 1), yh ^ dy, (x - dx) & (RING - 1)


def spread(row, eye):
    return jnp.sum(jnp.where(eye, row, 0.0), axis=1, keepdims=True)


def gathered_row(column, eye):
    return jnp.sum(jnp.where(eye, column, 0.0), axis=0, keepdims=True)


def diagonal():
    shape = (128, 128)
    return lax.broadcasted_iota(jnp.int32, shape, 0) == lax.broadcasted_iota(jnp.int32, shape, 1)


def stat_rows(m, l):
    high = l.astype(jnp.bfloat16).astype(jnp.float32)
    return jnp.concatenate([m, high, l - high, jnp.zeros((13, 128), jnp.float32)], axis=0).astype(jnp.bfloat16)


def attend_kernel(me_ref, len_ref, start_ref, q_ref, k_ref, v_ref, o_ref, vx, kx, *, db, kvs, first, nb, span, tile, scale):
    step = pl.program_id(0)
    rows = nb * 128

    @pl.when(step == 0)
    def _():
        me = tuple(me_ref[i] for i in range(5))
        shard = (me[0] * 2 + me[1]) * 4 + me[2]
        lane = lax.broadcasted_iota(jnp.int32, (1, 128), 1)
        z, yh, x = source(me, lane >> 4, db, (lane >> 3) & 1)
        seen = start_ref[0] + z * 64 + yh * 32 + x * 8 + (lane & 7) + 1 - shard * span
        seen = jnp.minimum(seen, len_ref[0])
        slot = lax.broadcasted_iota(jnp.int32, (span, 128), 0)
        mask = jnp.where((slot >= seen) & (lane < 64), NEG, 0.0).astype(jnp.bfloat16)
        for i, kv in enumerate(kvs):
            kx[i, :, :128] = k_ref[kv]
            kx[i, :, 128:] = mask
            vx[i, :, :128] = v_ref[kv]
            vx[i, :, 128:] = jnp.ones((span, 128), jnp.bfloat16)

    eye = diagonal()
    row = lax.broadcasted_iota(jnp.int32, (rows, 128), 0)
    lane = lax.broadcasted_iota(jnp.int32, (rows, 128), 1)
    hot = jnp.where(lane == (first + step * nb + (row >> 7)) * 8 + (row & 7), 1.0, 0.0).astype(jnp.bfloat16)

    def scores(i, t):
        q = jnp.concatenate([q_ref[:, kvs[i]].reshape(rows, 128), hot], axis=1)
        return lax.dot_general(
            q, kx[i, pl.ds(t, tile), :], (((1,), (1,)), ((), ())), preferred_element_type=jnp.float32
        )

    def point(m):
        return jnp.maximum(m * scale, 0.01 * NEG).astype(jnp.bfloat16).astype(jnp.float32)

    def put(i, m, acc):
        for b in range(nb):
            r = slice(b * 128, (b + 1) * 128)
            o_ref[b, i, :128, :] = acc[r, :128].astype(jnp.bfloat16)
            o_ref[b, i, 128:, :] = stat_rows(gathered_row(m[r], eye), gathered_row(acc[r, 128:], eye))

    ok = []
    for i in range(len(kvs)):
        s0 = scores(i, 0)
        m = point(jnp.max(s0, axis=1, keepdims=True))
        p = []
        for t in range(0, span, tile):
            s = s0 if t == 0 else scores(i, t)
            p.append(jnp.exp2(s * scale - m).astype(jnp.bfloat16))
        acc = jnp.dot(jnp.concatenate(p, axis=1), vx[i], preferred_element_type=jnp.float32)
        ok.append(jnp.min(jnp.where(acc[:, 128:] < BIG, 1.0, 0.0)))
        put(i, m, acc)

    @pl.when(functools.reduce(jnp.minimum, ok) < 0.5)
    def _():
        for i in range(len(kvs)):

            def top(n, m):
                s = scores(i, pl.multiple_of(n * tile, tile))
                return jnp.maximum(m, jnp.max(s, axis=1, keepdims=True))

            m = point(lax.fori_loop(0, span // tile, top, jnp.full((rows, 1), NEG, jnp.float32)))

            def add(n, acc):
                t = pl.multiple_of(n * tile, tile)
                p = jnp.exp2(scores(i, t) * scale - m).astype(jnp.bfloat16)
                return acc + jnp.dot(p, vx[i, pl.ds(t, tile), :], preferred_element_type=jnp.float32)

            put(i, m, lax.fori_loop(0, span // tile, add, jnp.zeros((rows, 256), jnp.float32)))


def attend(me, lengths, start, q, *, k, v, kvs, db, first=0, blocks=8):
    span = v.shape[1]
    nb, tile = 8 // len(kvs), 256
    skip = first // nb
    smem, vmem = pl.BlockSpec(memory_space=pltpu.SMEM), pl.BlockSpec(memory_space=pltpu.VMEM)
    return pl.pallas_call(
        functools.partial(
            attend_kernel, db=db, kvs=kvs, first=first, nb=nb, span=span, tile=tile, scale=math.log2(math.e) / math.sqrt(128)
        ),
        grid=(blocks // nb,),
        in_specs=[smem, smem, smem, pl.BlockSpec((nb, *q.shape[1:]), lambda i: (skip + i, 0, 0, 0)), vmem, vmem],
        out_specs=pl.BlockSpec((nb, len(kvs), 144, 128), lambda i: (i, 0, 0, 0)),
        out_shape=jax.ShapeDtypeStruct((blocks, len(kvs), 144, 128), jnp.bfloat16),
        scratch_shapes=[pltpu.VMEM((len(kvs), span, 256), jnp.bfloat16)] * 2,
        compiler_params=pltpu.CompilerParams(vmem_limit_bytes=28 * MIB, dimension_semantics=("arbitrary",)),
        cost_estimate=pl.CostEstimate(
            flops=8 * blocks * len(kvs) * 128 * span * 128,
            bytes_accessed=4 * MIB,
            transcendentals=blocks * len(kvs) * 128 * span,
        ),
        name="attend_plane",
    )(me, lengths, start, q, k, v)


def merged(parts, eye):
    stats = [p[128:, :].astype(jnp.float32) for p in parts]
    m = functools.reduce(jnp.maximum, [s[0:1] for s in stats])
    total = jnp.zeros((1, 128), jnp.float32)
    out = jnp.zeros((128, 128), jnp.float32)
    for p, s in zip(parts, stats):
        factor = jnp.exp2(s[0:1] - m)
        total = total + factor * (s[1:2] + s[2:3])
        out = out + spread(factor, eye) * p[:128, :].astype(jnp.float32)
    return out, m, total


def combine_kernel(*refs, own):
    o_ref = refs[-1]
    eye = diagonal()
    for b, kv in itertools.product(range(o_ref.shape[0]), range(o_ref.shape[1])):
        share = o_ref.shape[0] // own
        out, m, total = merged([refs[b // share][b % share, kv]] + [r[b, kv] for r in refs[own:-1]], eye)
        o_ref[b, kv, :128, :] = out.astype(jnp.bfloat16)
        o_ref[b, kv, 128:, :] = stat_rows(m, total)


def combine(own, others):
    vmem = pl.BlockSpec(memory_space=pltpu.VMEM)
    return pl.pallas_call(
        functools.partial(combine_kernel, own=len(own)),
        in_specs=[vmem] * (len(own) + len(others)),
        out_specs=vmem,
        out_shape=jax.ShapeDtypeStruct(others[0].shape, jnp.bfloat16),
        compiler_params=pltpu.CompilerParams(vmem_limit_bytes=8 * MIB),
        name="combine",
    )(*own, *others)


def finish_kernel(mine, theirs, o_ref):
    eye = diagonal()
    for kv in range(mine.shape[1]):
        attn = []
        for dy in range(2):
            out, _, total = merged([mine[dy, kv], theirs[1 - dy, kv]], eye)
            attn.append((out * spread(1.0 / total, eye)).astype(jnp.bfloat16))
        for h in range(16):
            c = (kv * 16 + h) * 128
            o_ref[:, c : c + 128] = jnp.concatenate([a[h * 8 : (h + 1) * 8, :] for a in attn], axis=0)


def finish(mine, theirs):
    vmem = pl.BlockSpec(memory_space=pltpu.VMEM)
    return pl.pallas_call(
        finish_kernel,
        in_specs=[vmem, vmem],
        out_specs=vmem,
        compiler_params=pltpu.CompilerParams(vmem_limit_bytes=4 * MIB),
        out_shape=jax.ShapeDtypeStruct((16, mine.shape[1] * 2048), jnp.bfloat16),
        name="finish",
    )(mine, theirs)


def assemble_kernel(x0, x1, x2, x3, _, o_ref):
    for i, x in enumerate((x0, x1, x2, x3)):
        o_ref[i * x.shape[0] : (i + 1) * x.shape[0], :] = x[...]


def assemble(*pieces):
    vmem = pl.BlockSpec(memory_space=pltpu.VMEM)
    rows, width = pieces[0].shape
    return pl.pallas_call(
        assemble_kernel,
        in_specs=[vmem] * 4 + [pl.BlockSpec(memory_space=pl.ANY)],
        out_specs=vmem,
        out_shape=jax.ShapeDtypeStruct((RING * rows, width), pieces[0].dtype),
        compiler_params=pltpu.CompilerParams(vmem_limit_bytes=4 * MIB),
        name="assemble",
    )(*pieces)


def project_kernel(x_ref, w_ref, o_ref):
    o_ref[...] = jnp.dot(x_ref[...], w_ref[...], preferred_element_type=jnp.float32)


def project(x, w):
    vmem = pl.BlockSpec(memory_space=pltpu.VMEM)
    return pl.pallas_call(
        project_kernel,
        in_specs=[vmem, vmem],
        out_specs=vmem,
        out_shape=jax.ShapeDtypeStruct((x.shape[0], w.shape[1]), jnp.float32),
        compiler_params=pltpu.CompilerParams(vmem_limit_bytes=8 * MIB),
        cost_estimate=pl.CostEstimate(
            flops=8 * x.shape[0] * w.shape[0] * w.shape[1], bytes_accessed=4 * MIB, transcendentals=0
        ),
        name="project",
    )(x, w)


def place_kernel(me_ref, y0, y1, y3, x_ref, w_ref, o_ref):
    me = tuple(me_ref[i] for i in range(5))
    yl, core = me[3], me[4]
    y2 = jnp.dot(x_ref[...], w_ref[...], preferred_element_type=jnp.float32)
    for db, y in ((0, y0), (1, y1), (2, y2), (3, y3)):
        for da, dy in itertools.product(range(RING), range(2)):
            z, yh, xx = source(me, da, db, dy)
            row = (((z & 1) ^ core) * 2 + ((z >> 1) ^ yl)) * 64 + yh * 32 + xx * 8
            at = da * 16 + dy * 8
            o_ref[pl.ds(pl.multiple_of(row, 8), 8), :] = y[at : at + 8, :]


def place(me, y0, y1, y3, x, w):
    vmem = pl.BlockSpec(memory_space=pltpu.VMEM)
    return pl.pallas_call(
        place_kernel,
        in_specs=[pl.BlockSpec(memory_space=pltpu.SMEM)] + [vmem] * 5,
        out_specs=vmem,
        out_shape=jax.ShapeDtypeStruct((RING * x.shape[0], w.shape[1]), jnp.float32),
        compiler_params=pltpu.CompilerParams(vmem_limit_bytes=8 * MIB),
        name="place",
    )(me, y0, y1, y3, x, w)


def on_device(queries, keys, values, lengths, start, out_weight):
    nkv = keys.shape[1]
    me = jnp.stack(coords(lax.axis_index("cp"), lax.axis_index("tp"))).astype(jnp.int32)
    k = keys.transpose(1, 0, 2)
    v = values.transpose(1, 0, 2)
    q = queries.reshape(8, nkv, 16, 128).transpose(1, 2, 0, 3).reshape(1, nkv, 128, 128)
    q = jnp.concatenate([q, moved(q, yh=1)], axis=0)
    q, k, v, me = together(q, k, v, me)
    q = jnp.concatenate([q] + [moved(q, a=d) for d in (1, 2, 3)], axis=0)
    q1, q3, q2 = (moved(q, b=d) for d in (1, 3, 2))

    kvs = tuple(range(nkv))
    part = functools.partial(attend, me, lengths, start, k=k, v=v, kvs=kvs)
    own0 = part(q, db=0, first=0, blocks=4)
    q1, own0 = together(q1, own0)
    p1 = part(q1, db=1)
    r1 = moved(p1, b=-1)
    q3, p1 = together(q3, p1)
    p3 = part(q3, db=3)
    r3 = moved(p3, b=-3)
    q2, p3, r1 = together(q2, p3, r1)
    p2 = part(q2, db=2)
    r2 = moved(p2, b=-2)
    q, p2, r3 = together(q, p2, r3)
    own1 = part(q, db=0, first=4, blocks=4)
    c = combine([own0, own1], [r1, r3, r2])
    c = combine([c[:2]], [moved(c[2 * d : 2 * d + 2], a=-d) for d in (1, 3, 2)])
    attn = finish(c, moved(c, yh=1))
    pieces = [moved(attn, a=d) for d in (1, 2, 3)]
    attn = assemble(attn, *pieces, moved(pieces[1], core=1))
    x1, x3, x2 = (moved(attn, b=d) for d in (1, 3, 2))
    y = place(me, project(attn, out_weight), project(x1, out_weight), project(x3, out_weight), x2, out_weight)
    y = y[:128] + moved(y[128:], core=1)
    y = y[:64] + moved(y[64:], yl=1)
    return y.astype(jnp.bfloat16)


def solution(mesh):
    in_specs = (
        P("cp", "tp", None),
        P("cp", "tp", None),
        P("cp", "tp", None),
        P("cp"),
        P(),
        P("tp", "cp"),
    )
    return jax.shard_map(on_device, mesh=mesh, in_specs=in_specs, out_specs=P("tp", "cp"), check_vma=False)
```

```python
import functools
import itertools
import math

import jax
import jax.numpy as jnp
from jax import lax
from jax.experimental import pallas as pl
from jax.experimental.pallas import tpu as pltpu
from jax.sharding import PartitionSpec as P

NEG = -1e30
BIG = 2.0**100
RING = 4
MIB = 2**20


def coords(cp, tp):
    z, yh, x = cp // 8, (cp // 4) % 2, cp % 4
    yl, core = tp // 2, tp % 2
    return z, yh, x, yl, core


def moved(x, a=0, b=0, yh=0, yl=0, core=0):
    pairs = []
    for cp, tp in itertools.product(range(32), range(4)):
        zi, yhi, xi, yli, ci = coords(cp, tp)
        dz, dx = (a, b) if ci == 0 else (b, a)
        zo, xo = (zi + dz) % RING, (xi + dx) % RING
        yho, ylo, co = yhi ^ yh, yli ^ yl, ci ^ core
        pairs.append((cp * 4 + tp, ((zo * 2 + yho) * 4 + xo) * 4 + ylo * 2 + co))
    return lax.ppermute(x, ("cp", "tp"), pairs)


def together(*arrays):
    return lax.optimization_barrier(arrays)


def source(me, da, db, dy):
    z, yh, x, _, core = me
    dz = jnp.where(core == 0, da, db)
    dx = jnp.where(core == 0, db, da)
    return (z - dz) & (RING - 1), yh ^ dy, (x - dx) & (RING - 1)


def spread(row, eye):
    return jnp.sum(jnp.where(eye, row, 0.0), axis=1, keepdims=True)


def gathered_row(column, eye):
    return jnp.sum(jnp.where(eye, column, 0.0), axis=0, keepdims=True)


def diagonal():
    shape = (128, 128)
    return lax.broadcasted_iota(jnp.int32, shape, 0) == lax.broadcasted_iota(jnp.int32, shape, 1)


def stat_rows(m, l):
    high = l.astype(jnp.bfloat16).astype(jnp.float32)
    return jnp.concatenate([m, high, l - high, jnp.zeros((13, 128), jnp.float32)], axis=0).astype(jnp.bfloat16)


def prepare_kernel(me_ref, len_ref, start_ref, k_ref, *refs, planes):
    nkv, span = k_ref.shape[:2]
    me = tuple(me_ref[i] for i in range(5))
    shard = (me[0] * 2 + me[1]) * 4 + me[2]
    lane = lax.broadcasted_iota(jnp.int32, (1, 128), 1)
    slot = lax.broadcasted_iota(jnp.int32, (span, 128), 0)
    for db, kx in zip(planes, refs[-len(planes) :]):
        z, yh, x = source(me, lane >> 4, db, (lane >> 3) & 1)
        seen = start_ref[0] + z * 64 + yh * 32 + x * 8 + (lane & 7) + 1 - shard * span
        seen = jnp.minimum(seen, len_ref[0])
        mask = jnp.where((slot >= seen) & (lane < 64), NEG, 0.0).astype(jnp.bfloat16)
        for kv in range(nkv):
            kx[kv, :, :128] = k_ref[kv]
            kx[kv, :, 128:] = mask
    if len(refs) > len(planes):
        v_ref, vx = refs[:2]
        for kv in range(nkv):
            vx[kv, :, :128] = v_ref[kv]
            vx[kv, :, 128:] = jnp.ones((span, 128), jnp.bfloat16)


def prepare(me, lengths, start, k, planes, *v):
    smem, vmem = pl.BlockSpec(memory_space=pltpu.SMEM), pl.BlockSpec(memory_space=pltpu.VMEM)
    count = len(planes) + len(v)
    return pl.pallas_call(
        functools.partial(prepare_kernel, planes=planes),
        in_specs=[smem, smem, smem, vmem] + [vmem] * len(v),
        out_specs=[vmem] * count,
        out_shape=[jax.ShapeDtypeStruct((*k.shape[:2], 256), jnp.bfloat16)] * count,
        compiler_params=pltpu.CompilerParams(vmem_limit_bytes=4 * MIB),
        name="prepare",
    )(me, lengths, start, k, *v)


def attend_kernel(q_ref, kx, vx, o_ref, *, kvs, first, nb, tile, scale):
    step = pl.program_id(0)
    rows = nb * 128
    span = vx.shape[1]
    eye = diagonal()
    row = lax.broadcasted_iota(jnp.int32, (rows, 128), 0)
    lane = lax.broadcasted_iota(jnp.int32, (rows, 128), 1)
    hot = jnp.where(lane == (first + step * nb + (row >> 7)) * 8 + (row & 7), 1.0, 0.0).astype(jnp.bfloat16)

    def scores(i, t):
        q = jnp.concatenate([q_ref[:, kvs[i]].reshape(rows, 128), hot], axis=1)
        return lax.dot_general(
            q, kx[kvs[i], pl.ds(t, tile), :], (((1,), (1,)), ((), ())), preferred_element_type=jnp.float32
        )

    def point(m):
        return jnp.maximum(m * scale, 0.01 * NEG).astype(jnp.bfloat16).astype(jnp.float32)

    def put(i, m, acc):
        for b in range(nb):
            r = slice(b * 128, (b + 1) * 128)
            o_ref[b, i, :128, :] = acc[r, :128].astype(jnp.bfloat16)
            o_ref[b, i, 128:, :] = stat_rows(gathered_row(m[r], eye), gathered_row(acc[r, 128:], eye))

    ok = []
    for i in range(len(kvs)):
        s0 = scores(i, 0)
        m = point(jnp.max(s0, axis=1, keepdims=True))
        p = []
        for t in range(0, span, tile):
            s = s0 if t == 0 else scores(i, t)
            p.append(jnp.exp2(s * scale - m).astype(jnp.bfloat16))
        acc = jnp.dot(jnp.concatenate(p, axis=1), vx[kvs[i]], preferred_element_type=jnp.float32)
        ok.append(jnp.min(jnp.where(acc[:, 128:] < BIG, 1.0, 0.0)))
        put(i, m, acc)

    @pl.when(functools.reduce(jnp.minimum, ok) < 0.5)
    def _():
        for i in range(len(kvs)):

            def top(n, m):
                s = scores(i, pl.multiple_of(n * tile, tile))
                return jnp.maximum(m, jnp.max(s, axis=1, keepdims=True))

            m = point(lax.fori_loop(0, span // tile, top, jnp.full((rows, 1), NEG, jnp.float32)))

            def add(n, acc):
                t = pl.multiple_of(n * tile, tile)
                p = jnp.exp2(scores(i, t) * scale - m).astype(jnp.bfloat16)
                return acc + jnp.dot(p, vx[kvs[i], pl.ds(t, tile), :], preferred_element_type=jnp.float32)

            put(i, m, lax.fori_loop(0, span // tile, add, jnp.zeros((rows, 256), jnp.float32)))


def attend(q, kx, vx, kvs, first=0, blocks=8):
    span = vx.shape[1]
    nb, tile = 8 // len(kvs), 256
    skip = first // nb
    vmem = pl.BlockSpec(memory_space=pltpu.VMEM)
    return pl.pallas_call(
        functools.partial(
            attend_kernel, kvs=kvs, first=first, nb=nb, tile=tile, scale=math.log2(math.e) / math.sqrt(128)
        ),
        grid=(blocks // nb,),
        in_specs=[pl.BlockSpec((nb, *q.shape[1:]), lambda i: (skip + i, 0, 0, 0)), vmem, vmem],
        out_specs=pl.BlockSpec((nb, len(kvs), 144, 128), lambda i: (i, 0, 0, 0)),
        out_shape=jax.ShapeDtypeStruct((blocks, len(kvs), 144, 128), jnp.bfloat16),
        compiler_params=pltpu.CompilerParams(vmem_limit_bytes=20 * MIB, dimension_semantics=("arbitrary",)),
        cost_estimate=pl.CostEstimate(
            flops=8 * blocks * len(kvs) * 128 * span * 128,
            bytes_accessed=4 * MIB,
            transcendentals=blocks * len(kvs) * 128 * span,
        ),
        name="attend_plane",
    )(q, kx, vx)


def merged(parts, eye):
    stats = [p[128:, :].astype(jnp.float32) for p in parts]
    m = functools.reduce(jnp.maximum, [s[0:1] for s in stats])
    total = jnp.zeros((1, 128), jnp.float32)
    out = jnp.zeros((128, 128), jnp.float32)
    for p, s in zip(parts, stats):
        factor = jnp.exp2(s[0:1] - m)
        total = total + factor * (s[1:2] + s[2:3])
        out = out + spread(factor, eye) * p[:128, :].astype(jnp.float32)
    return out, m, total


def combine_kernel(*refs, own):
    o_ref = refs[-1]
    eye = diagonal()
    for b, kv in itertools.product(range(o_ref.shape[0]), range(o_ref.shape[1])):
        share = o_ref.shape[0] // own
        out, m, total = merged([refs[b // share][b % share, kv]] + [r[b, kv] for r in refs[own:-1]], eye)
        o_ref[b, kv, :128, :] = out.astype(jnp.bfloat16)
        o_ref[b, kv, 128:, :] = stat_rows(m, total)


def combine(own, others):
    vmem = pl.BlockSpec(memory_space=pltpu.VMEM)
    return pl.pallas_call(
        functools.partial(combine_kernel, own=len(own)),
        in_specs=[vmem] * (len(own) + len(others)),
        out_specs=vmem,
        out_shape=jax.ShapeDtypeStruct(others[0].shape, jnp.bfloat16),
        compiler_params=pltpu.CompilerParams(vmem_limit_bytes=8 * MIB),
        name="combine",
    )(*own, *others)


def finish_kernel(mine, theirs, o_ref):
    eye = diagonal()
    for kv in range(mine.shape[1]):
        attn = []
        for dy in range(2):
            out, _, total = merged([mine[dy, kv], theirs[1 - dy, kv]], eye)
            attn.append((out * spread(1.0 / total, eye)).astype(jnp.bfloat16))
        for h in range(16):
            c = (kv * 16 + h) * 128
            o_ref[:, c : c + 128] = jnp.concatenate([a[h * 8 : (h + 1) * 8, :] for a in attn], axis=0)


def finish(mine, theirs):
    vmem = pl.BlockSpec(memory_space=pltpu.VMEM)
    return pl.pallas_call(
        finish_kernel,
        in_specs=[vmem, vmem],
        out_specs=vmem,
        compiler_params=pltpu.CompilerParams(vmem_limit_bytes=4 * MIB),
        out_shape=jax.ShapeDtypeStruct((16, mine.shape[1] * 2048), jnp.bfloat16),
        name="finish",
    )(mine, theirs)


def assemble_kernel(x0, x1, x2, x3, _, o_ref):
    for i, x in enumerate((x0, x1, x2, x3)):
        o_ref[i * x.shape[0] : (i + 1) * x.shape[0], :] = x[...]


def assemble(*pieces):
    vmem = pl.BlockSpec(memory_space=pltpu.VMEM)
    rows, width = pieces[0].shape
    return pl.pallas_call(
        assemble_kernel,
        in_specs=[vmem] * 4 + [pl.BlockSpec(memory_space=pl.ANY)],
        out_specs=vmem,
        out_shape=jax.ShapeDtypeStruct((RING * rows, width), pieces[0].dtype),
        compiler_params=pltpu.CompilerParams(vmem_limit_bytes=4 * MIB),
        name="assemble",
    )(*pieces)


def project_kernel(x_ref, w_ref, o_ref):
    o_ref[...] = jnp.dot(x_ref[...], w_ref[...], preferred_element_type=jnp.float32)


def project(x, w):
    vmem = pl.BlockSpec(memory_space=pltpu.VMEM)
    return pl.pallas_call(
        project_kernel,
        in_specs=[vmem, vmem],
        out_specs=vmem,
        out_shape=jax.ShapeDtypeStruct((x.shape[0], w.shape[1]), jnp.float32),
        compiler_params=pltpu.CompilerParams(vmem_limit_bytes=8 * MIB),
        cost_estimate=pl.CostEstimate(
            flops=8 * x.shape[0] * w.shape[0] * w.shape[1], bytes_accessed=4 * MIB, transcendentals=0
        ),
        name="project",
    )(x, w)


def place_kernel(me_ref, y0, y1, y3, x_ref, w_ref, o_ref):
    me = tuple(me_ref[i] for i in range(5))
    yl, core = me[3], me[4]
    y2 = jnp.dot(x_ref[...], w_ref[...], preferred_element_type=jnp.float32)
    for db, y in ((0, y0), (1, y1), (2, y2), (3, y3)):
        for da, dy in itertools.product(range(RING), range(2)):
            z, yh, xx = source(me, da, db, dy)
            row = (((z & 1) ^ core) * 2 + ((z >> 1) ^ yl)) * 64 + yh * 32 + xx * 8
            at = da * 16 + dy * 8
            o_ref[pl.ds(pl.multiple_of(row, 8), 8), :] = y[at : at + 8, :]


def place(me, y0, y1, y3, x, w):
    vmem = pl.BlockSpec(memory_space=pltpu.VMEM)
    return pl.pallas_call(
        place_kernel,
        in_specs=[pl.BlockSpec(memory_space=pltpu.SMEM)] + [vmem] * 5,
        out_specs=vmem,
        out_shape=jax.ShapeDtypeStruct((RING * x.shape[0], w.shape[1]), jnp.float32),
        compiler_params=pltpu.CompilerParams(vmem_limit_bytes=8 * MIB),
        name="place",
    )(me, y0, y1, y3, x, w)


def on_device(queries, keys, values, lengths, start, out_weight):
    nkv = keys.shape[1]
    me = jnp.stack(coords(lax.axis_index("cp"), lax.axis_index("tp"))).astype(jnp.int32)
    k = keys.transpose(1, 0, 2)
    v = values.transpose(1, 0, 2)
    q = queries.reshape(8, nkv, 16, 128).transpose(1, 2, 0, 3).reshape(1, nkv, 128, 128)
    q = jnp.concatenate([q, moved(q, yh=1)], axis=0)
    vx, kx0 = prepare(me, lengths, start, k, (0,), v)
    q, vx, kx0 = together(q, vx, kx0)
    kx1, kx2, kx3 = prepare(me, lengths, start, k, (1, 2, 3))
    q = jnp.concatenate([q] + [moved(q, a=d) for d in (1, 2, 3)], axis=0)
    q, kx1, kx2, kx3 = together(q, kx1, kx2, kx3)
    q1, q2, q3 = (moved(q, b=d) for d in (1, 2, 3))

    kvs = tuple(range(nkv))
    own0 = attend(q, kx0, vx, kvs, 0, 4)
    q1, own0 = together(q1, own0)
    p1 = attend(q1, kx1, vx, kvs)
    r1 = moved(p1, b=-1)
    q2, q3, p1 = together(q2, q3, p1)
    p2 = attend(q2, kx2, vx, kvs)
    r2 = moved(p2, b=-2)
    q3, p2, r1 = together(q3, p2, r1)
    p3 = attend(q3, kx3, vx, kvs)
    r3 = moved(p3, b=-3)
    q, p3, r2 = together(q, p3, r2)
    own1 = attend(q, kx0, vx, kvs, 4, 4)
    c = combine([own0, own1], [r1, r2, r3])
    c = combine([c[:2]], [moved(c[2 * d : 2 * d + 2], a=-d) for d in (1, 3, 2)])
    attn = finish(c, moved(c, yh=1))
    pieces = [moved(attn, a=d) for d in (1, 2, 3)]
    attn = assemble(attn, *pieces, moved(pieces[1], core=1))
    x1, x3, x2 = (moved(attn, b=d) for d in (1, 3, 2))
    y = place(me, project(attn, out_weight), project(x1, out_weight), project(x3, out_weight), x2, out_weight)
    y = y[:128] + moved(y[128:], core=1)
    y = y[:64] + moved(y[64:].astype(jnp.bfloat16), yl=1).astype(jnp.float32)
    return y.astype(jnp.bfloat16)


def solution(mesh):
    in_specs = (
        P("cp", "tp", None),
        P("cp", "tp", None),
        P("cp", "tp", None),
        P("cp"),
        P(),
        P("tp", "cp"),
    )
    return jax.shard_map(on_device, mesh=mesh, in_specs=in_specs, out_specs=P("tp", "cp"), check_vma=False)
```

```python
import functools
import itertools
import math

import jax
import jax.numpy as jnp
from jax import lax
from jax.experimental import pallas as pl
from jax.experimental.pallas import tpu as pltpu
from jax.sharding import PartitionSpec as P

NEG = -1e30
BIG = 2.0**100
RING = 4
MIB = 2**20


def coords(cp, tp):
    z, yh, x = cp // 8, (cp // 4) % 2, cp % 4
    yl, core = tp // 2, tp % 2
    return z, yh, x, yl, core


def moved(x, a=0, b=0, yh=0, yl=0, core=0):
    pairs = []
    for cp, tp in itertools.product(range(32), range(4)):
        zi, yhi, xi, yli, ci = coords(cp, tp)
        dz, dx = (a, b) if ci == 0 else (b, a)
        zo, xo = (zi + dz) % RING, (xi + dx) % RING
        yho, ylo, co = yhi ^ yh, yli ^ yl, ci ^ core
        pairs.append((cp * 4 + tp, ((zo * 2 + yho) * 4 + xo) * 4 + ylo * 2 + co))
    return lax.ppermute(x, ("cp", "tp"), pairs)


def together(*arrays):
    return lax.optimization_barrier(arrays)


def source(me, da, db, dy):
    z, yh, x, _, core = me
    dz = jnp.where(core == 0, da, db)
    dx = jnp.where(core == 0, db, da)
    return (z - dz) & (RING - 1), yh ^ dy, (x - dx) & (RING - 1)


def spread(row, eye):
    return jnp.sum(jnp.where(eye, row, 0.0), axis=1, keepdims=True)


def gathered_row(column, eye):
    return jnp.sum(jnp.where(eye, column, 0.0), axis=0, keepdims=True)


def diagonal():
    shape = (128, 128)
    return lax.broadcasted_iota(jnp.int32, shape, 0) == lax.broadcasted_iota(jnp.int32, shape, 1)


def stat_rows(m, l):
    high = l.astype(jnp.bfloat16).astype(jnp.float32)
    return jnp.concatenate([m, high, l - high, jnp.zeros((13, 128), jnp.float32)], axis=0).astype(jnp.bfloat16)


def prepare_kernel(info, k_ref, v_ref, vx, *masked):
    nkv, span = k_ref.shape[:2]
    me = tuple(info[i] for i in range(5))
    length, start = info[5], info[6]
    shard = (me[0] * 2 + me[1]) * 4 + me[2]
    lane = lax.broadcasted_iota(jnp.int32, (1, 128), 1)
    slot = lax.broadcasted_iota(jnp.int32, (span, 128), 0)
    for db, kx in enumerate(masked):
        z, yh, x = source(me, lane >> 4, db, (lane >> 3) & 1)
        seen = start + z * 64 + yh * 32 + x * 8 + (lane & 7) + 1 - shard * span
        seen = jnp.minimum(seen, length)
        mask = jnp.where((slot >= seen) & (lane < 64), NEG, 0.0).astype(jnp.bfloat16)
        for kv in range(nkv):
            kx[kv, :, :128] = k_ref[kv]
            kx[kv, :, 128:] = mask
    for kv in range(nkv):
        vx[kv, :, :128] = v_ref[kv]
        vx[kv, :, 128:] = jnp.ones((span, 128), jnp.bfloat16)


def prepare(info, k, v):
    vmem = pl.BlockSpec(memory_space=pltpu.VMEM)
    count = 1 + RING
    return pl.pallas_call(
        prepare_kernel,
        in_specs=[pl.BlockSpec(memory_space=pltpu.SMEM), vmem, vmem],
        out_specs=[vmem] * count,
        out_shape=[jax.ShapeDtypeStruct((*k.shape[:2], 256), jnp.bfloat16)] * count,
        compiler_params=pltpu.CompilerParams(vmem_limit_bytes=4 * MIB),
        name="prepare",
    )(info, k, v)


def attend_kernel(q_ref, kx, vx, o_ref, *, kvs, first, nb, tile, scale):
    step = pl.program_id(0)
    rows = nb * 128
    span = vx.shape[1]
    eye = diagonal()
    row = lax.broadcasted_iota(jnp.int32, (rows, 128), 0)
    lane = lax.broadcasted_iota(jnp.int32, (rows, 128), 1)
    hot = jnp.where(lane == (first + step * nb + (row >> 7)) * 8 + ((row >> 4) & 7), 1.0, 0.0).astype(jnp.bfloat16)

    def scores(i, t):
        heads = q_ref[:, :, kvs[i] * 16 : (kvs[i] + 1) * 16, :].reshape(rows, 128)
        q = jnp.concatenate([heads, hot], axis=1)
        return lax.dot_general(
            q, kx[kvs[i], pl.ds(t, tile), :], (((1,), (1,)), ((), ())), preferred_element_type=jnp.float32
        )

    def point(m):
        return jnp.maximum(m * scale, 0.01 * NEG).astype(jnp.bfloat16).astype(jnp.float32)

    def put(i, m, acc):
        for b in range(nb):
            r = slice(b * 128, (b + 1) * 128)
            o_ref[b, i, :128, :] = acc[r, :128].astype(jnp.bfloat16)
            o_ref[b, i, 128:, :] = stat_rows(gathered_row(m[r], eye), gathered_row(acc[r, 128:], eye))

    ok = []
    for i in range(len(kvs)):
        s0 = scores(i, 0)
        m = point(jnp.max(s0, axis=1, keepdims=True))
        p = []
        for t in range(0, span, tile):
            s = s0 if t == 0 else scores(i, t)
            p.append(jnp.exp2(s * scale - m).astype(jnp.bfloat16))
        acc = jnp.dot(jnp.concatenate(p, axis=1), vx[kvs[i]], preferred_element_type=jnp.float32)
        ok.append(jnp.min(jnp.where(acc[:, 128:] < BIG, 1.0, 0.0)))
        put(i, m, acc)

    @pl.when(functools.reduce(jnp.minimum, ok) < 0.5)
    def _():
        for i in range(len(kvs)):

            def top(n, m):
                s = scores(i, pl.multiple_of(n * tile, tile))
                return jnp.maximum(m, jnp.max(s, axis=1, keepdims=True))

            m = point(lax.fori_loop(0, span // tile, top, jnp.full((rows, 1), NEG, jnp.float32)))

            def add(n, acc):
                t = pl.multiple_of(n * tile, tile)
                p = jnp.exp2(scores(i, t) * scale - m).astype(jnp.bfloat16)
                return acc + jnp.dot(p, vx[kvs[i], pl.ds(t, tile), :], preferred_element_type=jnp.float32)

            put(i, m, lax.fori_loop(0, span // tile, add, jnp.zeros((rows, 256), jnp.float32)))


def attend(q, kx, vx, kvs, first=0, blocks=8):
    span = vx.shape[1]
    nb, tile = 8 // len(kvs), 256
    skip = first // nb
    vmem = pl.BlockSpec(memory_space=pltpu.VMEM)
    return pl.pallas_call(
        functools.partial(
            attend_kernel, kvs=kvs, first=first, nb=nb, tile=tile, scale=math.log2(math.e) / math.sqrt(128)
        ),
        grid=(blocks // nb,),
        in_specs=[pl.BlockSpec((nb, *q.shape[1:]), lambda i: (skip + i, 0, 0, 0)), vmem, vmem],
        out_specs=pl.BlockSpec((nb, len(kvs), 144, 128), lambda i: (i, 0, 0, 0)),
        out_shape=jax.ShapeDtypeStruct((blocks, len(kvs), 144, 128), jnp.bfloat16),
        compiler_params=pltpu.CompilerParams(vmem_limit_bytes=20 * MIB, dimension_semantics=("arbitrary",)),
        cost_estimate=pl.CostEstimate(
            flops=8 * blocks * len(kvs) * 128 * span * 128,
            bytes_accessed=4 * MIB,
            transcendentals=blocks * len(kvs) * 128 * span,
        ),
        name="attend_plane",
    )(q, kx, vx)


def merged(parts, eye):
    stats = [p[128:, :].astype(jnp.float32) for p in parts]
    m = functools.reduce(jnp.maximum, [s[0:1] for s in stats])
    total = jnp.zeros((1, 128), jnp.float32)
    out = jnp.zeros((128, 128), jnp.float32)
    for p, s in zip(parts, stats):
        factor = jnp.exp2(s[0:1] - m)
        total = total + factor * (s[1:2] + s[2:3])
        out = out + spread(factor, eye) * p[:128, :].astype(jnp.float32)
    return out, m, total


def combine_kernel(*refs, own):
    o_ref = refs[-1]
    eye = diagonal()
    for b, kv in itertools.product(range(o_ref.shape[0]), range(o_ref.shape[1])):
        share = o_ref.shape[0] // own
        out, m, total = merged([refs[b // share][b % share, kv]] + [r[b, kv] for r in refs[own:-1]], eye)
        o_ref[b, kv, :128, :] = out.astype(jnp.bfloat16)
        o_ref[b, kv, 128:, :] = stat_rows(m, total)


def combine(own, others):
    vmem = pl.BlockSpec(memory_space=pltpu.VMEM)
    return pl.pallas_call(
        functools.partial(combine_kernel, own=len(own)),
        in_specs=[vmem] * (len(own) + len(others)),
        out_specs=vmem,
        out_shape=jax.ShapeDtypeStruct(others[0].shape, jnp.bfloat16),
        compiler_params=pltpu.CompilerParams(vmem_limit_bytes=8 * MIB),
        name="combine",
    )(*own, *others)


def finish_kernel(mine, theirs, o_ref, rows):
    eye = diagonal()
    for kv in range(mine.shape[1]):
        for dy in range(2):
            out, _, total = merged([mine[dy, kv], theirs[1 - dy, kv]], eye)
            rows[kv, dy] = out * spread(1.0 / total, eye)
    for kv, h in itertools.product(range(mine.shape[1]), range(16)):
        c = (kv * 16 + h) * 128
        both = [rows[kv, dy, pl.ds(h, 8, stride=16), :] for dy in range(2)]
        o_ref[:, c : c + 128] = jnp.concatenate(both, axis=0).astype(jnp.bfloat16)


def finish(mine, theirs):
    vmem = pl.BlockSpec(memory_space=pltpu.VMEM)
    return pl.pallas_call(
        finish_kernel,
        in_specs=[vmem, vmem],
        out_specs=vmem,
        scratch_shapes=[pltpu.VMEM((mine.shape[1], 2, 128, 128), jnp.float32)],
        compiler_params=pltpu.CompilerParams(vmem_limit_bytes=4 * MIB),
        out_shape=jax.ShapeDtypeStruct((16, mine.shape[1] * 2048), jnp.bfloat16),
        name="finish",
    )(mine, theirs)


def assemble_kernel(x0, x1, x2, x3, _, o_ref):
    for i, x in enumerate((x0, x1, x2, x3)):
        o_ref[i * x.shape[0] : (i + 1) * x.shape[0], :] = x[...]


def assemble(*pieces):
    vmem = pl.BlockSpec(memory_space=pltpu.VMEM)
    rows, width = pieces[0].shape
    return pl.pallas_call(
        assemble_kernel,
        in_specs=[vmem] * 4 + [pl.BlockSpec(memory_space=pl.ANY)],
        out_specs=vmem,
        out_shape=jax.ShapeDtypeStruct((RING * rows, width), pieces[0].dtype),
        compiler_params=pltpu.CompilerParams(vmem_limit_bytes=4 * MIB),
        name="assemble",
    )(*pieces)


def project_kernel(x_ref, w_ref, o_ref):
    o_ref[...] = jnp.dot(x_ref[...], w_ref[...], preferred_element_type=jnp.float32)


def project(x, w):
    vmem = pl.BlockSpec(memory_space=pltpu.VMEM)
    return pl.pallas_call(
        project_kernel,
        in_specs=[vmem, vmem],
        out_specs=vmem,
        out_shape=jax.ShapeDtypeStruct((x.shape[0], w.shape[1]), jnp.float32),
        compiler_params=pltpu.CompilerParams(vmem_limit_bytes=8 * MIB),
        cost_estimate=pl.CostEstimate(
            flops=8 * x.shape[0] * w.shape[0] * w.shape[1], bytes_accessed=4 * MIB, transcendentals=0
        ),
        name="project",
    )(x, w)


def place_kernel(info, y0, y1, y3, xa_ref, xb_ref, w_ref, o_ref):
    me = tuple(info[i] for i in range(5))
    yl, core = me[3], me[4]
    x = jnp.concatenate([xa_ref[...], xb_ref[...]], axis=0)
    y2 = jnp.dot(x, w_ref[...], preferred_element_type=jnp.float32)
    for db, y in ((0, y0), (1, y1), (2, y2), (3, y3)):
        for da, dy in itertools.product(range(RING), range(2)):
            z, yh, xx = source(me, da, db, dy)
            row = (((z & 1) ^ core) * 2 + ((z >> 1) ^ yl)) * 64 + yh * 32 + xx * 8
            at = da * 16 + dy * 8
            o_ref[pl.ds(pl.multiple_of(row, 8), 8), :] = y[at : at + 8, :]


def place(info, y0, y1, y3, xa, xb, w):
    vmem = pl.BlockSpec(memory_space=pltpu.VMEM)
    return pl.pallas_call(
        place_kernel,
        in_specs=[pl.BlockSpec(memory_space=pltpu.SMEM)] + [vmem] * 6,
        out_specs=vmem,
        out_shape=jax.ShapeDtypeStruct((RING * y0.shape[0], w.shape[1]), jnp.float32),
        compiler_params=pltpu.CompilerParams(vmem_limit_bytes=8 * MIB),
        name="place",
    )(info, y0, y1, y3, xa, xb, w)


def on_device(queries, keys, values, lengths, start, out_weight):
    nkv = keys.shape[1]
    me = coords(lax.axis_index("cp"), lax.axis_index("tp"))
    info = jnp.concatenate([jnp.stack(me).astype(jnp.int32), lengths, start])
    k = keys.transpose(1, 0, 2)
    v = values.transpose(1, 0, 2)
    q = queries[None]
    q = jnp.concatenate([q, moved(q, yh=1)], axis=0)
    q, k, v, info = together(q, k, v, info)
    vx, kx0, kx1, kx2, kx3 = prepare(info, k, v)
    q = jnp.concatenate([q] + [moved(q, a=d) for d in (1, 2, 3)], axis=0)
    q, vx, kx0, kx1, kx2, kx3 = together(q, vx, kx0, kx1, kx2, kx3)

    def neighbours(x):
        x1, x3 = moved(x, b=1), moved(x, b=3)
        half = x.shape[0] // 2
        return x1, x3, moved(x1[:half], b=1), moved(x3[half:], b=3)

    q1, q3, q2a, q2b = neighbours(q)
    kvs = tuple(range(nkv))
    own0 = attend(q, kx0, vx, kvs, 0, 4)
    q1, own0 = together(q1, own0)
    p1 = attend(q1, kx1, vx, kvs)
    r1 = moved(p1, b=-1)
    q2a, q2b, p1 = together(q2a, q2b, p1)
    p2 = attend(jnp.concatenate([q2a, q2b], axis=0), kx2, vx, kvs)
    r2 = moved(p2, b=-2)
    q3, p2, r1 = together(q3, p2, r1)
    p3 = attend(q3, kx3, vx, kvs)
    r3 = moved(p3, b=-3)
    q, p3, r2 = together(q, p3, r2)
    own1 = attend(q, kx0, vx, kvs, 4, 4)
    c = combine([own0, own1], [r1, r2, r3])
    c = combine([c[:2]], [moved(c[2 * d : 2 * d + 2], a=-d) for d in (1, 3, 2)])
    attn = finish(c, moved(c, yh=1))
    pieces = [moved(attn, a=d) for d in (1, 2, 3)]
    attn = assemble(attn, *pieces, moved(pieces[1], core=1))
    x1, x3, x2a, x2b = neighbours(attn)
    y = place(info, project(attn, out_weight), project(x1, out_weight), project(x3, out_weight), x2a, x2b, out_weight)
    y = y[:128] + moved(y[128:], core=1)
    y = y[:64] + moved(y[64:].astype(jnp.bfloat16), yl=1).astype(jnp.float32)
    return y.astype(jnp.bfloat16)


def solution(mesh):
    in_specs = (
        P("cp", "tp", None),
        P("cp", "tp", None),
        P("cp", "tp", None),
        P("cp"),
        P(),
        P("tp", "cp"),
    )
    return jax.shard_map(on_device, mesh=mesh, in_specs=in_specs, out_specs=P("tp", "cp"), check_vma=False)
```

```python
import functools
import itertools
import math

import jax
import jax.numpy as jnp
from jax import lax
from jax.experimental import pallas as pl
from jax.experimental.pallas import tpu as pltpu
from jax.sharding import PartitionSpec as P

NEG = -1e30
BIG = 2.0**100
RING = 4
MIB = 2**20


def coords(cp, tp):
    z, yh, x = cp // 8, (cp // 4) % 2, cp % 4
    yl, core = tp // 2, tp % 2
    return z, yh, x, yl, core


def moved(x, a=0, b=0, yh=0, yl=0, core=0):
    pairs = []
    for cp, tp in itertools.product(range(32), range(4)):
        zi, yhi, xi, yli, ci = coords(cp, tp)
        dz, dx = (a, b) if ci == 0 else (b, a)
        zo, xo = (zi + dz) % RING, (xi + dx) % RING
        yho, ylo, co = yhi ^ yh, yli ^ yl, ci ^ core
        pairs.append((cp * 4 + tp, ((zo * 2 + yho) * 4 + xo) * 4 + ylo * 2 + co))
    return lax.ppermute(x, ("cp", "tp"), pairs)


def together(*arrays):
    return lax.optimization_barrier(arrays)


def source(me, da, db, dy):
    z, yh, x, _, core = me
    dz = jnp.where(core == 0, da, db)
    dx = jnp.where(core == 0, db, da)
    return (z - dz) & (RING - 1), yh ^ dy, (x - dx) & (RING - 1)


def spread(row, eye):
    return jnp.sum(jnp.where(eye, row, 0.0), axis=1, keepdims=True)


def gathered_row(column, eye):
    return jnp.sum(jnp.where(eye, column, 0.0), axis=0, keepdims=True)


def diagonal():
    shape = (128, 128)
    return lax.broadcasted_iota(jnp.int32, shape, 0) == lax.broadcasted_iota(jnp.int32, shape, 1)


def stat_rows(m, l):
    high = l.astype(jnp.bfloat16).astype(jnp.float32)
    return jnp.concatenate([m, high, l - high, jnp.zeros((13, 128), jnp.float32)], axis=0).astype(jnp.bfloat16)


def prepare_kernel(info, k_ref, v_ref, vx, *masked):
    nkv, span = k_ref.shape[:2]
    me = tuple(info[i] for i in range(5))
    length, start = info[5], info[6]
    shard = (me[0] * 2 + me[1]) * 4 + me[2]
    lane = lax.broadcasted_iota(jnp.int32, (1, 128), 1)
    slot = lax.broadcasted_iota(jnp.int32, (span, 128), 0)
    for db, kx in enumerate(masked):
        z, yh, x = source(me, lane >> 4, db, (lane >> 3) & 1)
        seen = start + z * 64 + yh * 32 + x * 8 + (lane & 7) + 1 - shard * span
        seen = jnp.minimum(seen, length)
        mask = jnp.where((slot >= seen) & (lane < 64), NEG, 0.0).astype(jnp.bfloat16)
        for kv in range(nkv):
            kx[kv, :, :128] = k_ref[kv]
            kx[kv, :, 128:] = mask
    for kv in range(nkv):
        vx[kv, :, :128] = v_ref[kv]
        vx[kv, :, 128:] = jnp.ones((span, 128), jnp.bfloat16)


def prepare(info, k, v):
    vmem = pl.BlockSpec(memory_space=pltpu.VMEM)
    count = 1 + RING
    return pl.pallas_call(
        prepare_kernel,
        in_specs=[pl.BlockSpec(memory_space=pltpu.SMEM), vmem, vmem],
        out_specs=[vmem] * count,
        out_shape=[jax.ShapeDtypeStruct((*k.shape[:2], 256), jnp.bfloat16)] * count,
        compiler_params=pltpu.CompilerParams(vmem_limit_bytes=4 * MIB),
        name="prepare",
    )(info, k, v)


def attend_kernel(q_ref, kx, vx, o_ref, *, kvs, first, nb, tile, scale):
    step = pl.program_id(0)
    rows = nb * 128
    span = vx.shape[1]
    eye = diagonal()
    row = lax.broadcasted_iota(jnp.int32, (rows, 128), 0)
    lane = lax.broadcasted_iota(jnp.int32, (rows, 128), 1)
    hot = jnp.where(lane == (first + step * nb + (row >> 7)) * 8 + ((row >> 4) & 7), 1.0, 0.0).astype(jnp.bfloat16)

    def scores(i, t):
        heads = q_ref[:, :, kvs[i] * 16 : (kvs[i] + 1) * 16, :].reshape(rows, 128)
        q = jnp.concatenate([heads, hot], axis=1)
        return lax.dot_general(
            q, kx[kvs[i], pl.ds(t, tile), :], (((1,), (1,)), ((), ())), preferred_element_type=jnp.float32
        )

    def point(m):
        return jnp.maximum(m * scale, 0.01 * NEG).astype(jnp.bfloat16).astype(jnp.float32)

    def put(i, m, acc):
        for b in range(nb):
            r = slice(b * 128, (b + 1) * 128)
            o_ref[b, i, :128, :] = acc[r, :128].astype(jnp.bfloat16)
            o_ref[b, i, 128:, :] = stat_rows(gathered_row(m[r], eye), gathered_row(acc[r, 128:], eye))

    ok = []
    for i in range(len(kvs)):
        s0 = scores(i, 0)
        m = point(jnp.max(s0, axis=1, keepdims=True))
        p = []
        for t in range(0, span, tile):
            s = s0 if t == 0 else scores(i, t)
            p.append(jnp.exp2(s * scale - m).astype(jnp.bfloat16))
        acc = jnp.dot(jnp.concatenate(p, axis=1), vx[kvs[i]], preferred_element_type=jnp.float32)
        ok.append(jnp.min(jnp.where(acc[:, 128:] < BIG, 1.0, 0.0)))
        put(i, m, acc)

    @pl.when(functools.reduce(jnp.minimum, ok) < 0.5)
    def _():
        for i in range(len(kvs)):

            def top(n, m):
                s = scores(i, pl.multiple_of(n * tile, tile))
                return jnp.maximum(m, jnp.max(s, axis=1, keepdims=True))

            m = point(lax.fori_loop(0, span // tile, top, jnp.full((rows, 1), NEG, jnp.float32)))

            def add(n, acc):
                t = pl.multiple_of(n * tile, tile)
                p = jnp.exp2(scores(i, t) * scale - m).astype(jnp.bfloat16)
                return acc + jnp.dot(p, vx[kvs[i], pl.ds(t, tile), :], preferred_element_type=jnp.float32)

            put(i, m, lax.fori_loop(0, span // tile, add, jnp.zeros((rows, 256), jnp.float32)))


def attend(q, kx, vx, kvs, first=0, blocks=8):
    span = vx.shape[1]
    nb, tile = 8 // len(kvs), 256
    skip = first // nb
    vmem = pl.BlockSpec(memory_space=pltpu.VMEM)
    return pl.pallas_call(
        functools.partial(
            attend_kernel, kvs=kvs, first=first, nb=nb, tile=tile, scale=math.log2(math.e) / math.sqrt(128)
        ),
        grid=(blocks // nb,),
        in_specs=[pl.BlockSpec((nb, *q.shape[1:]), lambda i: (skip + i, 0, 0, 0)), vmem, vmem],
        out_specs=pl.BlockSpec((nb, len(kvs), 144, 128), lambda i: (i, 0, 0, 0)),
        out_shape=jax.ShapeDtypeStruct((blocks, len(kvs), 144, 128), jnp.bfloat16),
        compiler_params=pltpu.CompilerParams(vmem_limit_bytes=20 * MIB, dimension_semantics=("arbitrary",)),
        cost_estimate=pl.CostEstimate(
            flops=8 * blocks * len(kvs) * 128 * span * 128,
            bytes_accessed=4 * MIB,
            transcendentals=blocks * len(kvs) * 128 * span,
        ),
        name="attend_plane",
    )(q, kx, vx)


def merged(parts, eye):
    stats = [p[128:, :].astype(jnp.float32) for p in parts]
    m = functools.reduce(jnp.maximum, [s[0:1] for s in stats])
    total = jnp.zeros((1, 128), jnp.float32)
    out = jnp.zeros((128, 128), jnp.float32)
    for p, s in zip(parts, stats):
        factor = jnp.exp2(s[0:1] - m)
        total = total + factor * (s[1:2] + s[2:3])
        out = out + spread(factor, eye) * p[:128, :].astype(jnp.float32)
    return out, m, total


def combine_kernel(*refs, own):
    o_ref = refs[-1]
    eye = diagonal()
    for b, kv in itertools.product(range(o_ref.shape[0]), range(o_ref.shape[1])):
        share = o_ref.shape[0] // own
        out, m, total = merged([refs[b // share][b % share, kv]] + [r[b, kv] for r in refs[own:-1]], eye)
        o_ref[b, kv, :128, :] = out.astype(jnp.bfloat16)
        o_ref[b, kv, 128:, :] = stat_rows(m, total)


def combine(own, others):
    vmem = pl.BlockSpec(memory_space=pltpu.VMEM)
    return pl.pallas_call(
        functools.partial(combine_kernel, own=len(own)),
        in_specs=[vmem] * (len(own) + len(others)),
        out_specs=vmem,
        out_shape=jax.ShapeDtypeStruct(others[0].shape, jnp.bfloat16),
        compiler_params=pltpu.CompilerParams(vmem_limit_bytes=8 * MIB),
        name="combine",
    )(*own, *others)


def finish_kernel(mine, theirs, o_ref, rows, *, kv):
    eye = diagonal()
    for dy in range(2):
        out, _, total = merged([mine[dy, kv], theirs[1 - dy]], eye)
        rows[dy] = out * spread(1.0 / total, eye)
    for h in range(16):
        both = [rows[dy, pl.ds(h, 8, stride=16), :] for dy in range(2)]
        o_ref[:, h * 128 : (h + 1) * 128] = jnp.concatenate(both, axis=0).astype(jnp.bfloat16)


def finish(mine, theirs, kv):
    vmem = pl.BlockSpec(memory_space=pltpu.VMEM)
    return pl.pallas_call(
        functools.partial(finish_kernel, kv=kv),
        in_specs=[vmem, vmem],
        out_specs=vmem,
        scratch_shapes=[pltpu.VMEM((2, 128, 128), jnp.float32)],
        compiler_params=pltpu.CompilerParams(vmem_limit_bytes=4 * MIB),
        out_shape=jax.ShapeDtypeStruct((16, 2048), jnp.bfloat16),
        name="finish",
    )(mine, theirs)


def assemble_kernel(x0, x1, x2, x3, o_ref):
    for i, x in enumerate((x0, x1, x2, x3)):
        o_ref[i * x.shape[0] : (i + 1) * x.shape[0], :] = x[...]


def assemble(*pieces):
    vmem = pl.BlockSpec(memory_space=pltpu.VMEM)
    rows, width = pieces[0].shape
    return pl.pallas_call(
        assemble_kernel,
        in_specs=[vmem] * RING,
        out_specs=vmem,
        out_shape=jax.ShapeDtypeStruct((RING * rows, width), pieces[0].dtype),
        compiler_params=pltpu.CompilerParams(vmem_limit_bytes=4 * MIB),
        name="assemble",
    )(*pieces)


def times_weight(xs, w_ref, kv):
    depth = xs[0].shape[1]
    x = jnp.concatenate([x[...] for x in xs], axis=0)
    return jnp.dot(x, w_ref[kv * depth : (kv + 1) * depth, :], preferred_element_type=jnp.float32)


def project_kernel(*refs, kv):
    w_ref, o_ref = refs[-2:]
    o_ref[...] = times_weight(refs[:-2], w_ref, kv)


def project(xs, w, kv):
    vmem = pl.BlockSpec(memory_space=pltpu.VMEM)
    rows, depth = len(xs) * xs[0].shape[0], xs[0].shape[1]
    return pl.pallas_call(
        functools.partial(project_kernel, kv=kv),
        in_specs=[vmem] * (len(xs) + 1),
        out_specs=vmem,
        out_shape=jax.ShapeDtypeStruct((rows, w.shape[1]), jnp.float32),
        compiler_params=pltpu.CompilerParams(vmem_limit_bytes=8 * MIB),
        cost_estimate=pl.CostEstimate(flops=4 * rows * depth * w.shape[1], bytes_accessed=4 * MIB, transcendentals=0),
        name="project",
    )(*xs, w)


def place_kernel(info, y0, y1, x_ref, w_ref, o_ref):
    me = tuple(info[i] for i in range(5))
    yl, core = me[3], me[4]
    last = times_weight([x_ref], w_ref, 1)
    for kv, d2, d1, dy in itertools.product(range(2), range(RING), range(RING), range(2)):
        da, db = (d1, d2) if kv == 0 else (d2, d1)
        z, yh, x = source(me, da, db, dy)
        row = (((z & 1) ^ core) * 2 + ((z >> 1) ^ yl)) * 64 + yh * 32 + x * 8
        at = pl.ds(pl.multiple_of(row, 8), 8)
        within = d1 * 16 + dy * 8
        if kv == 0:
            o_ref[at, :] = y0[d2 * 64 + within : d2 * 64 + within + 8, :]
        elif d2 == 2:
            o_ref[at, :] += last[within : within + 8, :]
        else:
            i = min(d2, 2) * 64 + within
            o_ref[at, :] += y1[i : i + 8, :]


def place(info, y0, y1, x, w):
    vmem = pl.BlockSpec(memory_space=pltpu.VMEM)
    return pl.pallas_call(
        place_kernel,
        in_specs=[pl.BlockSpec(memory_space=pltpu.SMEM)] + [vmem] * 4,
        out_specs=vmem,
        out_shape=jax.ShapeDtypeStruct(y0.shape, jnp.float32),
        compiler_params=pltpu.CompilerParams(vmem_limit_bytes=8 * MIB),
        name="place",
    )(info, y0, y1, x, w)


def on_device(queries, keys, values, lengths, start, out_weight):
    nkv = keys.shape[1]
    me = coords(lax.axis_index("cp"), lax.axis_index("tp"))
    info = jnp.concatenate([jnp.stack(me).astype(jnp.int32), lengths, start])
    k = keys.transpose(1, 0, 2)
    v = values.transpose(1, 0, 2)
    q = queries[None]
    q = jnp.concatenate([q, moved(q, yh=1)], axis=0)
    q, k, v, info = together(q, k, v, info)
    vx, kx0, kx1, kx2, kx3 = prepare(info, k, v)
    q = jnp.concatenate([q] + [moved(q, a=d) for d in (1, 2, 3)], axis=0)
    q, vx, kx0, kx1, kx2, kx3 = together(q, vx, kx0, kx1, kx2, kx3)

    q1, q2, q3 = (moved(q, b=d) for d in (1, 2, 3))

    kvs = tuple(range(nkv))
    own0 = attend(q, kx0, vx, kvs, 0, 4)
    q1, own0 = together(q1, own0)
    p1 = attend(q1, kx1, vx, kvs)
    r1 = moved(p1, b=-1)
    q2, q3, p1 = together(q2, q3, p1)
    p2 = attend(q2, kx2, vx, kvs)
    r2 = moved(p2, b=-2)
    q3, p2, r1 = together(q3, p2, r1)
    p3 = attend(q3, kx3, vx, kvs)
    r3 = moved(p3, b=-3)
    q, p3, r2 = together(q, p3, r2)
    own1 = attend(q, kx0, vx, kvs, 4, 4)
    c = combine([own0, own1], [r1, r2, r3])
    c = combine([c[:2]], [moved(c[2 * d : 2 * d + 2], a=-d) for d in (1, 3, 2)])
    theirs = [moved(c[:, kv], yh=1) for kv in kvs]
    attn = finish(c, theirs[0], 0)
    pieces = [moved(attn, a=d) for d in (1, 2, 3)]
    later = finish(c, theirs[1], 1)
    others = [moved(later, b=d) for d in (1, 2, 3)]
    attn = assemble(attn, *pieces)
    attn, *others = together(attn, *others)
    x = [attn] + [moved(attn, b=d) for d in (1, 2, 3)]
    later = assemble(later, *others)
    later = [later] + [moved(later, a=d) for d in (1, 2, 3)]
    y0 = project(x, out_weight, 0)
    y0, *later = together(y0, *later[:2], later[3]) + (later[2],)
    y1 = project(later[:3], out_weight, 1)
    y = place(info, y0, y1, later[3], out_weight)
    y = y[:128] + moved(y[128:], core=1)
    y = y[:64] + moved(y[64:].astype(jnp.bfloat16), yl=1).astype(jnp.float32)
    return y.astype(jnp.bfloat16)


def solution(mesh):
    in_specs = (
        P("cp", "tp", None),
        P("cp", "tp", None),
        P("cp", "tp", None),
        P("cp"),
        P(),
        P("tp", "cp"),
    )
    return jax.shard_map(on_device, mesh=mesh, in_specs=in_specs, out_specs=P("tp", "cp"), check_vma=False)
```

```python
import functools
import itertools
import math

import jax
import jax.numpy as jnp
from jax import lax
from jax.experimental import pallas as pl
from jax.experimental.pallas import tpu as pltpu
from jax.sharding import PartitionSpec as P

NEG = -1e30
BIG = 2.0**100
RING = 4
MIB = 2**20


def coords(cp, tp):
    z, yh, x = cp // 8, (cp // 4) % 2, cp % 4
    yl, core = tp // 2, tp % 2
    return z, yh, x, yl, core


def moved(x, a=0, b=0, yh=0, yl=0, core=0):
    pairs = []
    for cp, tp in itertools.product(range(32), range(4)):
        zi, yhi, xi, yli, ci = coords(cp, tp)
        dz, dx = (a, b) if ci == 0 else (b, a)
        zo, xo = (zi + dz) % RING, (xi + dx) % RING
        yho, ylo, co = yhi ^ yh, yli ^ yl, ci ^ core
        pairs.append((cp * 4 + tp, ((zo * 2 + yho) * 4 + xo) * 4 + ylo * 2 + co))
    return lax.ppermute(x, ("cp", "tp"), pairs)


def together(*arrays):
    return lax.optimization_barrier(arrays)


def source(me, da, db, dy):
    z, yh, x, _, core = me
    dz = jnp.where(core == 0, da, db)
    dx = jnp.where(core == 0, db, da)
    return (z - dz) & (RING - 1), yh ^ dy, (x - dx) & (RING - 1)


def spread(row, eye):
    return jnp.sum(jnp.where(eye, row, 0.0), axis=1, keepdims=True)


def gathered_row(column, eye):
    return jnp.sum(jnp.where(eye, column, 0.0), axis=0, keepdims=True)


def diagonal():
    shape = (128, 128)
    return lax.broadcasted_iota(jnp.int32, shape, 0) == lax.broadcasted_iota(jnp.int32, shape, 1)


def stat_rows(m, l):
    high = l.astype(jnp.bfloat16).astype(jnp.float32)
    return jnp.concatenate([m, high, l - high, jnp.zeros((5, 128), jnp.float32)], axis=0)


def prepare_kernel(info, k_ref, v_ref, vx, *masked):
    nkv, span = k_ref.shape[:2]
    me = tuple(info[i] for i in range(5))
    length, start = info[5], info[6]
    shard = (me[0] * 2 + me[1]) * 4 + me[2]
    lane = lax.broadcasted_iota(jnp.int32, (1, 128), 1)
    slot = lax.broadcasted_iota(jnp.int32, (span, 128), 0)
    for db, kx in enumerate(masked):
        z, yh, x = source(me, lane >> 4, db, (lane >> 3) & 1)
        seen = start + z * 64 + yh * 32 + x * 8 + (lane & 7) + 1 - shard * span
        seen = jnp.minimum(seen, length)
        mask = jnp.where((slot >= seen) & (lane < 64), NEG, 0.0).astype(jnp.bfloat16)
        for kv in range(nkv):
            kx[kv, :, :128] = k_ref[kv]
            kx[kv, :, 128:] = mask
    for kv in range(nkv):
        vx[kv, :, :128] = v_ref[kv]
        vx[kv, :, 128:] = jnp.ones((span, 128), jnp.bfloat16)


def prepare(info, k, v):
    vmem = pl.BlockSpec(memory_space=pltpu.VMEM)
    count = 1 + RING
    return pl.pallas_call(
        prepare_kernel,
        in_specs=[pl.BlockSpec(memory_space=pltpu.SMEM), vmem, vmem],
        out_specs=[vmem] * count,
        out_shape=[jax.ShapeDtypeStruct((*k.shape[:2], 256), jnp.bfloat16)] * count,
        compiler_params=pltpu.CompilerParams(vmem_limit_bytes=4 * MIB),
        name="prepare",
    )(info, k, v)


def attend_kernel(q_ref, kx, vx, o_ref, *, kvs, first, nb, tile, scale):
    step = pl.program_id(0)
    rows = nb * 128
    span = vx.shape[1]
    eye = diagonal()
    row = lax.broadcasted_iota(jnp.int32, (rows, 128), 0)
    lane = lax.broadcasted_iota(jnp.int32, (rows, 128), 1)
    hot = jnp.where(lane == (first + step * nb + (row >> 7)) * 8 + ((row >> 4) & 7), 1.0, 0.0).astype(jnp.bfloat16)

    def scores(i, t):
        heads = q_ref[:, :, kvs[i] * 16 : (kvs[i] + 1) * 16, :].reshape(rows, 128)
        q = jnp.concatenate([heads, hot], axis=1)
        return lax.dot_general(
            q, kx[kvs[i], pl.ds(t, tile), :], (((1,), (1,)), ((), ())), preferred_element_type=jnp.float32
        )

    def point(m):
        return jnp.maximum(m * scale, 0.01 * NEG).astype(jnp.bfloat16).astype(jnp.float32)

    def put(results):
        for b in range(nb):
            r = slice(b * 128, (b + 1) * 128)
            stats = []
            for i, (m, acc) in enumerate(results):
                o_ref[b, i * 128 : (i + 1) * 128, :] = acc[r, :128].astype(jnp.bfloat16)
                stats.append(stat_rows(gathered_row(m[r], eye), gathered_row(acc[r, 128:], eye)))
            o_ref[b, len(results) * 128 :, :] = jnp.concatenate(stats, axis=0).astype(jnp.bfloat16)

    ok, results = [], []
    for i in range(len(kvs)):
        s0 = scores(i, 0)
        m = point(jnp.max(s0, axis=1, keepdims=True))
        p = []
        for t in range(0, span, tile):
            s = s0 if t == 0 else scores(i, t)
            p.append(jnp.exp2(s * scale - m).astype(jnp.bfloat16))
        acc = jnp.dot(jnp.concatenate(p, axis=1), vx[kvs[i]], preferred_element_type=jnp.float32)
        ok.append(jnp.min(jnp.where(acc[:, 128:] < BIG, 1.0, 0.0)))
        results.append((m, acc))
    put(results)

    @pl.when(functools.reduce(jnp.minimum, ok) < 0.5)
    def _():
        results = []
        for i in range(len(kvs)):

            def top(n, m):
                s = scores(i, pl.multiple_of(n * tile, tile))
                return jnp.maximum(m, jnp.max(s, axis=1, keepdims=True))

            m = point(lax.fori_loop(0, span // tile, top, jnp.full((rows, 1), NEG, jnp.float32)))

            def add(n, acc):
                t = pl.multiple_of(n * tile, tile)
                p = jnp.exp2(scores(i, t) * scale - m).astype(jnp.bfloat16)
                return acc + jnp.dot(p, vx[kvs[i], pl.ds(t, tile), :], preferred_element_type=jnp.float32)

            results.append((m, lax.fori_loop(0, span // tile, add, jnp.zeros((rows, 256), jnp.float32))))
        put(results)


def attend(q, kx, vx, kvs, first=0, blocks=8):
    span = vx.shape[1]
    nb, tile = 8 // len(kvs), 256
    skip = first // nb
    vmem = pl.BlockSpec(memory_space=pltpu.VMEM)
    return pl.pallas_call(
        functools.partial(
            attend_kernel, kvs=kvs, first=first, nb=nb, tile=tile, scale=math.log2(math.e) / math.sqrt(128)
        ),
        grid=(blocks // nb,),
        in_specs=[pl.BlockSpec((nb, *q.shape[1:]), lambda i: (skip + i, 0, 0, 0)), vmem, vmem],
        out_specs=pl.BlockSpec((nb, len(kvs) * 136, 128), lambda i: (i, 0, 0)),
        out_shape=jax.ShapeDtypeStruct((blocks, len(kvs) * 136, 128), jnp.bfloat16),
        compiler_params=pltpu.CompilerParams(vmem_limit_bytes=20 * MIB, dimension_semantics=("arbitrary",)),
        cost_estimate=pl.CostEstimate(
            flops=8 * blocks * len(kvs) * 128 * span * 128,
            bytes_accessed=4 * MIB,
            transcendentals=blocks * len(kvs) * 128 * span,
        ),
        name="attend_plane",
    )(q, kx, vx)


def merged(parts, kv, nkv, eye):
    stats = [p[nkv * 128 :, :].astype(jnp.float32)[kv * 8 : kv * 8 + 8] for p in parts]
    m = functools.reduce(jnp.maximum, [s[0:1] for s in stats])
    total = jnp.zeros((1, 128), jnp.float32)
    out = jnp.zeros((128, 128), jnp.float32)
    for p, s in zip(parts, stats):
        factor = jnp.exp2(s[0:1] - m)
        total = total + factor * (s[1:2] + s[2:3])
        out = out + spread(factor, eye) * p[kv * 128 : (kv + 1) * 128, :].astype(jnp.float32)
    return out, m, total


def combine_kernel(*refs, pieces):
    o_ref = refs[-1]
    blocks, nkv = o_ref.shape[0], o_ref.shape[1] // 136
    eye = diagonal()
    for b in range(blocks):
        parts, at = [], 0
        for count in pieces:
            share = blocks // count
            parts.append(refs[at + b // share].at[b % share])
            at += count
        stats = []
        for kv in range(nkv):
            out, m, total = merged(parts, kv, nkv, eye)
            o_ref[b, kv * 128 : (kv + 1) * 128, :] = out.astype(jnp.bfloat16)
            stats.append(stat_rows(m, total))
        o_ref[b, nkv * 128 :, :] = jnp.concatenate(stats, axis=0).astype(jnp.bfloat16)


def combine(parts):
    vmem = pl.BlockSpec(memory_space=pltpu.VMEM)
    flat = [piece for part in parts for piece in part]
    blocks = sum(piece.shape[0] for piece in parts[0])
    return pl.pallas_call(
        functools.partial(combine_kernel, pieces=[len(part) for part in parts]),
        in_specs=[vmem] * len(flat),
        out_specs=vmem,
        out_shape=jax.ShapeDtypeStruct((blocks, *flat[0].shape[1:]), jnp.bfloat16),
        compiler_params=pltpu.CompilerParams(vmem_limit_bytes=8 * MIB),
        name="combine",
    )(*flat)


def finish_kernel(mine, theirs, o_ref, rows):
    eye = diagonal()
    nkv = mine.shape[1] // 136
    for kv in range(nkv):
        for dy in range(2):
            out, _, total = merged([mine.at[dy], theirs.at[1 - dy]], kv, nkv, eye)
            rows[kv, dy] = out * spread(1.0 / total, eye)
    for kv, h in itertools.product(range(nkv), range(16)):
        c = (kv * 16 + h) * 128
        both = [rows[kv, dy, pl.ds(h, 8, stride=16), :] for dy in range(2)]
        o_ref[:, c : c + 128] = jnp.concatenate(both, axis=0).astype(jnp.bfloat16)


def finish(mine, theirs):
    vmem = pl.BlockSpec(memory_space=pltpu.VMEM)
    nkv = mine.shape[1] // 136
    return pl.pallas_call(
        finish_kernel,
        in_specs=[vmem, vmem],
        out_specs=vmem,
        scratch_shapes=[pltpu.VMEM((nkv, 2, 128, 128), jnp.float32)],
        compiler_params=pltpu.CompilerParams(vmem_limit_bytes=4 * MIB),
        out_shape=jax.ShapeDtypeStruct((16, nkv * 2048), jnp.bfloat16),
        name="finish",
    )(mine, theirs)


def assemble_kernel(x0, x1, x2, x3, _, o_ref):
    for i, x in enumerate((x0, x1, x2, x3)):
        o_ref[i * x.shape[0] : (i + 1) * x.shape[0], :] = x[...]


def assemble(*pieces):
    vmem = pl.BlockSpec(memory_space=pltpu.VMEM)
    rows, width = pieces[0].shape
    return pl.pallas_call(
        assemble_kernel,
        in_specs=[vmem] * 4 + [pl.BlockSpec(memory_space=pl.ANY)],
        out_specs=vmem,
        out_shape=jax.ShapeDtypeStruct((RING * rows, width), pieces[0].dtype),
        compiler_params=pltpu.CompilerParams(vmem_limit_bytes=4 * MIB),
        name="assemble",
    )(*pieces)


def project_kernel(x_ref, w_ref, o_ref):
    o_ref[...] = jnp.dot(x_ref[...], w_ref[...], preferred_element_type=jnp.float32)


def project(x, w):
    vmem = pl.BlockSpec(memory_space=pltpu.VMEM)
    return pl.pallas_call(
        project_kernel,
        in_specs=[vmem, vmem],
        out_specs=vmem,
        out_shape=jax.ShapeDtypeStruct((x.shape[0], w.shape[1]), jnp.float32),
        compiler_params=pltpu.CompilerParams(vmem_limit_bytes=8 * MIB),
        cost_estimate=pl.CostEstimate(
            flops=8 * x.shape[0] * w.shape[0] * w.shape[1], bytes_accessed=4 * MIB, transcendentals=0
        ),
        name="project",
    )(x, w)


def place_kernel(info, y0, y1, y3, x_ref, w_ref, o_ref):
    me = tuple(info[i] for i in range(5))
    yl, core = me[3], me[4]
    y2 = jnp.dot(x_ref[...], w_ref[...], preferred_element_type=jnp.float32)
    for db, y in ((0, y0), (1, y1), (2, y2), (3, y3)):
        for da, dy in itertools.product(range(RING), range(2)):
            z, yh, xx = source(me, da, db, dy)
            row = (((z & 1) ^ core) * 2 + ((z >> 1) ^ yl)) * 64 + yh * 32 + xx * 8
            at = da * 16 + dy * 8
            o_ref[pl.ds(pl.multiple_of(row, 8), 8), :] = y[at : at + 8, :]


def place(info, y0, y1, y3, x, w):
    vmem = pl.BlockSpec(memory_space=pltpu.VMEM)
    return pl.pallas_call(
        place_kernel,
        in_specs=[pl.BlockSpec(memory_space=pltpu.SMEM)] + [vmem] * 5,
        out_specs=vmem,
        out_shape=jax.ShapeDtypeStruct((RING * y0.shape[0], w.shape[1]), jnp.float32),
        compiler_params=pltpu.CompilerParams(vmem_limit_bytes=8 * MIB),
        name="place",
    )(info, y0, y1, y3, x, w)


def on_device(queries, keys, values, lengths, start, out_weight):
    nkv = keys.shape[1]
    me = coords(lax.axis_index("cp"), lax.axis_index("tp"))
    info = jnp.concatenate([jnp.stack(me).astype(jnp.int32), lengths, start])
    k = keys.transpose(1, 0, 2)
    v = values.transpose(1, 0, 2)
    q = queries[None]
    q = jnp.concatenate([q, moved(q, yh=1)], axis=0)
    q, k, v, info = together(q, k, v, info)
    vx, kx0, kx1, kx2, kx3 = prepare(info, k, v)
    q2, q1, q3 = (moved(q, a=d) for d in (2, 1, 3))
    q = jnp.concatenate([q, q1, q2, q3], axis=0)
    q, vx, kx0, kx1, kx2, kx3 = together(q, vx, kx0, kx1, kx2, kx3)

    q1, q2, q3 = (moved(q, b=d) for d in (1, 2, 3))

    kvs = tuple(range(nkv))
    own0 = attend(q, kx0, vx, kvs, 0, 4)
    q1, own0 = together(q1, own0)
    p1 = attend(q1, kx1, vx, kvs)
    r1 = moved(p1, b=-1)
    q2, q3, p1 = together(q2, q3, p1)
    p2 = attend(q2, kx2, vx, kvs)
    r2 = moved(p2, b=-2)
    q3, p2, r1 = together(q3, p2, r1)
    p3a = attend(q3, kx3, vx, kvs, 0, 4)
    r3a = moved(p3a, b=-3)
    q3, p3a = together(q3, p3a)
    p3b = attend(q3, kx3, vx, kvs, 4, 4)
    r3b = moved(p3b, b=-3)
    q, p3b, r2, r3a = together(q, p3b, r2, r3a)
    own1 = attend(q, kx0, vx, kvs, 4, 4)
    c = combine([[own0, own1], [r1], [r2], [r3a, r3b]])
    c = combine([[c[:2]]] + [[moved(c[2 * d : 2 * d + 2], a=-d)] for d in (2, 1, 3)])
    attn = finish(c, moved(c, yh=1))
    x2, x1, x3 = (moved(attn, a=d) for d in (2, 1, 3))
    attn = assemble(attn, x1, x2, x3, moved(x2, core=1))
    x1, x3, x2 = (moved(attn, b=d) for d in (1, 3, 2))
    y = place(info, project(attn, out_weight), project(x1, out_weight), project(x3, out_weight), x2, out_weight)
    y = y[:128] + moved(y[128:], core=1)
    y = y[:64] + moved(y[64:].astype(jnp.bfloat16), yl=1).astype(jnp.float32)
    return y.astype(jnp.bfloat16)


def solution(mesh):
    in_specs = (
        P("cp", "tp", None),
        P("cp", "tp", None),
        P("cp", "tp", None),
        P("cp"),
        P(),
        P("tp", "cp"),
    )
    return jax.shard_map(on_device, mesh=mesh, in_specs=in_specs, out_specs=P("tp", "cp"), check_vma=False)
```

```python
import functools
import itertools
import math

import jax
import jax.numpy as jnp
from jax import lax
from jax.experimental import pallas as pl
from jax.experimental.pallas import tpu as pltpu
from jax.sharding import PartitionSpec as P

NEG = -1e30
BIG = 2.0**100
RING = 4
MIB = 2**20


def coords(cp, tp):
    z, yh, x = cp // 8, (cp // 4) % 2, cp % 4
    yl, core = tp // 2, tp % 2
    return z, yh, x, yl, core


def moved(x, a=0, b=0, yh=0, yl=0, core=0):
    pairs = []
    for cp, tp in itertools.product(range(32), range(4)):
        zi, yhi, xi, yli, ci = coords(cp, tp)
        dz, dx = (a, b) if ci == 0 else (b, a)
        zo, xo = (zi + dz) % RING, (xi + dx) % RING
        yho, ylo, co = yhi ^ yh, yli ^ yl, ci ^ core
        pairs.append((cp * 4 + tp, ((zo * 2 + yho) * 4 + xo) * 4 + ylo * 2 + co))
    return lax.ppermute(x, ("cp", "tp"), pairs)


def together(*arrays):
    return lax.optimization_barrier(arrays)


def source(me, da, db, dy):
    z, yh, x, _, core = me
    dz = jnp.where(core == 0, da, db)
    dx = jnp.where(core == 0, db, da)
    return (z - dz) & (RING - 1), yh ^ dy, (x - dx) & (RING - 1)


def spread(row, eye):
    return jnp.sum(jnp.where(eye, row, 0.0), axis=1, keepdims=True)


def gathered_row(column, eye):
    return jnp.sum(jnp.where(eye, column, 0.0), axis=0, keepdims=True)


def diagonal():
    shape = (128, 128)
    return lax.broadcasted_iota(jnp.int32, shape, 0) == lax.broadcasted_iota(jnp.int32, shape, 1)


def stat_rows(m, l):
    high = l.astype(jnp.bfloat16).astype(jnp.float32)
    return jnp.concatenate([m, high, l - high, jnp.zeros((5, 128), jnp.float32)], axis=0)


def prepare_kernel(info, k_ref, v_ref, vx, *masked):
    nkv, span = k_ref.shape[:2]
    me = tuple(info[i] for i in range(5))
    length, start = info[5], info[6]
    shard = (me[0] * 2 + me[1]) * 4 + me[2]
    lane = lax.broadcasted_iota(jnp.int32, (1, 128), 1)
    slot = lax.broadcasted_iota(jnp.int32, (span, 128), 0)
    for db, kx in enumerate(masked):
        z, yh, x = source(me, lane >> 4, db, (lane >> 3) & 1)
        seen = start + z * 64 + yh * 32 + x * 8 + (lane & 7) + 1 - shard * span
        seen = jnp.minimum(seen, length)
        mask = jnp.where((slot >= seen) & (lane < 64), NEG, 0.0).astype(jnp.bfloat16)
        for kv in range(nkv):
            kx[kv, :, :128] = k_ref[kv]
            kx[kv, :, 128:] = mask
    for kv in range(nkv):
        vx[kv, :, :128] = v_ref[kv]
        vx[kv, :, 128:] = jnp.ones((span, 128), jnp.bfloat16)


def prepare(info, k, v):
    vmem = pl.BlockSpec(memory_space=pltpu.VMEM)
    count = 1 + RING
    return pl.pallas_call(
        prepare_kernel,
        in_specs=[pl.BlockSpec(memory_space=pltpu.SMEM), vmem, vmem],
        out_specs=[vmem] * count,
        out_shape=[jax.ShapeDtypeStruct((*k.shape[:2], 256), jnp.bfloat16)] * count,
        compiler_params=pltpu.CompilerParams(vmem_limit_bytes=4 * MIB),
        name="prepare",
    )(info, k, v)


def attend_kernel(q_ref, kx, vx, o_ref, *, kvs, first, nb, tile, scale):
    step = pl.program_id(0)
    span = vx.shape[1]
    eye = diagonal()

    def rows_of(b, count):
        row = lax.broadcasted_iota(jnp.int32, (count * 128, 128), 0)
        lane = lax.broadcasted_iota(jnp.int32, (count * 128, 128), 1)
        token = (first + step * nb + b + (row >> 7)) * 8 + ((row >> 4) & 7)
        hot = jnp.where(lane == token, 1.0, 0.0).astype(jnp.bfloat16)
        heads = [q_ref[pl.ds(b, count), :, kv * 16 : (kv + 1) * 16, :].reshape(count * 128, 128) for kv in kvs]
        return [jnp.concatenate([h, hot], axis=1) for h in heads]

    def scores(q, kv, t):
        return lax.dot_general(
            q, kx[kv, pl.ds(t, tile), :], (((1,), (1,)), ((), ())), preferred_element_type=jnp.float32
        )

    def point(m):
        return jnp.maximum(m * scale, 0.01 * NEG).astype(jnp.bfloat16).astype(jnp.float32)

    def put(b, r, results):
        stats = []
        for i, (m, acc) in enumerate(results):
            o_ref[b, i * 128 : (i + 1) * 128, :] = acc[r, :128].astype(jnp.bfloat16)
            stats.append(stat_rows(gathered_row(m[r], eye), gathered_row(acc[r, 128:], eye)))
        o_ref[b, len(results) * 128 :, :] = jnp.concatenate(stats, axis=0).astype(jnp.bfloat16)

    ok, results = [], []
    for q, kv in zip(rows_of(0, nb), kvs):
        s0 = scores(q, kv, 0)
        m = point(jnp.max(s0, axis=1, keepdims=True))
        p = []
        for t in range(0, span, tile):
            s = s0 if t == 0 else scores(q, kv, t)
            p.append(jnp.exp2(s * scale - m).astype(jnp.bfloat16))
        acc = jnp.dot(jnp.concatenate(p, axis=1), vx[kv], preferred_element_type=jnp.float32)
        ok.append(jnp.min(jnp.where(acc[:, 128:] < BIG, 1.0, 0.0)))
        results.append((m, acc))
    for b in range(nb):
        put(b, slice(b * 128, (b + 1) * 128), results)

    @pl.when(functools.reduce(jnp.minimum, ok) < 0.5)
    def _():
        def block(b, _):
            results = []
            for q, kv in zip(rows_of(b, 1), kvs):

                def top(n, m):
                    s = scores(q, kv, pl.multiple_of(n * tile, tile))
                    return jnp.maximum(m, jnp.max(s, axis=1, keepdims=True))

                m = point(lax.fori_loop(0, span // tile, top, jnp.full((128, 1), NEG, jnp.float32)))

                def add(n, acc):
                    t = pl.multiple_of(n * tile, tile)
                    p = jnp.exp2(scores(q, kv, t) * scale - m).astype(jnp.bfloat16)
                    return acc + jnp.dot(p, vx[kv, pl.ds(t, tile), :], preferred_element_type=jnp.float32)

                results.append((m, lax.fori_loop(0, span // tile, add, jnp.zeros((128, 256), jnp.float32))))
            put(b, slice(0, 128), results)
            return 0

        lax.fori_loop(0, nb, block, 0)


def attend(q, kx, vx, kvs, first=0, blocks=8):
    span = vx.shape[1]
    nb, tile = 8 // len(kvs), 256
    skip = first // nb
    vmem = pl.BlockSpec(memory_space=pltpu.VMEM)
    return pl.pallas_call(
        functools.partial(
            attend_kernel, kvs=kvs, first=first, nb=nb, tile=tile, scale=math.log2(math.e) / math.sqrt(128)
        ),
        grid=(blocks // nb,),
        in_specs=[pl.BlockSpec((nb, *q.shape[1:]), lambda i: (skip + i, 0, 0, 0)), vmem, vmem],
        out_specs=pl.BlockSpec((nb, len(kvs) * 136, 128), lambda i: (i, 0, 0)),
        out_shape=jax.ShapeDtypeStruct((blocks, len(kvs) * 136, 128), jnp.bfloat16),
        compiler_params=pltpu.CompilerParams(vmem_limit_bytes=20 * MIB, dimension_semantics=("arbitrary",)),
        cost_estimate=pl.CostEstimate(
            flops=8 * blocks * len(kvs) * 128 * span * 128,
            bytes_accessed=4 * MIB,
            transcendentals=blocks * len(kvs) * 128 * span,
        ),
        name="attend_plane",
    )(q, kx, vx)


def merged(parts, kv, nkv, eye):
    stats = [p[nkv * 128 :, :].astype(jnp.float32)[kv * 8 : kv * 8 + 8] for p in parts]
    m = functools.reduce(jnp.maximum, [s[0:1] for s in stats])
    total = jnp.zeros((1, 128), jnp.float32)
    out = jnp.zeros((128, 128), jnp.float32)
    for p, s in zip(parts, stats):
        factor = jnp.exp2(s[0:1] - m)
        total = total + factor * (s[1:2] + s[2:3])
        out = out + spread(factor, eye) * p[kv * 128 : (kv + 1) * 128, :].astype(jnp.float32)
    return out, m, total


def combine_kernel(*refs, pieces):
    o_ref = refs[-1]
    blocks, nkv = o_ref.shape[0], o_ref.shape[1] // 136
    eye = diagonal()
    for b in range(blocks):
        parts, at = [], 0
        for count in pieces:
            share = blocks // count
            parts.append(refs[at + b // share].at[b % share])
            at += count
        stats = []
        for kv in range(nkv):
            out, m, total = merged(parts, kv, nkv, eye)
            o_ref[b, kv * 128 : (kv + 1) * 128, :] = out.astype(jnp.bfloat16)
            stats.append(stat_rows(m, total))
        o_ref[b, nkv * 128 :, :] = jnp.concatenate(stats, axis=0).astype(jnp.bfloat16)


def combine(parts):
    vmem = pl.BlockSpec(memory_space=pltpu.VMEM)
    flat = [piece for part in parts for piece in part]
    blocks = sum(piece.shape[0] for piece in parts[0])
    return pl.pallas_call(
        functools.partial(combine_kernel, pieces=[len(part) for part in parts]),
        in_specs=[vmem] * len(flat),
        out_specs=vmem,
        out_shape=jax.ShapeDtypeStruct((blocks, *flat[0].shape[1:]), jnp.bfloat16),
        compiler_params=pltpu.CompilerParams(vmem_limit_bytes=8 * MIB),
        name="combine",
    )(*flat)


def finish_kernel(mine, theirs, o_ref, rows):
    eye = diagonal()
    nkv = mine.shape[1] // 136
    for kv in range(nkv):
        for dy in range(2):
            out, _, total = merged([mine.at[dy], theirs.at[1 - dy]], kv, nkv, eye)
            rows[kv, dy] = out * spread(1.0 / total, eye)
    for kv, h in itertools.product(range(nkv), range(16)):
        c = (kv * 16 + h) * 128
        both = [rows[kv, dy, pl.ds(h, 8, stride=16), :] for dy in range(2)]
        o_ref[:, c : c + 128] = jnp.concatenate(both, axis=0).astype(jnp.bfloat16)


def finish(mine, theirs):
    vmem = pl.BlockSpec(memory_space=pltpu.VMEM)
    nkv = mine.shape[1] // 136
    return pl.pallas_call(
        finish_kernel,
        in_specs=[vmem, vmem],
        out_specs=vmem,
        scratch_shapes=[pltpu.VMEM((nkv, 2, 128, 128), jnp.float32)],
        compiler_params=pltpu.CompilerParams(vmem_limit_bytes=4 * MIB),
        out_shape=jax.ShapeDtypeStruct((16, nkv * 2048), jnp.bfloat16),
        name="finish",
    )(mine, theirs)


def assemble_kernel(x0, x1, x2, x3, _, o_ref):
    for i, x in enumerate((x0, x1, x2, x3)):
        o_ref[i * x.shape[0] : (i + 1) * x.shape[0], :] = x[...]


def assemble(*pieces):
    vmem = pl.BlockSpec(memory_space=pltpu.VMEM)
    rows, width = pieces[0].shape
    return pl.pallas_call(
        assemble_kernel,
        in_specs=[vmem] * 4 + [pl.BlockSpec(memory_space=pl.ANY)],
        out_specs=vmem,
        out_shape=jax.ShapeDtypeStruct((RING * rows, width), pieces[0].dtype),
        compiler_params=pltpu.CompilerParams(vmem_limit_bytes=4 * MIB),
        name="assemble",
    )(*pieces)


def project_kernel(x_ref, w_ref, o_ref):
    o_ref[...] = jnp.dot(x_ref[...], w_ref[...], preferred_element_type=jnp.float32)


def project(x, w):
    vmem = pl.BlockSpec(memory_space=pltpu.VMEM)
    return pl.pallas_call(
        project_kernel,
        in_specs=[vmem, vmem],
        out_specs=vmem,
        out_shape=jax.ShapeDtypeStruct((x.shape[0], w.shape[1]), jnp.float32),
        compiler_params=pltpu.CompilerParams(vmem_limit_bytes=8 * MIB),
        cost_estimate=pl.CostEstimate(
            flops=8 * x.shape[0] * w.shape[0] * w.shape[1], bytes_accessed=4 * MIB, transcendentals=0
        ),
        name="project",
    )(x, w)


def place_kernel(info, y0, y1, y3, x_ref, w_ref, o_ref):
    me = tuple(info[i] for i in range(5))
    yl, core = me[3], me[4]
    y2 = jnp.dot(x_ref[...], w_ref[...], preferred_element_type=jnp.float32)
    for db, y in ((0, y0), (1, y1), (2, y2), (3, y3)):
        for da, dy in itertools.product(range(RING), range(2)):
            z, yh, xx = source(me, da, db, dy)
            row = (((z & 1) ^ core) * 2 + ((z >> 1) ^ yl)) * 64 + yh * 32 + xx * 8
            at = da * 16 + dy * 8
            o_ref[pl.ds(pl.multiple_of(row, 8), 8), :] = y[at : at + 8, :]


def place(info, y0, y1, y3, x, w):
    vmem = pl.BlockSpec(memory_space=pltpu.VMEM)
    return pl.pallas_call(
        place_kernel,
        in_specs=[pl.BlockSpec(memory_space=pltpu.SMEM)] + [vmem] * 5,
        out_specs=vmem,
        out_shape=jax.ShapeDtypeStruct((RING * y0.shape[0], w.shape[1]), jnp.float32),
        compiler_params=pltpu.CompilerParams(vmem_limit_bytes=8 * MIB),
        name="place",
    )(info, y0, y1, y3, x, w)


def on_device(queries, keys, values, lengths, start, out_weight):
    nkv = keys.shape[1]
    me = coords(lax.axis_index("cp"), lax.axis_index("tp"))
    info = jnp.concatenate([jnp.stack(me).astype(jnp.int32), lengths, start])
    k = keys.transpose(1, 0, 2)
    v = values.transpose(1, 0, 2)
    q = queries[None]
    q = jnp.concatenate([q, moved(q, yh=1)], axis=0)
    q, k, v, info = together(q, k, v, info)
    vx, kx0, kx1, kx2, kx3 = prepare(info, k, v)
    q2, q1, q3 = (moved(q, a=d) for d in (2, 1, 3))
    q = jnp.concatenate([q, q1, q2, q3], axis=0)
    q, vx, kx0, kx1, kx2, kx3 = together(q, vx, kx0, kx1, kx2, kx3)

    q1, q2, q3 = (moved(q, b=d) for d in (1, 2, 3))

    kvs = tuple(range(nkv))
    own0 = attend(q, kx0, vx, kvs, 0, 4)
    q1, own0 = together(q1, own0)
    p1 = attend(q1, kx1, vx, kvs)
    r1 = moved(p1, b=-1)
    q2, q3, p1 = together(q2, q3, p1)
    p2 = attend(q2, kx2, vx, kvs)
    r2 = moved(p2, b=-2)
    q3, p2, r1 = together(q3, p2, r1)
    p3a = attend(q3, kx3, vx, kvs, 0, 4)
    r3a = moved(p3a, b=-3)
    q3, p3a = together(q3, p3a)
    p3b = attend(q3, kx3, vx, kvs, 4, 4)
    r3b = moved(p3b, b=-3)
    q, p3b, r2, r3a = together(q, p3b, r2, r3a)
    own1 = attend(q, kx0, vx, kvs, 4, 4)
    c = combine([[own0, own1], [r1], [r2], [r3a, r3b]])
    c = combine([[c[:2]]] + [[moved(c[2 * d : 2 * d + 2], a=-d)] for d in (2, 1, 3)])
    attn = finish(c, moved(c, yh=1))
    x2, x1, x3 = (moved(attn, a=d) for d in (2, 1, 3))
    attn = assemble(attn, x1, x2, x3, moved(x2, core=1))
    x1, x3, x2 = (moved(attn, b=d) for d in (1, 3, 2))
    y = place(info, project(attn, out_weight), project(x1, out_weight), project(x3, out_weight), x2, out_weight)
    y = y[:128] + moved(y[128:], core=1)
    y = y[:64] + moved(y[64:].astype(jnp.bfloat16), yl=1).astype(jnp.float32)
    return y.astype(jnp.bfloat16)


def solution(mesh):
    in_specs = (
        P("cp", "tp", None),
        P("cp", "tp", None),
        P("cp", "tp", None),
        P("cp"),
        P(),
        P("tp", "cp"),
    )
    return jax.shard_map(on_device, mesh=mesh, in_specs=in_specs, out_specs=P("tp", "cp"), check_vma=False)
```

```python
import functools
import itertools
import math

import jax
import jax.numpy as jnp
from jax import lax
from jax.experimental import pallas as pl
from jax.experimental.pallas import tpu as pltpu
from jax.sharding import PartitionSpec as P

NEG = -1e30
BIG = 2.0**100
RING = 4
MIB = 2**20


def coords(cp, tp):
    z, yh, x = cp // 8, (cp // 4) % 2, cp % 4
    yl, core = tp // 2, tp % 2
    return z, yh, x, yl, core


def moved(x, a=0, b=0, yh=0, yl=0, core=0):
    pairs = []
    for cp, tp in itertools.product(range(32), range(4)):
        zi, yhi, xi, yli, ci = coords(cp, tp)
        dz, dx = (a, b) if ci == 0 else (b, a)
        zo, xo = (zi + dz) % RING, (xi + dx) % RING
        yho, ylo, co = yhi ^ yh, yli ^ yl, ci ^ core
        pairs.append((cp * 4 + tp, ((zo * 2 + yho) * 4 + xo) * 4 + ylo * 2 + co))
    return lax.ppermute(x, ("cp", "tp"), pairs)


def together(*arrays):
    return lax.optimization_barrier(arrays)


def source(me, da, db, dy):
    z, yh, x, _, core = me
    dz = jnp.where(core == 0, da, db)
    dx = jnp.where(core == 0, db, da)
    return (z - dz) & (RING - 1), yh ^ dy, (x - dx) & (RING - 1)


def spread(row, eye):
    return jnp.sum(jnp.where(eye, row, 0.0), axis=1, keepdims=True)


def gathered_row(column, eye):
    return jnp.sum(jnp.where(eye, column, 0.0), axis=0, keepdims=True)


def diagonal():
    shape = (128, 128)
    return lax.broadcasted_iota(jnp.int32, shape, 0) == lax.broadcasted_iota(jnp.int32, shape, 1)


def stat_rows(m, l):
    high = l.astype(jnp.bfloat16).astype(jnp.float32)
    return jnp.concatenate([m, high, l - high, jnp.zeros((5, 128), jnp.float32)], axis=0)


def prepare_kernel(info, k_ref, v_ref, vx, *masked):
    nkv, span = k_ref.shape[:2]
    me = tuple(info[i] for i in range(5))
    length, start = info[5], info[6]
    shard = (me[0] * 2 + me[1]) * 4 + me[2]
    lane = lax.broadcasted_iota(jnp.int32, (1, 128), 1)
    slot = lax.broadcasted_iota(jnp.int32, (span, 128), 0)
    for db, kx in enumerate(masked):
        z, yh, x = source(me, lane >> 4, db, (lane >> 3) & 1)
        seen = start + z * 64 + yh * 32 + x * 8 + (lane & 7) + 1 - shard * span
        seen = jnp.minimum(seen, length)
        mask = jnp.where((slot >= seen) & (lane < 64), NEG, 0.0).astype(jnp.bfloat16)
        for kv in range(nkv):
            kx[kv, :, :128] = k_ref[kv]
            kx[kv, :, 128:] = mask
    for kv in range(nkv):
        vx[kv, :, :128] = v_ref[kv]
        vx[kv, :, 128:] = jnp.ones((span, 128), jnp.bfloat16)


def prepare(info, k, v):
    vmem = pl.BlockSpec(memory_space=pltpu.VMEM)
    count = 1 + RING
    return pl.pallas_call(
        prepare_kernel,
        in_specs=[pl.BlockSpec(memory_space=pltpu.SMEM), vmem, vmem],
        out_specs=[vmem] * count,
        out_shape=[jax.ShapeDtypeStruct((*k.shape[:2], 256), jnp.bfloat16)] * count,
        compiler_params=pltpu.CompilerParams(vmem_limit_bytes=4 * MIB),
        name="prepare",
    )(info, k, v)


def attend_kernel(q_ref, kx, vx, o_ref, *, kvs, first, nb, tile, scale):
    step = pl.program_id(0)
    span = vx.shape[1]
    eye = diagonal()

    def rows_of(b, count):
        row = lax.broadcasted_iota(jnp.int32, (count * 128, 128), 0)
        lane = lax.broadcasted_iota(jnp.int32, (count * 128, 128), 1)
        token = (first + step * nb + b + (row >> 7)) * 8 + ((row >> 4) & 7)
        hot = jnp.where(lane == token, 1.0, 0.0).astype(jnp.bfloat16)
        heads = [q_ref[pl.ds(b, count), :, kv * 16 : (kv + 1) * 16, :].reshape(count * 128, 128) for kv in kvs]
        return [jnp.concatenate([h, hot], axis=1) for h in heads]

    def scores(q, kv, t):
        return lax.dot_general(
            q, kx[kv, pl.ds(t, tile), :], (((1,), (1,)), ((), ())), preferred_element_type=jnp.float32
        )

    def point(m):
        return jnp.maximum(m * scale, 0.01 * NEG).astype(jnp.bfloat16).astype(jnp.float32)

    def put(b, r, results):
        stats = []
        for i, (m, acc) in enumerate(results):
            o_ref[b, i * 128 : (i + 1) * 128, :] = acc[r, :128].astype(jnp.bfloat16)
            stats.append(stat_rows(gathered_row(m[r], eye), gathered_row(acc[r, 128:], eye)))
        o_ref[b, len(results) * 128 :, :] = jnp.concatenate(stats, axis=0).astype(jnp.bfloat16)

    ok, results = [], []
    for q, kv in zip(rows_of(0, nb), kvs):
        s0 = scores(q, kv, 0)
        m = point(jnp.max(s0, axis=1, keepdims=True))
        p = []
        for t in range(0, span, tile):
            s = s0 if t == 0 else scores(q, kv, t)
            p.append(jnp.exp2(s * scale - m).astype(jnp.bfloat16))
        acc = jnp.dot(jnp.concatenate(p, axis=1), vx[kv], preferred_element_type=jnp.float32)
        ok.append(jnp.min(jnp.where(acc[:, 128:] < BIG, 1.0, 0.0)))
        results.append((m, acc))
    for b in range(nb):
        put(b, slice(b * 128, (b + 1) * 128), results)

    @pl.when(functools.reduce(jnp.minimum, ok) < 0.5)
    def _():
        def block(b, _):
            results = []
            for q, kv in zip(rows_of(b, 1), kvs):

                def top(n, m):
                    s = scores(q, kv, pl.multiple_of(n * tile, tile))
                    return jnp.maximum(m, jnp.max(s, axis=1, keepdims=True))

                m = point(lax.fori_loop(0, span // tile, top, jnp.full((128, 1), NEG, jnp.float32)))

                def add(n, acc):
                    t = pl.multiple_of(n * tile, tile)
                    p = jnp.exp2(scores(q, kv, t) * scale - m).astype(jnp.bfloat16)
                    return acc + jnp.dot(p, vx[kv, pl.ds(t, tile), :], preferred_element_type=jnp.float32)

                results.append((m, lax.fori_loop(0, span // tile, add, jnp.zeros((128, 256), jnp.float32))))
            put(b, slice(0, 128), results)
            return 0

        lax.fori_loop(0, nb, block, 0)


def attend(q, kx, vx, kvs, first=0, blocks=8):
    span = vx.shape[1]
    nb, tile = 8 // len(kvs), 256
    skip = first // nb
    vmem = pl.BlockSpec(memory_space=pltpu.VMEM)
    return pl.pallas_call(
        functools.partial(
            attend_kernel, kvs=kvs, first=first, nb=nb, tile=tile, scale=math.log2(math.e) / math.sqrt(128)
        ),
        grid=(blocks // nb,),
        in_specs=[pl.BlockSpec((nb, *q.shape[1:]), lambda i: (skip + i, 0, 0, 0)), vmem, vmem],
        out_specs=pl.BlockSpec((nb, len(kvs) * 136, 128), lambda i: (i, 0, 0)),
        out_shape=jax.ShapeDtypeStruct((blocks, len(kvs) * 136, 128), jnp.bfloat16),
        compiler_params=pltpu.CompilerParams(vmem_limit_bytes=20 * MIB, dimension_semantics=("arbitrary",)),
        cost_estimate=pl.CostEstimate(
            flops=8 * blocks * len(kvs) * 128 * span * 128,
            bytes_accessed=4 * MIB,
            transcendentals=blocks * len(kvs) * 128 * span,
        ),
        name="attend_plane",
    )(q, kx, vx)


def merged(parts, kv, nkv, eye):
    stats = [p[nkv * 128 :, :].astype(jnp.float32)[kv * 8 : kv * 8 + 8] for p in parts]
    m = functools.reduce(jnp.maximum, [s[0:1] for s in stats])
    total = jnp.zeros((1, 128), jnp.float32)
    out = jnp.zeros((128, 128), jnp.float32)
    for p, s in zip(parts, stats):
        factor = jnp.exp2(s[0:1] - m)
        total = total + factor * (s[1:2] + s[2:3])
        out = out + spread(factor, eye) * p[kv * 128 : (kv + 1) * 128, :].astype(jnp.float32)
    return out, m, total


def combine_kernel(*refs, starts):
    parts, o_ref = refs[:-1], refs[-1]
    nkv = o_ref.shape[1] // 136
    eye = diagonal()
    for b in range(o_ref.shape[0]):
        here = [part.at[at + b] for part, at in zip(parts, starts)]
        stats = []
        for kv in range(nkv):
            out, m, total = merged(here, kv, nkv, eye)
            o_ref[b, kv * 128 : (kv + 1) * 128, :] = out.astype(jnp.bfloat16)
            stats.append(stat_rows(m, total))
        o_ref[b, nkv * 128 :, :] = jnp.concatenate(stats, axis=0).astype(jnp.bfloat16)


def combine(blocks, *parts):
    vmem = pl.BlockSpec(memory_space=pltpu.VMEM)
    arrays, starts = zip(*parts)
    return pl.pallas_call(
        functools.partial(combine_kernel, starts=starts),
        in_specs=[vmem] * len(arrays),
        out_specs=vmem,
        out_shape=jax.ShapeDtypeStruct((blocks, *arrays[0].shape[1:]), jnp.bfloat16),
        compiler_params=pltpu.CompilerParams(vmem_limit_bytes=8 * MIB),
        name="combine",
    )(*arrays)


def finish_kernel(mine, theirs, o_ref, rows):
    eye = diagonal()
    nkv = mine.shape[1] // 136
    for kv in range(nkv):
        for dy in range(2):
            out, _, total = merged([mine.at[dy], theirs.at[1 - dy]], kv, nkv, eye)
            rows[kv, dy] = out * spread(1.0 / total, eye)
    for kv, h in itertools.product(range(nkv), range(16)):
        c = (kv * 16 + h) * 128
        both = [rows[kv, dy, pl.ds(h, 8, stride=16), :] for dy in range(2)]
        o_ref[:, c : c + 128] = jnp.concatenate(both, axis=0).astype(jnp.bfloat16)


def finish(mine, theirs):
    vmem = pl.BlockSpec(memory_space=pltpu.VMEM)
    nkv = mine.shape[1] // 136
    return pl.pallas_call(
        finish_kernel,
        in_specs=[vmem, vmem],
        out_specs=vmem,
        scratch_shapes=[pltpu.VMEM((nkv, 2, 128, 128), jnp.float32)],
        compiler_params=pltpu.CompilerParams(vmem_limit_bytes=4 * MIB),
        out_shape=jax.ShapeDtypeStruct((16, nkv * 2048), jnp.bfloat16),
        name="finish",
    )(mine, theirs)


def assemble_kernel(x0, x1, x2, x3, _, o_ref):
    for i, x in enumerate((x0, x1, x2, x3)):
        o_ref[i * x.shape[0] : (i + 1) * x.shape[0], :] = x[...]


def assemble(*pieces):
    vmem = pl.BlockSpec(memory_space=pltpu.VMEM)
    rows, width = pieces[0].shape
    return pl.pallas_call(
        assemble_kernel,
        in_specs=[vmem] * 4 + [pl.BlockSpec(memory_space=pl.ANY)],
        out_specs=vmem,
        out_shape=jax.ShapeDtypeStruct((RING * rows, width), pieces[0].dtype),
        compiler_params=pltpu.CompilerParams(vmem_limit_bytes=4 * MIB),
        name="assemble",
    )(*pieces)


def project_kernel(x_ref, w_ref, o_ref):
    o_ref[...] = jnp.dot(x_ref[...], w_ref[...], preferred_element_type=jnp.float32)


def project(x, w):
    vmem = pl.BlockSpec(memory_space=pltpu.VMEM)
    return pl.pallas_call(
        project_kernel,
        in_specs=[vmem, vmem],
        out_specs=vmem,
        out_shape=jax.ShapeDtypeStruct((x.shape[0], w.shape[1]), jnp.float32),
        compiler_params=pltpu.CompilerParams(vmem_limit_bytes=8 * MIB),
        cost_estimate=pl.CostEstimate(
            flops=8 * x.shape[0] * w.shape[0] * w.shape[1], bytes_accessed=4 * MIB, transcendentals=0
        ),
        name="project",
    )(x, w)


def place_kernel(info, y0, y1, y3, x_ref, w_ref, o_ref):
    me = tuple(info[i] for i in range(5))
    yl, core = me[3], me[4]
    y2 = jnp.dot(x_ref[...], w_ref[...], preferred_element_type=jnp.float32)
    for db, y in ((0, y0), (1, y1), (2, y2), (3, y3)):
        for da, dy in itertools.product(range(RING), range(2)):
            z, yh, xx = source(me, da, db, dy)
            row = (((z & 1) ^ core) * 2 + ((z >> 1) ^ yl)) * 64 + yh * 32 + xx * 8
            at = da * 16 + dy * 8
            o_ref[pl.ds(pl.multiple_of(row, 8), 8), :] = y[at : at + 8, :]


def place(info, y0, y1, y3, x, w):
    vmem = pl.BlockSpec(memory_space=pltpu.VMEM)
    return pl.pallas_call(
        place_kernel,
        in_specs=[pl.BlockSpec(memory_space=pltpu.SMEM)] + [vmem] * 5,
        out_specs=vmem,
        out_shape=jax.ShapeDtypeStruct((RING * y0.shape[0], w.shape[1]), jnp.float32),
        compiler_params=pltpu.CompilerParams(vmem_limit_bytes=8 * MIB),
        name="place",
    )(info, y0, y1, y3, x, w)


def on_device(queries, keys, values, lengths, start, out_weight):
    nkv = keys.shape[1]
    me = coords(lax.axis_index("cp"), lax.axis_index("tp"))
    info = jnp.concatenate([jnp.stack(me).astype(jnp.int32), lengths, start])
    k = keys.transpose(1, 0, 2)
    v = values.transpose(1, 0, 2)
    q = queries[None]
    q = jnp.concatenate([q, moved(q, yh=1)], axis=0)
    q, k, v, info = together(q, k, v, info)
    vx, kx0, kx1, kx2, kx3 = prepare(info, k, v)
    q2, q1, q3 = (moved(q, a=d) for d in (2, 1, 3))
    q = jnp.concatenate([q, q1, q2, q3], axis=0)
    q, vx, kx0, kx1, kx2, kx3 = together(q, vx, kx0, kx1, kx2, kx3)

    q2, q1, q3 = (moved(q, b=d) for d in (2, 1, 3))
    kvs = tuple(range(nkv))
    own0 = attend(q, kx0, vx, kvs, 0, 4)
    q2, own0 = together(q2, own0)
    p2 = attend(q2, kx2, vx, kvs)
    r2 = moved(p2, b=-2)
    q1, q3, p2 = together(q1, q3, p2)
    p1 = attend(q1, kx1, vx, kvs)
    r1 = moved(p1, b=-1)
    q3, p1 = together(q3, p1)
    p3a = attend(q3, kx3, vx, kvs, 0, 4)
    r3a = moved(p3a, b=-3)
    q3, p3a, r2 = together(q3, p3a, r2)
    p3b = attend(q3, kx3, vx, kvs, 4, 4)
    r3b = moved(p3b, b=-3)
    q, p3b, r1, r3a = together(q, p3b, r1, r3a)
    low = combine(4, (own0, 0), (r1, 0), (r2, 0), (r3a, 0))
    q, low = together(q, low)
    own1 = attend(q, kx0, vx, kvs, 4, 4)
    s1 = moved(low[2:], a=-1)
    high = combine(4, (own1, 0), (r1, 4), (r2, 4), (r3b, 0))
    s2, s3 = moved(high[:2], a=-2), moved(high[2:], a=-3)
    c = combine(2, (low, 0), (s1, 0), (s2, 0), (s3, 0))
    attn = finish(c, moved(c, yh=1))
    x2, x1, x3 = (moved(attn, a=d) for d in (2, 1, 3))
    attn = assemble(attn, x1, x2, x3, moved(x2, core=1))
    x1, x3, x2 = (moved(attn, b=d) for d in (1, 3, 2))
    y = place(info, project(attn, out_weight), project(x1, out_weight), project(x3, out_weight), x2, out_weight)
    y = y[:128] + moved(y[128:], core=1)
    y = y[:64] + moved(y[64:].astype(jnp.bfloat16), yl=1).astype(jnp.float32)
    return y.astype(jnp.bfloat16)


def solution(mesh):
    in_specs = (
        P("cp", "tp", None),
        P("cp", "tp", None),
        P("cp", "tp", None),
        P("cp"),
        P(),
        P("tp", "cp"),
    )
    return jax.shard_map(on_device, mesh=mesh, in_specs=in_specs, out_specs=P("tp", "cp"), check_vma=False)
```

```python
import functools
import itertools
import math

import jax
import jax.numpy as jnp
from jax import lax
from jax.experimental import pallas as pl
from jax.experimental.pallas import tpu as pltpu
from jax.sharding import PartitionSpec as P

NEG = -1e30
BIG = 2.0**100
RING = 4
MIB = 2**20


def coords(cp, tp):
    z, yh, x = cp // 8, (cp // 4) % 2, cp % 4
    yl, core = tp // 2, tp % 2
    return z, yh, x, yl, core


def moved(x, a=0, b=0, yh=0, yl=0, core=0):
    pairs = []
    for cp, tp in itertools.product(range(32), range(4)):
        zi, yhi, xi, yli, ci = coords(cp, tp)
        dz, dx = (a, b) if ci == 0 else (b, a)
        zo, xo = (zi + dz) % RING, (xi + dx) % RING
        yho, ylo, co = yhi ^ yh, yli ^ yl, ci ^ core
        pairs.append((cp * 4 + tp, ((zo * 2 + yho) * 4 + xo) * 4 + ylo * 2 + co))
    return lax.ppermute(x, ("cp", "tp"), pairs)


def together(*arrays):
    return lax.optimization_barrier(arrays)


def source(me, da, db, dy):
    z, yh, x, _, core = me
    dz = jnp.where(core == 0, da, db)
    dx = jnp.where(core == 0, db, da)
    return (z - dz) & (RING - 1), yh ^ dy, (x - dx) & (RING - 1)


def spread(row, eye):
    return jnp.sum(jnp.where(eye, row, 0.0), axis=1, keepdims=True)


def gathered_row(column, eye):
    return jnp.sum(jnp.where(eye, column, 0.0), axis=0, keepdims=True)


def diagonal():
    shape = (128, 128)
    return lax.broadcasted_iota(jnp.int32, shape, 0) == lax.broadcasted_iota(jnp.int32, shape, 1)


def stat_rows(m, l):
    high = l.astype(jnp.bfloat16).astype(jnp.float32)
    return jnp.concatenate([m, high, l - high, jnp.zeros((5, 128), jnp.float32)], axis=0)


def prepare_kernel(info, k_ref, v_ref, vx, *masked):
    nkv, span = k_ref.shape[:2]
    me = tuple(info[i] for i in range(5))
    length, start = info[5], info[6]
    shard = (me[0] * 2 + me[1]) * 4 + me[2]
    lane = lax.broadcasted_iota(jnp.int32, (1, 128), 1)
    slot = lax.broadcasted_iota(jnp.int32, (span, 128), 0)
    for db, kx in enumerate(masked):
        z, yh, x = source(me, lane >> 4, db, (lane >> 3) & 1)
        seen = start + z * 64 + yh * 32 + x * 8 + (lane & 7) + 1 - shard * span
        seen = jnp.minimum(seen, length)
        mask = jnp.where((slot >= seen) & (lane < 64), NEG, 0.0).astype(jnp.bfloat16)
        for kv in range(nkv):
            kx[kv, :, :128] = k_ref[kv]
            kx[kv, :, 128:] = mask
    for kv in range(nkv):
        vx[kv, :, :128] = v_ref[kv]
        vx[kv, :, 128:] = jnp.ones((span, 128), jnp.bfloat16)


def prepare(info, k, v):
    vmem = pl.BlockSpec(memory_space=pltpu.VMEM)
    count = 1 + RING
    return pl.pallas_call(
        prepare_kernel,
        in_specs=[pl.BlockSpec(memory_space=pltpu.SMEM), vmem, vmem],
        out_specs=[vmem] * count,
        out_shape=[jax.ShapeDtypeStruct((*k.shape[:2], 256), jnp.bfloat16)] * count,
        compiler_params=pltpu.CompilerParams(vmem_limit_bytes=4 * MIB),
        name="prepare",
    )(info, k, v)


def attend_kernel(q_ref, kx, vx, o_ref, *, kvs, first, nb, tile, scale):
    step = pl.program_id(0)
    span = vx.shape[1]
    eye = diagonal()

    def rows_of(b, count):
        row = lax.broadcasted_iota(jnp.int32, (count * 128, 128), 0)
        lane = lax.broadcasted_iota(jnp.int32, (count * 128, 128), 1)
        token = (first + step * nb + b + (row >> 7)) * 8 + ((row >> 4) & 7)
        hot = jnp.where(lane == token, 1.0, 0.0).astype(jnp.bfloat16)
        heads = [q_ref[pl.ds(b, count), :, kv * 16 : (kv + 1) * 16, :].reshape(count * 128, 128) for kv in kvs]
        return [jnp.concatenate([h, hot], axis=1) for h in heads]

    def scores(q, kv, t):
        return lax.dot_general(
            q, kx[kv, pl.ds(t, tile), :], (((1,), (1,)), ((), ())), preferred_element_type=jnp.float32
        )

    def point(m):
        return jnp.maximum(m * scale, 0.01 * NEG).astype(jnp.bfloat16).astype(jnp.float32)

    def put(b, r, results):
        stats = []
        for i, (m, acc) in enumerate(results):
            o_ref[b, i * 128 : (i + 1) * 128, :] = acc[r, :128].astype(jnp.bfloat16)
            stats.append(stat_rows(gathered_row(m[r], eye), gathered_row(acc[r, 128:], eye)))
        o_ref[b, len(results) * 128 :, :] = jnp.concatenate(stats, axis=0).astype(jnp.bfloat16)

    ok, results = [], []
    for q, kv in zip(rows_of(0, nb), kvs):
        s0 = scores(q, kv, 0)
        m = point(jnp.max(s0, axis=1, keepdims=True))
        p = []
        for t in range(0, span, tile):
            s = s0 if t == 0 else scores(q, kv, t)
            p.append(jnp.exp2(s * scale - m).astype(jnp.bfloat16))
        acc = jnp.dot(jnp.concatenate(p, axis=1), vx[kv], preferred_element_type=jnp.float32)
        ok.append(jnp.min(jnp.where(acc[:, 128:] < BIG, 1.0, 0.0)))
        results.append((m, acc))
    for b in range(nb):
        put(b, slice(b * 128, (b + 1) * 128), results)

    @pl.when(functools.reduce(jnp.minimum, ok) < 0.5)
    def _():
        def block(b, _):
            results = []
            for q, kv in zip(rows_of(b, 1), kvs):

                def top(n, m):
                    s = scores(q, kv, pl.multiple_of(n * tile, tile))
                    return jnp.maximum(m, jnp.max(s, axis=1, keepdims=True))

                m = point(lax.fori_loop(0, span // tile, top, jnp.full((128, 1), NEG, jnp.float32)))

                def add(n, acc):
                    t = pl.multiple_of(n * tile, tile)
                    p = jnp.exp2(scores(q, kv, t) * scale - m).astype(jnp.bfloat16)
                    return acc + jnp.dot(p, vx[kv, pl.ds(t, tile), :], preferred_element_type=jnp.float32)

                results.append((m, lax.fori_loop(0, span // tile, add, jnp.zeros((128, 256), jnp.float32))))
            put(b, slice(0, 128), results)
            return 0

        lax.fori_loop(0, nb, block, 0)


def attend(q, kx, vx, kvs, first=0, blocks=8):
    span = vx.shape[1]
    nb, tile = 8 // len(kvs), 256
    skip = first // nb
    vmem = pl.BlockSpec(memory_space=pltpu.VMEM)
    return pl.pallas_call(
        functools.partial(
            attend_kernel, kvs=kvs, first=first, nb=nb, tile=tile, scale=math.log2(math.e) / math.sqrt(128)
        ),
        grid=(blocks // nb,),
        in_specs=[pl.BlockSpec((nb, *q.shape[1:]), lambda i: (skip + i, 0, 0, 0)), vmem, vmem],
        out_specs=pl.BlockSpec((nb, len(kvs) * 136, 128), lambda i: (i, 0, 0)),
        out_shape=jax.ShapeDtypeStruct((blocks, len(kvs) * 136, 128), jnp.bfloat16),
        compiler_params=pltpu.CompilerParams(vmem_limit_bytes=20 * MIB, dimension_semantics=("arbitrary",)),
        cost_estimate=pl.CostEstimate(
            flops=8 * blocks * len(kvs) * 128 * span * 128,
            bytes_accessed=4 * MIB,
            transcendentals=blocks * len(kvs) * 128 * span,
        ),
        name="attend_plane",
    )(q, kx, vx)


def merged(parts, kv, nkv, eye):
    stats = [p[nkv * 128 :, :].astype(jnp.float32)[kv * 8 : kv * 8 + 8] for p in parts]
    m = functools.reduce(jnp.maximum, [s[0:1] for s in stats])
    total = jnp.zeros((1, 128), jnp.float32)
    out = jnp.zeros((128, 128), jnp.float32)
    for p, s in zip(parts, stats):
        factor = jnp.exp2(s[0:1] - m)
        total = total + factor * (s[1:2] + s[2:3])
        out = out + spread(factor, eye) * p[kv * 128 : (kv + 1) * 128, :].astype(jnp.float32)
    return out, m, total


def combine_kernel(*refs, starts):
    parts, o_ref = refs[:-1], refs[-1]
    nkv = o_ref.shape[1] // 136
    eye = diagonal()
    for b in range(o_ref.shape[0]):
        here = [part.at[at + b] for part, at in zip(parts, starts)]
        stats = []
        for kv in range(nkv):
            out, m, total = merged(here, kv, nkv, eye)
            o_ref[b, kv * 128 : (kv + 1) * 128, :] = out.astype(jnp.bfloat16)
            stats.append(stat_rows(m, total))
        o_ref[b, nkv * 128 :, :] = jnp.concatenate(stats, axis=0).astype(jnp.bfloat16)


def combine(blocks, *parts):
    vmem = pl.BlockSpec(memory_space=pltpu.VMEM)
    arrays, starts = zip(*parts)
    return pl.pallas_call(
        functools.partial(combine_kernel, starts=starts),
        in_specs=[vmem] * len(arrays),
        out_specs=vmem,
        out_shape=jax.ShapeDtypeStruct((blocks, *arrays[0].shape[1:]), jnp.bfloat16),
        compiler_params=pltpu.CompilerParams(vmem_limit_bytes=8 * MIB),
        name="combine",
    )(*arrays)


def finish_kernel(mine, theirs, o_ref, rows):
    eye = diagonal()
    nkv = mine.shape[1] // 136
    for kv in range(nkv):
        for dy in range(2):
            out, _, total = merged([mine.at[dy], theirs.at[1 - dy]], kv, nkv, eye)
            rows[kv, dy] = out * spread(1.0 / total, eye)
    for kv, h in itertools.product(range(nkv), range(16)):
        c = (kv * 16 + h) * 128
        both = [rows[kv, dy, pl.ds(h, 8, stride=16), :] for dy in range(2)]
        o_ref[:, c : c + 128] = jnp.concatenate(both, axis=0).astype(jnp.bfloat16)


def finish(mine, theirs):
    vmem = pl.BlockSpec(memory_space=pltpu.VMEM)
    nkv = mine.shape[1] // 136
    return pl.pallas_call(
        finish_kernel,
        in_specs=[vmem, vmem],
        out_specs=vmem,
        scratch_shapes=[pltpu.VMEM((nkv, 2, 128, 128), jnp.float32)],
        compiler_params=pltpu.CompilerParams(vmem_limit_bytes=4 * MIB),
        out_shape=jax.ShapeDtypeStruct((16, nkv * 2048), jnp.bfloat16),
        name="finish",
    )(mine, theirs)


def assemble_kernel(*refs, count):
    at = 0
    for x in refs[:count]:
        refs[-1][at : at + x.shape[0], :] = x[...]
        at += x.shape[0]


def assemble(pieces, *others):
    vmem = pl.BlockSpec(memory_space=pltpu.VMEM)
    rows, width = sum(p.shape[0] for p in pieces), pieces[0].shape[1]
    return pl.pallas_call(
        functools.partial(assemble_kernel, count=len(pieces)),
        in_specs=[vmem] * len(pieces) + [pl.BlockSpec(memory_space=pl.ANY)] * len(others),
        out_specs=vmem,
        out_shape=jax.ShapeDtypeStruct((rows, width), pieces[0].dtype),
        compiler_params=pltpu.CompilerParams(vmem_limit_bytes=4 * MIB),
        name="assemble",
    )(*pieces, *others)


def times_weight(halves, w_ref):
    x = jnp.concatenate([h[...] for h in halves], axis=0)
    return jnp.dot(x, w_ref[...], preferred_element_type=jnp.float32)


def project_kernel(xa, xb, w_ref, o_ref):
    o_ref[...] = times_weight((xa, xb), w_ref)


def project(xa, xb, w):
    vmem = pl.BlockSpec(memory_space=pltpu.VMEM)
    rows = xa.shape[0] + xb.shape[0]
    return pl.pallas_call(
        project_kernel,
        in_specs=[vmem] * 3,
        out_specs=vmem,
        out_shape=jax.ShapeDtypeStruct((rows, w.shape[1]), jnp.float32),
        compiler_params=pltpu.CompilerParams(vmem_limit_bytes=8 * MIB),
        cost_estimate=pl.CostEstimate(flops=2 * rows * w.shape[0] * w.shape[1], bytes_accessed=MIB, transcendentals=0),
        name="project",
    )(xa, xb, w)


def place_kernel(info, y0, y1, y3, xa, xb, w_ref, o_ref):
    me = tuple(info[i] for i in range(5))
    yl, core = me[3], me[4]
    y2 = times_weight((xa, xb), w_ref)
    for db, y in ((0, y0), (1, y1), (2, y2), (3, y3)):
        for da, dy in itertools.product(range(RING), range(2)):
            z, yh, xx = source(me, da, db, dy)
            row = (((z & 1) ^ core) * 2 + ((z >> 1) ^ yl)) * 64 + yh * 32 + xx * 8
            at = da * 16 + dy * 8
            o_ref[pl.ds(pl.multiple_of(row, 8), 8), :] = y[at : at + 8, :]


def place(info, y0, y1, y3, xa, xb, w):
    vmem = pl.BlockSpec(memory_space=pltpu.VMEM)
    return pl.pallas_call(
        place_kernel,
        in_specs=[pl.BlockSpec(memory_space=pltpu.SMEM)] + [vmem] * 6,
        out_specs=vmem,
        out_shape=jax.ShapeDtypeStruct((RING * y0.shape[0], w.shape[1]), jnp.float32),
        compiler_params=pltpu.CompilerParams(vmem_limit_bytes=8 * MIB),
        name="place",
    )(info, y0, y1, y3, xa, xb, w)


def on_device(queries, keys, values, lengths, start, out_weight):
    nkv = keys.shape[1]
    me = coords(lax.axis_index("cp"), lax.axis_index("tp"))
    info = jnp.concatenate([jnp.stack(me).astype(jnp.int32), lengths, start])
    k = keys.transpose(1, 0, 2)
    v = values.transpose(1, 0, 2)
    q = queries[None]
    q = jnp.concatenate([q, moved(q, yh=1)], axis=0)
    q, k, v, info = together(q, k, v, info)
    vx, kx0, kx1, kx2, kx3 = prepare(info, k, v)
    q2, q1, q3 = (moved(q, a=d) for d in (2, 1, 3))
    q = jnp.concatenate([q, q1, q2, q3], axis=0)
    q, vx, kx0, kx1, kx2, kx3 = together(q, vx, kx0, kx1, kx2, kx3)

    q2, q1, q3 = (moved(q, b=d) for d in (2, 1, 3))
    kvs = tuple(range(nkv))
    own0 = attend(q, kx0, vx, kvs, 0, 4)
    q2, own0 = together(q2, own0)
    p2 = attend(q2, kx2, vx, kvs)
    r2 = moved(p2, b=-2)
    q1, q3, p2 = together(q1, q3, p2)
    p1 = attend(q1, kx1, vx, kvs)
    r1 = moved(p1, b=-1)
    q3, p1 = together(q3, p1)
    p3a = attend(q3, kx3, vx, kvs, 0, 4)
    r3a = moved(p3a, b=-3)
    q3, p3a, r2 = together(q3, p3a, r2)
    p3b = attend(q3, kx3, vx, kvs, 4, 4)
    r3b = moved(p3b, b=-3)
    q, p3b, r1, r3a = together(q, p3b, r1, r3a)
    low = combine(4, (own0, 0), (r1, 0), (r2, 0), (r3a, 0))
    q, low = together(q, low)
    own1 = attend(q, kx0, vx, kvs, 4, 4)
    s1 = moved(low[2:], a=-1)
    high = combine(4, (own1, 0), (r1, 4), (r2, 4), (r3b, 0))
    s2, s3 = moved(high[:2], a=-2), moved(high[2:], a=-3)
    c = combine(2, (low, 0), (s1, 0), (s2, 0), (s3, 0))
    attn = finish(c, moved(c, yh=1))
    x2, x1, x3 = (moved(attn, a=d) for d in (2, 1, 3))
    low = assemble([attn, x1], moved(x2, core=1))
    high = assemble([x2, x3])
    x1a, x3b = moved(low, b=1), moved(high, b=3)
    x1b, x3a = moved(high, b=1), moved(low, b=3)
    x2a, x2b = moved(x1a, b=1), moved(x3b, b=3)
    ys = [project(xa, xb, out_weight) for xa, xb in ((low, high), (x1a, x1b), (x3a, x3b))]
    y = place(info, *ys, x2a, x2b, out_weight)
    y = y[:128] + moved(y[128:], core=1)
    y = y[:64] + moved(y[64:].astype(jnp.bfloat16), yl=1).astype(jnp.float32)
    return y.astype(jnp.bfloat16)


def solution(mesh):
    in_specs = (
        P("cp", "tp", None),
        P("cp", "tp", None),
        P("cp", "tp", None),
        P("cp"),
        P(),
        P("tp", "cp"),
    )
    return jax.shard_map(on_device, mesh=mesh, in_specs=in_specs, out_specs=P("tp", "cp"), check_vma=False)
```

```python
import functools
import itertools
import math

import jax
import jax.numpy as jnp
from jax import lax
from jax.experimental import pallas as pl
from jax.experimental.pallas import tpu as pltpu
from jax.sharding import PartitionSpec as P

NEG = -1e30
BIG = 2.0**100
RING = 4
MIB = 2**20


def coords(cp, tp):
    z, yh, x = cp // 8, (cp // 4) % 2, cp % 4
    yl, core = tp // 2, tp % 2
    return z, yh, x, yl, core


def moved(x, a=0, b=0, yh=0, yl=0, core=0):
    pairs = []
    for cp, tp in itertools.product(range(32), range(4)):
        zi, yhi, xi, yli, ci = coords(cp, tp)
        dz, dx = (a, b) if ci == 0 else (b, a)
        zo, xo = (zi + dz) % RING, (xi + dx) % RING
        yho, ylo, co = yhi ^ yh, yli ^ yl, ci ^ core
        pairs.append((cp * 4 + tp, ((zo * 2 + yho) * 4 + xo) * 4 + ylo * 2 + co))
    return lax.ppermute(x, ("cp", "tp"), pairs)


def together(*arrays):
    return lax.optimization_barrier(arrays)


def source(me, da, db, dy):
    z, yh, x, _, core = me
    dz = jnp.where(core == 0, da, db)
    dx = jnp.where(core == 0, db, da)
    return (z - dz) & (RING - 1), yh ^ dy, (x - dx) & (RING - 1)


def spread(row, eye):
    return jnp.sum(jnp.where(eye, row, 0.0), axis=1, keepdims=True)


def gathered_row(column, eye):
    return jnp.sum(jnp.where(eye, column, 0.0), axis=0, keepdims=True)


def diagonal():
    shape = (128, 128)
    return lax.broadcasted_iota(jnp.int32, shape, 0) == lax.broadcasted_iota(jnp.int32, shape, 1)


def stat_rows(m, l):
    high = l.astype(jnp.bfloat16).astype(jnp.float32)
    return jnp.concatenate([m, high, l - high, jnp.zeros((5, 128), jnp.float32)], axis=0)


def prepare_kernel(info, k_ref, v_ref, vx, *masked):
    nkv, span = k_ref.shape[:2]
    me = tuple(info[i] for i in range(5))
    length, start = info[5], info[6]
    shard = (me[0] * 2 + me[1]) * 4 + me[2]
    lane = lax.broadcasted_iota(jnp.int32, (1, 128), 1)
    slot = lax.broadcasted_iota(jnp.int32, (span, 128), 0)
    for db, kx in enumerate(masked):
        da = ((lane >> 5) & 1) | ((lane >> 3) & 2)
        z, yh, x = source(me, da, db, (lane >> 3) & 1)
        seen = start + z * 64 + yh * 32 + x * 8 + (lane & 7) + 1 - shard * span
        seen = jnp.minimum(seen, length)
        mask = jnp.where((slot >= seen) & (lane < 64), NEG, 0.0).astype(jnp.bfloat16)
        for kv in range(nkv):
            kx[kv, :, :128] = k_ref[kv]
            kx[kv, :, 128:] = mask
    for kv in range(nkv):
        vx[kv, :, :128] = v_ref[kv]
        vx[kv, :, 128:] = jnp.ones((span, 128), jnp.bfloat16)


def prepare(info, k, v):
    vmem = pl.BlockSpec(memory_space=pltpu.VMEM)
    count = 1 + RING
    return pl.pallas_call(
        prepare_kernel,
        in_specs=[pl.BlockSpec(memory_space=pltpu.SMEM), vmem, vmem],
        out_specs=[vmem] * count,
        out_shape=[jax.ShapeDtypeStruct((*k.shape[:2], 256), jnp.bfloat16)] * count,
        compiler_params=pltpu.CompilerParams(vmem_limit_bytes=4 * MIB),
        name="prepare",
    )(info, k, v)


def attend_kernel(q_ref, kx, vx, o_ref, *, kvs, first, nb, tile, scale):
    step = pl.program_id(0)
    span = vx.shape[1]
    eye = diagonal()

    def rows_of(b, count):
        row = lax.broadcasted_iota(jnp.int32, (count * 128, 128), 0)
        lane = lax.broadcasted_iota(jnp.int32, (count * 128, 128), 1)
        token = (first + step * nb + b + (row >> 7)) * 8 + ((row >> 4) & 7)
        hot = jnp.where(lane == token, 1.0, 0.0).astype(jnp.bfloat16)
        heads = [q_ref[pl.ds(b, count), :, kv * 16 : (kv + 1) * 16, :].reshape(count * 128, 128) for kv in kvs]
        return [jnp.concatenate([h, hot], axis=1) for h in heads]

    def scores(q, kv, t):
        return lax.dot_general(
            q, kx[kv, pl.ds(t, tile), :], (((1,), (1,)), ((), ())), preferred_element_type=jnp.float32
        )

    def point(m):
        return jnp.maximum(m * scale, 0.01 * NEG).astype(jnp.bfloat16).astype(jnp.float32)

    def put(b, r, results):
        stats = []
        for i, (m, acc) in enumerate(results):
            o_ref[b, i * 128 : (i + 1) * 128, :] = acc[r, :128].astype(jnp.bfloat16)
            stats.append(stat_rows(gathered_row(m[r], eye), gathered_row(acc[r, 128:], eye)))
        o_ref[b, len(results) * 128 :, :] = jnp.concatenate(stats, axis=0).astype(jnp.bfloat16)

    ok, results = [], []
    for q, kv in zip(rows_of(0, nb), kvs):
        s0 = scores(q, kv, 0)
        m = point(jnp.max(s0, axis=1, keepdims=True))
        p = []
        for t in range(0, span, tile):
            s = s0 if t == 0 else scores(q, kv, t)
            p.append(jnp.exp2(s * scale - m).astype(jnp.bfloat16))
        acc = jnp.dot(jnp.concatenate(p, axis=1), vx[kv], preferred_element_type=jnp.float32)
        ok.append(jnp.min(jnp.where(acc[:, 128:] < BIG, 1.0, 0.0)))
        results.append((m, acc))
    for b in range(nb):
        put(b, slice(b * 128, (b + 1) * 128), results)

    @pl.when(functools.reduce(jnp.minimum, ok) < 0.5)
    def _():
        def block(b, _):
            results = []
            for q, kv in zip(rows_of(b, 1), kvs):

                def top(n, m):
                    s = scores(q, kv, pl.multiple_of(n * tile, tile))
                    return jnp.maximum(m, jnp.max(s, axis=1, keepdims=True))

                m = point(lax.fori_loop(0, span // tile, top, jnp.full((128, 1), NEG, jnp.float32)))

                def add(n, acc):
                    t = pl.multiple_of(n * tile, tile)
                    p = jnp.exp2(scores(q, kv, t) * scale - m).astype(jnp.bfloat16)
                    return acc + jnp.dot(p, vx[kv, pl.ds(t, tile), :], preferred_element_type=jnp.float32)

                results.append((m, lax.fori_loop(0, span // tile, add, jnp.zeros((128, 256), jnp.float32))))
            put(b, slice(0, 128), results)
            return 0

        lax.fori_loop(0, nb, block, 0)


def attend(q, kx, vx, kvs, first=0, blocks=8):
    span = vx.shape[1]
    nb, tile = 8 // len(kvs), 256
    skip = first // nb
    vmem = pl.BlockSpec(memory_space=pltpu.VMEM)
    return pl.pallas_call(
        functools.partial(
            attend_kernel, kvs=kvs, first=first, nb=nb, tile=tile, scale=math.log2(math.e) / math.sqrt(128)
        ),
        grid=(blocks // nb,),
        in_specs=[pl.BlockSpec((nb, *q.shape[1:]), lambda i: (skip + i, 0, 0, 0)), vmem, vmem],
        out_specs=pl.BlockSpec((nb, len(kvs) * 136, 128), lambda i: (i, 0, 0)),
        out_shape=jax.ShapeDtypeStruct((blocks, len(kvs) * 136, 128), jnp.bfloat16),
        compiler_params=pltpu.CompilerParams(vmem_limit_bytes=20 * MIB, dimension_semantics=("arbitrary",)),
        cost_estimate=pl.CostEstimate(
            flops=8 * blocks * len(kvs) * 128 * span * 128,
            bytes_accessed=4 * MIB,
            transcendentals=blocks * len(kvs) * 128 * span,
        ),
        name="attend_plane",
    )(q, kx, vx)


def merged(parts, kv, nkv, eye):
    stats = [p[nkv * 128 :, :].astype(jnp.float32)[kv * 8 : kv * 8 + 8] for p in parts]
    m = functools.reduce(jnp.maximum, [s[0:1] for s in stats])
    total = jnp.zeros((1, 128), jnp.float32)
    out = jnp.zeros((128, 128), jnp.float32)
    for p, s in zip(parts, stats):
        factor = jnp.exp2(s[0:1] - m)
        total = total + factor * (s[1:2] + s[2:3])
        out = out + spread(factor, eye) * p[kv * 128 : (kv + 1) * 128, :].astype(jnp.float32)
    return out, m, total


def combine_kernel(*refs, starts):
    parts, o_ref = refs[:-1], refs[-1]
    nkv = o_ref.shape[1] // 136
    eye = diagonal()
    for b in range(o_ref.shape[0]):
        here = [part.at[at + b] for part, at in zip(parts, starts)]
        stats = []
        for kv in range(nkv):
            out, m, total = merged(here, kv, nkv, eye)
            o_ref[b, kv * 128 : (kv + 1) * 128, :] = out.astype(jnp.bfloat16)
            stats.append(stat_rows(m, total))
        o_ref[b, nkv * 128 :, :] = jnp.concatenate(stats, axis=0).astype(jnp.bfloat16)


def combine(blocks, *parts):
    vmem = pl.BlockSpec(memory_space=pltpu.VMEM)
    arrays, starts = zip(*parts)
    return pl.pallas_call(
        functools.partial(combine_kernel, starts=starts),
        in_specs=[vmem] * len(arrays),
        out_specs=vmem,
        out_shape=jax.ShapeDtypeStruct((blocks, *arrays[0].shape[1:]), jnp.bfloat16),
        compiler_params=pltpu.CompilerParams(vmem_limit_bytes=8 * MIB),
        name="combine",
    )(*arrays)


def finish_kernel(mine, theirs, o_ref, rows):
    eye = diagonal()
    nkv = mine.shape[1] // 136
    for kv in range(nkv):
        for dy in range(2):
            out, _, total = merged([mine.at[dy], theirs.at[1 - dy]], kv, nkv, eye)
            rows[kv, dy] = out * spread(1.0 / total, eye)
    for kv, h in itertools.product(range(nkv), range(16)):
        c = (kv * 16 + h) * 128
        both = [rows[kv, dy, pl.ds(h, 8, stride=16), :] for dy in range(2)]
        o_ref[:, c : c + 128] = jnp.concatenate(both, axis=0).astype(jnp.bfloat16)


def finish(mine, theirs):
    vmem = pl.BlockSpec(memory_space=pltpu.VMEM)
    nkv = mine.shape[1] // 136
    return pl.pallas_call(
        finish_kernel,
        in_specs=[vmem, vmem],
        out_specs=vmem,
        scratch_shapes=[pltpu.VMEM((nkv, 2, 128, 128), jnp.float32)],
        compiler_params=pltpu.CompilerParams(vmem_limit_bytes=4 * MIB),
        out_shape=jax.ShapeDtypeStruct((16, nkv * 2048), jnp.bfloat16),
        name="finish",
    )(mine, theirs)


def assemble_kernel(*refs, count):
    at = 0
    for x in refs[:count]:
        refs[-1][at : at + x.shape[0], :] = x[...]
        at += x.shape[0]


def assemble(pieces, *others):
    vmem = pl.BlockSpec(memory_space=pltpu.VMEM)
    rows, width = sum(p.shape[0] for p in pieces), pieces[0].shape[1]
    return pl.pallas_call(
        functools.partial(assemble_kernel, count=len(pieces)),
        in_specs=[vmem] * len(pieces) + [pl.BlockSpec(memory_space=pl.ANY)] * len(others),
        out_specs=vmem,
        out_shape=jax.ShapeDtypeStruct((rows, width), pieces[0].dtype),
        compiler_params=pltpu.CompilerParams(vmem_limit_bytes=4 * MIB),
        name="assemble",
    )(*pieces, *others)


def times_weight(halves, w_ref):
    x = jnp.concatenate([h[...] for h in halves], axis=0)
    return jnp.dot(x, w_ref[...], preferred_element_type=jnp.float32)


def project_kernel(xa, xb, w_ref, o_ref):
    o_ref[...] = times_weight((xa, xb), w_ref)


def project(xa, xb, w):
    vmem = pl.BlockSpec(memory_space=pltpu.VMEM)
    rows = xa.shape[0] + xb.shape[0]
    return pl.pallas_call(
        project_kernel,
        in_specs=[vmem] * 3,
        out_specs=vmem,
        out_shape=jax.ShapeDtypeStruct((rows, w.shape[1]), jnp.float32),
        compiler_params=pltpu.CompilerParams(vmem_limit_bytes=8 * MIB),
        cost_estimate=pl.CostEstimate(flops=2 * rows * w.shape[0] * w.shape[1], bytes_accessed=MIB, transcendentals=0),
        name="project",
    )(xa, xb, w)


def place_kernel(info, y0, y1, y3, xa, xb, w_ref, o_ref):
    me = tuple(info[i] for i in range(5))
    yl, core = me[3], me[4]
    y2 = times_weight((xa, xb), w_ref)
    for db, y in ((0, y0), (1, y1), (2, y2), (3, y3)):
        for da, dy in itertools.product(range(RING), range(2)):
            z, yh, xx = source(me, da, db, dy)
            row = (((z & 1) ^ core) * 2 + ((z >> 1) ^ yl)) * 64 + yh * 32 + xx * 8
            at = da * 16 + dy * 8
            o_ref[pl.ds(pl.multiple_of(row, 8), 8), :] = y[at : at + 8, :]


def place(info, y0, y1, y3, xa, xb, w):
    vmem = pl.BlockSpec(memory_space=pltpu.VMEM)
    return pl.pallas_call(
        place_kernel,
        in_specs=[pl.BlockSpec(memory_space=pltpu.SMEM)] + [vmem] * 6,
        out_specs=vmem,
        out_shape=jax.ShapeDtypeStruct((RING * y0.shape[0], w.shape[1]), jnp.float32),
        compiler_params=pltpu.CompilerParams(vmem_limit_bytes=8 * MIB),
        name="place",
    )(info, y0, y1, y3, xa, xb, w)


def on_device(queries, keys, values, lengths, start, out_weight):
    nkv = keys.shape[1]
    me = coords(lax.axis_index("cp"), lax.axis_index("tp"))
    info = jnp.concatenate([jnp.stack(me).astype(jnp.int32), lengths, start])
    k = keys.transpose(1, 0, 2)
    v = values.transpose(1, 0, 2)
    q = queries[None]
    q = jnp.concatenate([q, moved(q, yh=1)], axis=0)
    q, k, v, info = together(q, k, v, info)
    vx, kx0, kx1, kx2, kx3 = prepare(info, k, v)
    q1, q3 = moved(q, a=1), moved(q, a=3)
    q = jnp.concatenate([q, moved(q1, a=1), q1, q3], axis=0)
    q, vx, kx0, kx1, kx2, kx3 = together(q, vx, kx0, kx1, kx2, kx3)

    q2, q1, q3 = (moved(q, b=d) for d in (2, 1, 3))
    kvs = tuple(range(nkv))
    own0 = attend(q, kx0, vx, kvs, 0, 4)
    q2, own0 = together(q2, own0)
    p2 = attend(q2, kx2, vx, kvs)
    r2 = moved(p2, b=-2)
    q1, q3, p2 = together(q1, q3, p2)
    p1 = attend(q1, kx1, vx, kvs)
    r1 = moved(p1, b=-1)
    q3, p1 = together(q3, p1)
    p3a = attend(q3, kx3, vx, kvs, 0, 4)
    r3a = moved(p3a, b=-3)
    q3, p3a, r2 = together(q3, p3a, r2)
    p3b = attend(q3, kx3, vx, kvs, 4, 4)
    r3b = moved(p3b, b=-3)
    q, p3b, r1, r3a = together(q, p3b, r1, r3a)
    low = combine(4, (own0, 0), (r1, 0), (r2, 0), (r3a, 0))
    q, low = together(q, low)
    own1 = attend(q, kx0, vx, kvs, 4, 4)
    s2 = moved(low[2:], a=-2)
    high = combine(4, (own1, 0), (r1, 4), (r2, 4), (r3b, 0))
    s1, s3 = moved(high[:2], a=-1), moved(high[2:], a=-3)
    c = combine(2, (low, 0), (s1, 0), (s2, 0), (s3, 0))
    attn = finish(c, moved(c, yh=1))
    x1, x3 = moved(attn, a=1), moved(attn, a=3)
    low = assemble([attn, x1], moved(x1, core=1))
    high = assemble([moved(x1, a=1), x3])
    x1a, x3b = moved(low, b=1), moved(high, b=3)
    x1b, x3a = moved(high, b=1), moved(low, b=3)
    x2a, x2b = moved(x1a, b=1), moved(x3b, b=3)
    ys = [project(xa, xb, out_weight) for xa, xb in ((low, high), (x1a, x1b), (x3a, x3b))]
    y = place(info, *ys, x2a, x2b, out_weight)
    y = y[:128] + moved(y[128:], core=1)
    y = y[:64] + moved(y[64:].astype(jnp.bfloat16), yl=1).astype(jnp.float32)
    return y.astype(jnp.bfloat16)


def solution(mesh):
    in_specs = (
        P("cp", "tp", None),
        P("cp", "tp", None),
        P("cp", "tp", None),
        P("cp"),
        P(),
        P("tp", "cp"),
    )
    return jax.shard_map(on_device, mesh=mesh, in_specs=in_specs, out_specs=P("tp", "cp"), check_vma=False)
```

```python
import functools
import itertools
import math

import jax
import jax.numpy as jnp
from jax import lax
from jax.experimental import pallas as pl
from jax.experimental.pallas import tpu as pltpu
from jax.sharding import PartitionSpec as P

NEG = -1e30
BIG = 2.0**100
RING = 4
MIB = 2**20


def coords(cp, tp):
    z, yh, x = cp // 8, (cp // 4) % 2, cp % 4
    yl, core = tp // 2, tp % 2
    return z, yh, x, yl, core


def moved(x, a=0, b=0, yh=0, yl=0, core=0):
    pairs = []
    for cp, tp in itertools.product(range(32), range(4)):
        zi, yhi, xi, yli, ci = coords(cp, tp)
        dz, dx = (a, b) if ci == 0 else (b, a)
        zo, xo = (zi + dz) % RING, (xi + dx) % RING
        yho, ylo, co = yhi ^ yh, yli ^ yl, ci ^ core
        pairs.append((cp * 4 + tp, ((zo * 2 + yho) * 4 + xo) * 4 + ylo * 2 + co))
    return lax.ppermute(x, ("cp", "tp"), pairs)


def together(*arrays):
    return lax.optimization_barrier(arrays)


def source(me, da, db, dy):
    z, yh, x, _, core = me
    dz = jnp.where(core == 0, da, db)
    dx = jnp.where(core == 0, db, da)
    return (z - dz) & (RING - 1), yh ^ dy, (x - dx) & (RING - 1)


def spread(row, eye):
    return jnp.sum(jnp.where(eye, row, 0.0), axis=1, keepdims=True)


def gathered_row(column, eye):
    return jnp.sum(jnp.where(eye, column, 0.0), axis=0, keepdims=True)


def diagonal():
    shape = (128, 128)
    return lax.broadcasted_iota(jnp.int32, shape, 0) == lax.broadcasted_iota(jnp.int32, shape, 1)


def stat_rows(m, l):
    high = l.astype(jnp.bfloat16).astype(jnp.float32)
    return jnp.concatenate([m, high, l - high, jnp.zeros((5, 128), jnp.float32)], axis=0)


def prepare_kernel(info, k_ref, v_ref, vx, *masked):
    nkv, span = k_ref.shape[:2]
    me = tuple(info[i] for i in range(5))
    length, start = info[5], info[6]
    shard = (me[0] * 2 + me[1]) * 4 + me[2]
    lane = lax.broadcasted_iota(jnp.int32, (1, 128), 1)
    slot = lax.broadcasted_iota(jnp.int32, (span, 128), 0)
    for db, kx in enumerate(masked):
        da = ((lane >> 5) & 1) | ((lane >> 3) & 2)
        z, yh, x = source(me, da, db, (lane >> 3) & 1)
        seen = start + z * 64 + yh * 32 + x * 8 + (lane & 7) + 1 - shard * span
        seen = jnp.minimum(seen, length)
        mask = jnp.where((slot >= seen) & (lane < 64), NEG, 0.0).astype(jnp.bfloat16)
        for kv in range(nkv):
            kx[kv, :, :128] = k_ref[kv]
            kx[kv, :, 128:] = mask
    for kv in range(nkv):
        vx[kv, :, :128] = v_ref[kv]
        vx[kv, :, 128:] = jnp.ones((span, 128), jnp.bfloat16)


def prepare(info, k, v):
    vmem = pl.BlockSpec(memory_space=pltpu.VMEM)
    count = 1 + RING
    return pl.pallas_call(
        prepare_kernel,
        in_specs=[pl.BlockSpec(memory_space=pltpu.SMEM), vmem, vmem],
        out_specs=[vmem] * count,
        out_shape=[jax.ShapeDtypeStruct((*k.shape[:2], 256), jnp.bfloat16)] * count,
        compiler_params=pltpu.CompilerParams(vmem_limit_bytes=4 * MIB),
        name="prepare",
    )(info, k, v)


def attend_kernel(q_ref, kx, vx, o_ref, *, kvs, first, nb, tile, scale):
    step = pl.program_id(0)
    span = vx.shape[1]
    eye = diagonal()

    def rows_of(b, count):
        row = lax.broadcasted_iota(jnp.int32, (count * 128, 128), 0)
        lane = lax.broadcasted_iota(jnp.int32, (count * 128, 128), 1)
        token = (first + step * nb + b + (row >> 7)) * 8 + ((row >> 4) & 7)
        hot = jnp.where(lane == token, 1.0, 0.0).astype(jnp.bfloat16)
        heads = [q_ref[pl.ds(b, count), :, kv * 16 : (kv + 1) * 16, :].reshape(count * 128, 128) for kv in kvs]
        return [jnp.concatenate([h, hot], axis=1) for h in heads]

    def scores(q, kv, t):
        return lax.dot_general(
            q, kx[kv, pl.ds(t, tile), :], (((1,), (1,)), ((), ())), preferred_element_type=jnp.float32
        )

    def point(m):
        return jnp.maximum(m * scale, 0.01 * NEG).astype(jnp.bfloat16).astype(jnp.float32)

    def put(b, r, results):
        stats = []
        for i, (m, acc) in enumerate(results):
            o_ref[b, i * 128 : (i + 1) * 128, :] = acc[r, :128].astype(jnp.bfloat16)
            stats.append(stat_rows(gathered_row(m[r], eye), gathered_row(acc[r, 128:], eye)))
        o_ref[b, len(results) * 128 :, :] = jnp.concatenate(stats, axis=0).astype(jnp.bfloat16)

    ok, results = [], []
    for q, kv in zip(rows_of(0, nb), kvs):
        s0 = scores(q, kv, 0)
        m = point(jnp.max(s0, axis=1, keepdims=True))
        p = []
        for t in range(0, span, tile):
            s = s0 if t == 0 else scores(q, kv, t)
            p.append(jnp.exp2(s * scale - m).astype(jnp.bfloat16))
        acc = jnp.dot(jnp.concatenate(p, axis=1), vx[kv], preferred_element_type=jnp.float32)
        ok.append(jnp.min(jnp.where(acc[:, 128:] < BIG, 1.0, 0.0)))
        results.append((m, acc))
    for b in range(nb):
        put(b, slice(b * 128, (b + 1) * 128), results)

    @pl.when(functools.reduce(jnp.minimum, ok) < 0.5)
    def _():
        def block(b, _):
            results = []
            for q, kv in zip(rows_of(b, 1), kvs):

                def top(n, m):
                    s = scores(q, kv, pl.multiple_of(n * tile, tile))
                    return jnp.maximum(m, jnp.max(s, axis=1, keepdims=True))

                m = point(lax.fori_loop(0, span // tile, top, jnp.full((128, 1), NEG, jnp.float32)))

                def add(n, acc):
                    t = pl.multiple_of(n * tile, tile)
                    p = jnp.exp2(scores(q, kv, t) * scale - m).astype(jnp.bfloat16)
                    return acc + jnp.dot(p, vx[kv, pl.ds(t, tile), :], preferred_element_type=jnp.float32)

                results.append((m, lax.fori_loop(0, span // tile, add, jnp.zeros((128, 256), jnp.float32))))
            put(b, slice(0, 128), results)
            return 0

        lax.fori_loop(0, nb, block, 0)


def attend(q, kx, vx, kvs, first=0, blocks=8):
    span = vx.shape[1]
    nb, tile = 8 // len(kvs), 256
    skip = first // nb
    vmem = pl.BlockSpec(memory_space=pltpu.VMEM)
    return pl.pallas_call(
        functools.partial(
            attend_kernel, kvs=kvs, first=first, nb=nb, tile=tile, scale=math.log2(math.e) / math.sqrt(128)
        ),
        grid=(blocks // nb,),
        in_specs=[pl.BlockSpec((nb, *q.shape[1:]), lambda i: (skip + i, 0, 0, 0)), vmem, vmem],
        out_specs=pl.BlockSpec((nb, len(kvs) * 136, 128), lambda i: (i, 0, 0)),
        out_shape=jax.ShapeDtypeStruct((blocks, len(kvs) * 136, 128), jnp.bfloat16),
        compiler_params=pltpu.CompilerParams(vmem_limit_bytes=20 * MIB, dimension_semantics=("arbitrary",)),
        cost_estimate=pl.CostEstimate(
            flops=8 * blocks * len(kvs) * 128 * span * 128,
            bytes_accessed=4 * MIB,
            transcendentals=blocks * len(kvs) * 128 * span,
        ),
        name="attend_plane",
    )(q, kx, vx)


def merged(parts, kv, nkv, eye):
    stats = [p[nkv * 128 :, :].astype(jnp.float32)[kv * 8 : kv * 8 + 8] for p in parts]
    m = functools.reduce(jnp.maximum, [s[0:1] for s in stats])
    total = jnp.zeros((1, 128), jnp.float32)
    out = jnp.zeros((128, 128), jnp.float32)
    for p, s in zip(parts, stats):
        factor = jnp.exp2(s[0:1] - m)
        total = total + factor * (s[1:2] + s[2:3])
        out = out + spread(factor, eye) * p[kv * 128 : (kv + 1) * 128, :].astype(jnp.float32)
    return out, m, total


def combine_kernel(*refs, starts):
    parts, o_ref = refs[:-1], refs[-1]
    nkv = o_ref.shape[1] // 136
    eye = diagonal()
    for b in range(o_ref.shape[0]):
        here = [part.at[at + b] for part, at in zip(parts, starts)]
        stats = []
        for kv in range(nkv):
            out, m, total = merged(here, kv, nkv, eye)
            o_ref[b, kv * 128 : (kv + 1) * 128, :] = out.astype(jnp.bfloat16)
            stats.append(stat_rows(m, total))
        o_ref[b, nkv * 128 :, :] = jnp.concatenate(stats, axis=0).astype(jnp.bfloat16)


def combine(blocks, *parts):
    vmem = pl.BlockSpec(memory_space=pltpu.VMEM)
    arrays, starts = zip(*parts)
    return pl.pallas_call(
        functools.partial(combine_kernel, starts=starts),
        in_specs=[vmem] * len(arrays),
        out_specs=vmem,
        out_shape=jax.ShapeDtypeStruct((blocks, *arrays[0].shape[1:]), jnp.bfloat16),
        compiler_params=pltpu.CompilerParams(vmem_limit_bytes=8 * MIB),
        name="combine",
    )(*arrays)


def finish_kernel(mine, theirs, o_ref, rows):
    eye = diagonal()
    nkv = mine.shape[1] // 136
    for kv in range(nkv):
        for dy in range(2):
            out, _, total = merged([mine.at[dy], theirs.at[1 - dy]], kv, nkv, eye)
            rows[kv, dy] = out * spread(1.0 / total, eye)
    for kv, h in itertools.product(range(nkv), range(16)):
        c = (kv * 16 + h) * 128
        both = [rows[kv, dy, pl.ds(h, 8, stride=16), :] for dy in range(2)]
        o_ref[:, c : c + 128] = jnp.concatenate(both, axis=0).astype(jnp.bfloat16)


def finish(mine, theirs):
    vmem = pl.BlockSpec(memory_space=pltpu.VMEM)
    nkv = mine.shape[1] // 136
    return pl.pallas_call(
        finish_kernel,
        in_specs=[vmem, vmem],
        out_specs=vmem,
        scratch_shapes=[pltpu.VMEM((nkv, 2, 128, 128), jnp.float32)],
        compiler_params=pltpu.CompilerParams(vmem_limit_bytes=4 * MIB),
        out_shape=jax.ShapeDtypeStruct((16, nkv * 2048), jnp.bfloat16),
        name="finish",
    )(mine, theirs)


def assemble_kernel(*refs, count):
    at = 0
    for x in refs[:count]:
        refs[-1][at : at + x.shape[0]] = x[...]
        at += x.shape[0]


def assemble(pieces, *others):
    vmem = pl.BlockSpec(memory_space=pltpu.VMEM)
    rows = sum(p.shape[0] for p in pieces)
    return pl.pallas_call(
        functools.partial(assemble_kernel, count=len(pieces)),
        in_specs=[vmem] * len(pieces) + [pl.BlockSpec(memory_space=pl.ANY)] * len(others),
        out_specs=vmem,
        out_shape=jax.ShapeDtypeStruct((rows, *pieces[0].shape[1:]), pieces[0].dtype),
        compiler_params=pltpu.CompilerParams(vmem_limit_bytes=4 * MIB),
        name="assemble",
    )(*pieces, *others)


def times_weight(halves, w_ref):
    x = jnp.concatenate([h[...] for h in halves], axis=0)
    return jnp.dot(x, w_ref[...], preferred_element_type=jnp.float32)


def project_kernel(xa, xb, w_ref, o_ref):
    o_ref[...] = times_weight((xa, xb), w_ref)


def project(xa, xb, w):
    vmem = pl.BlockSpec(memory_space=pltpu.VMEM)
    rows = xa.shape[0] + xb.shape[0]
    return pl.pallas_call(
        project_kernel,
        in_specs=[vmem] * 3,
        out_specs=vmem,
        out_shape=jax.ShapeDtypeStruct((rows, w.shape[1]), jnp.float32),
        compiler_params=pltpu.CompilerParams(vmem_limit_bytes=8 * MIB),
        cost_estimate=pl.CostEstimate(flops=2 * rows * w.shape[0] * w.shape[1], bytes_accessed=MIB, transcendentals=0),
        name="project",
    )(xa, xb, w)


def place_kernel(info, y0, y1, y3, xa, xb, w_ref, o_ref):
    me = tuple(info[i] for i in range(5))
    yl, core = me[3], me[4]
    y2 = times_weight((xa, xb), w_ref)
    for db, y in ((0, y0), (1, y1), (2, y2), (3, y3)):
        for da, dy in itertools.product(range(RING), range(2)):
            z, yh, xx = source(me, da, db, dy)
            row = (((z & 1) ^ core) * 2 + ((z >> 1) ^ yl)) * 64 + yh * 32 + xx * 8
            at = da * 16 + dy * 8
            o_ref[pl.ds(pl.multiple_of(row, 8), 8), :] = y[at : at + 8, :]


def place(info, y0, y1, y3, xa, xb, w):
    vmem = pl.BlockSpec(memory_space=pltpu.VMEM)
    return pl.pallas_call(
        place_kernel,
        in_specs=[pl.BlockSpec(memory_space=pltpu.SMEM)] + [vmem] * 6,
        out_specs=vmem,
        out_shape=jax.ShapeDtypeStruct((RING * y0.shape[0], w.shape[1]), jnp.float32),
        compiler_params=pltpu.CompilerParams(vmem_limit_bytes=8 * MIB),
        name="place",
    )(info, y0, y1, y3, xa, xb, w)


def on_device(queries, keys, values, lengths, start, out_weight):
    nkv = keys.shape[1]
    me = coords(lax.axis_index("cp"), lax.axis_index("tp"))
    info = jnp.concatenate([jnp.stack(me).astype(jnp.int32), lengths, start])
    k = keys.transpose(1, 0, 2)
    v = values.transpose(1, 0, 2)
    q = queries[None]
    q = jnp.concatenate([q, moved(q, yh=1)], axis=0)
    q, k, v, info = together(q, k, v, info)
    vx, kx0, kx1, kx2, kx3 = prepare(info, k, v)
    q2, q1, q3 = (moved(q, a=d) for d in (2, 1, 3))
    q2, vx, kx0, kx1, kx2, kx3 = together(q2, vx, kx0, kx1, kx2, kx3)
    q = assemble([q, q2, q1, q3], moved(q2, core=1))

    q2, q1, q3 = (moved(q, b=d) for d in (2, 1, 3))
    kvs = tuple(range(nkv))
    own0 = attend(q, kx0, vx, kvs, 0, 4)
    q2, own0 = together(q2, own0)
    p2 = attend(q2, kx2, vx, kvs)
    r2 = moved(p2, b=-2)
    q1, q3, p2 = together(q1, q3, p2)
    p1 = attend(q1, kx1, vx, kvs)
    r1 = moved(p1, b=-1)
    q3, p1 = together(q3, p1)
    p3a = attend(q3, kx3, vx, kvs, 0, 4)
    r3a = moved(p3a, b=-3)
    q3, p3a, r2 = together(q3, p3a, r2)
    p3b = attend(q3, kx3, vx, kvs, 4, 4)
    r3b = moved(p3b, b=-3)
    q, p3b, r1, r3a = together(q, p3b, r1, r3a)
    low = combine(4, (own0, 0), (r1, 0), (r2, 0), (r3a, 0))
    q, low = together(q, low)
    own1 = attend(q, kx0, vx, kvs, 4, 4)
    s2 = moved(low[2:], a=-2)
    high = combine(4, (own1, 0), (r1, 4), (r2, 4), (r3b, 0))
    s1, s3 = moved(high[:2], a=-1), moved(high[2:], a=-3)
    c = combine(2, (low, 0), (s1, 0), (s2, 0), (s3, 0))
    attn = finish(c, moved(c, yh=1))
    x2, x1, x3 = (moved(attn, a=d) for d in (2, 1, 3))
    low = assemble([attn, x1], moved(x2, core=1))
    high = assemble([x2, x3])
    x1a, x3b = moved(low, b=1), moved(high, b=3)
    x1b, x3a = moved(high, b=1), moved(low, b=3)
    x2a, x2b = moved(x1a, b=1), moved(x3b, b=3)
    ys = [project(xa, xb, out_weight) for xa, xb in ((low, high), (x1a, x1b), (x3a, x3b))]
    y = place(info, *ys, x2a, x2b, out_weight)
    y = y[:128] + moved(y[128:], core=1)
    y = y[:64] + moved(y[64:].astype(jnp.bfloat16), yl=1).astype(jnp.float32)
    return y.astype(jnp.bfloat16)


def solution(mesh):
    in_specs = (
        P("cp", "tp", None),
        P("cp", "tp", None),
        P("cp", "tp", None),
        P("cp"),
        P(),
        P("tp", "cp"),
    )
    return jax.shard_map(on_device, mesh=mesh, in_specs=in_specs, out_specs=P("tp", "cp"), check_vma=False)
```

```python
import functools
import itertools
import math

import jax
import jax.numpy as jnp
from jax import lax
from jax.experimental import pallas as pl
from jax.experimental.pallas import tpu as pltpu
from jax.sharding import PartitionSpec as P

NEG = -1e30
BIG = 2.0**100
RING = 4
MIB = 2**20


def coords(cp, tp):
    z, yh, x = cp // 8, (cp // 4) % 2, cp % 4
    yl, core = tp // 2, tp % 2
    return z, yh, x, yl, core


def moved(x, a=0, b=0, yh=0, yl=0, core=0):
    pairs = []
    for cp, tp in itertools.product(range(32), range(4)):
        zi, yhi, xi, yli, ci = coords(cp, tp)
        dz, dx = (a, b) if ci == 0 else (b, a)
        zo, xo = (zi + dz) % RING, (xi + dx) % RING
        yho, ylo, co = yhi ^ yh, yli ^ yl, ci ^ core
        pairs.append((cp * 4 + tp, ((zo * 2 + yho) * 4 + xo) * 4 + ylo * 2 + co))
    return lax.ppermute(x, ("cp", "tp"), pairs)


def together(*arrays):
    return lax.optimization_barrier(arrays)


def source(me, da, db, dy):
    z, yh, x, _, core = me
    dz = jnp.where(core == 0, da, db)
    dx = jnp.where(core == 0, db, da)
    return (z - dz) & (RING - 1), yh ^ dy, (x - dx) & (RING - 1)


def spread(row, eye):
    return jnp.sum(jnp.where(eye, row, 0.0), axis=1, keepdims=True)


def gathered_row(column, eye):
    return jnp.sum(jnp.where(eye, column, 0.0), axis=0, keepdims=True)


def diagonal():
    shape = (128, 128)
    return lax.broadcasted_iota(jnp.int32, shape, 0) == lax.broadcasted_iota(jnp.int32, shape, 1)


def stat_rows(m, l):
    high = l.astype(jnp.bfloat16).astype(jnp.float32)
    return jnp.concatenate([m, high, l - high, jnp.zeros((5, 128), jnp.float32)], axis=0)


def prepare_kernel(info, k_ref, v_ref, vx, *masked):
    nkv, span = k_ref.shape[:2]
    me = tuple(info[i] for i in range(5))
    length, start = info[5], info[6]
    shard = (me[0] * 2 + me[1]) * 4 + me[2]
    lane = lax.broadcasted_iota(jnp.int32, (1, 128), 1)
    slot = lax.broadcasted_iota(jnp.int32, (span, 128), 0)
    for db, kx in enumerate(masked):
        da = ((lane >> 5) & 1) | ((lane >> 3) & 2)
        z, yh, x = source(me, da, db, (lane >> 3) & 1)
        seen = start + z * 64 + yh * 32 + x * 8 + (lane & 7) + 1 - shard * span
        seen = jnp.minimum(seen, length)
        mask = jnp.where((slot >= seen) & (lane < 64), NEG, 0.0).astype(jnp.bfloat16)
        for kv in range(nkv):
            kx[kv, :, :128] = k_ref[kv]
            kx[kv, :, 128:] = mask
    for kv in range(nkv):
        vx[kv, :, :128] = v_ref[kv]
        vx[kv, :, 128:] = jnp.ones((span, 128), jnp.bfloat16)


def prepare(info, k, v):
    vmem = pl.BlockSpec(memory_space=pltpu.VMEM)
    count = 1 + RING
    return pl.pallas_call(
        prepare_kernel,
        in_specs=[pl.BlockSpec(memory_space=pltpu.SMEM), vmem, vmem],
        out_specs=[vmem] * count,
        out_shape=[jax.ShapeDtypeStruct((*k.shape[:2], 256), jnp.bfloat16)] * count,
        compiler_params=pltpu.CompilerParams(vmem_limit_bytes=4 * MIB),
        name="prepare",
    )(info, k, v)


def attend_kernel(q_ref, kx, vx, o_ref, *, kvs, first, nb, tile, scale):
    step = pl.program_id(0)
    span = vx.shape[1]
    eye = diagonal()

    def rows_of(b, count):
        row = lax.broadcasted_iota(jnp.int32, (count * 128, 128), 0)
        lane = lax.broadcasted_iota(jnp.int32, (count * 128, 128), 1)
        token = (first + step * nb + b + (row >> 7)) * 8 + ((row >> 4) & 7)
        hot = jnp.where(lane == token, 1.0, 0.0).astype(jnp.bfloat16)
        heads = [q_ref[pl.ds(b, count), :, kv * 16 : (kv + 1) * 16, :].reshape(count * 128, 128) for kv in kvs]
        return [jnp.concatenate([h, hot], axis=1) for h in heads]

    def scores(q, kv, t):
        return lax.dot_general(
            q, kx[kv, pl.ds(t, tile), :], (((1,), (1,)), ((), ())), preferred_element_type=jnp.float32
        )

    def point(m):
        return jnp.maximum(m * scale, 0.01 * NEG).astype(jnp.bfloat16).astype(jnp.float32)

    def put(b, r, results):
        stats = []
        for i, (m, acc) in enumerate(results):
            o_ref[b, i * 128 : (i + 1) * 128, :] = acc[r, :128].astype(jnp.bfloat16)
            stats.append(stat_rows(gathered_row(m[r], eye), gathered_row(acc[r, 128:], eye)))
        o_ref[b, len(results) * 128 :, :] = jnp.concatenate(stats, axis=0).astype(jnp.bfloat16)

    ok, results = [], []
    for q, kv in zip(rows_of(0, nb), kvs):
        s0 = scores(q, kv, 0)
        m = point(jnp.max(s0, axis=1, keepdims=True))
        p = []
        for t in range(0, span, tile):
            s = s0 if t == 0 else scores(q, kv, t)
            p.append(jnp.exp2(s * scale - m).astype(jnp.bfloat16))
        acc = jnp.dot(jnp.concatenate(p, axis=1), vx[kv], preferred_element_type=jnp.float32)
        ok.append(jnp.min(jnp.where(acc[:, 128:] < BIG, 1.0, 0.0)))
        results.append((m, acc))
    for b in range(nb):
        put(b, slice(b * 128, (b + 1) * 128), results)

    @pl.when(functools.reduce(jnp.minimum, ok) < 0.5)
    def _():
        def block(b, _):
            results = []
            for q, kv in zip(rows_of(b, 1), kvs):

                def top(n, m):
                    s = scores(q, kv, pl.multiple_of(n * tile, tile))
                    return jnp.maximum(m, jnp.max(s, axis=1, keepdims=True))

                m = point(lax.fori_loop(0, span // tile, top, jnp.full((128, 1), NEG, jnp.float32)))

                def add(n, acc):
                    t = pl.multiple_of(n * tile, tile)
                    p = jnp.exp2(scores(q, kv, t) * scale - m).astype(jnp.bfloat16)
                    return acc + jnp.dot(p, vx[kv, pl.ds(t, tile), :], preferred_element_type=jnp.float32)

                results.append((m, lax.fori_loop(0, span // tile, add, jnp.zeros((128, 256), jnp.float32))))
            put(b, slice(0, 128), results)
            return 0

        lax.fori_loop(0, nb, block, 0)


def attend(q, kx, vx, kvs, first=0, blocks=8):
    span = vx.shape[1]
    nb, tile = blocks, 256
    skip = first // nb
    vmem = pl.BlockSpec(memory_space=pltpu.VMEM)
    return pl.pallas_call(
        functools.partial(
            attend_kernel, kvs=kvs, first=first, nb=nb, tile=tile, scale=math.log2(math.e) / math.sqrt(128)
        ),
        grid=(blocks // nb,),
        in_specs=[pl.BlockSpec((nb, *q.shape[1:]), lambda i: (skip + i, 0, 0, 0)), vmem, vmem],
        out_specs=pl.BlockSpec((nb, len(kvs) * 136, 128), lambda i: (i, 0, 0)),
        out_shape=jax.ShapeDtypeStruct((blocks, len(kvs) * 136, 128), jnp.bfloat16),
        compiler_params=pltpu.CompilerParams(vmem_limit_bytes=20 * MIB, dimension_semantics=("arbitrary",)),
        cost_estimate=pl.CostEstimate(
            flops=8 * blocks * len(kvs) * 128 * span * 128,
            bytes_accessed=4 * MIB,
            transcendentals=blocks * len(kvs) * 128 * span,
        ),
        name="attend_plane",
    )(q, kx, vx)


def merged(parts, kv, nkv, eye):
    stats = [p[nkv * 128 :, :].astype(jnp.float32)[kv * 8 : kv * 8 + 8] for p in parts]
    m = functools.reduce(jnp.maximum, [s[0:1] for s in stats])
    total = jnp.zeros((1, 128), jnp.float32)
    out = jnp.zeros((128, 128), jnp.float32)
    for p, s in zip(parts, stats):
        factor = jnp.exp2(s[0:1] - m)
        total = total + factor * (s[1:2] + s[2:3])
        out = out + spread(factor, eye) * p[kv * 128 : (kv + 1) * 128, :].astype(jnp.float32)
    return out, m, total


def combine_kernel(*refs, starts):
    parts, o_ref = refs[:-1], refs[-1]
    nkv = o_ref.shape[1] // 136
    eye = diagonal()
    for b in range(o_ref.shape[0]):
        here = [part.at[at + b] for part, at in zip(parts, starts)]
        stats = []
        for kv in range(nkv):
            out, m, total = merged(here, kv, nkv, eye)
            o_ref[b, kv * 128 : (kv + 1) * 128, :] = out.astype(jnp.bfloat16)
            stats.append(stat_rows(m, total))
        o_ref[b, nkv * 128 :, :] = jnp.concatenate(stats, axis=0).astype(jnp.bfloat16)


def combine(blocks, *parts):
    vmem = pl.BlockSpec(memory_space=pltpu.VMEM)
    arrays, starts = zip(*parts)
    return pl.pallas_call(
        functools.partial(combine_kernel, starts=starts),
        in_specs=[vmem] * len(arrays),
        out_specs=vmem,
        out_shape=jax.ShapeDtypeStruct((blocks, *arrays[0].shape[1:]), jnp.bfloat16),
        compiler_params=pltpu.CompilerParams(vmem_limit_bytes=8 * MIB),
        name="combine",
    )(*arrays)


def finish_kernel(mine, theirs, o_ref, rows):
    eye = diagonal()
    nkv = mine.shape[1] // 136
    for kv in range(nkv):
        for dy in range(2):
            out, _, total = merged([mine.at[dy], theirs.at[1 - dy]], kv, nkv, eye)
            rows[kv, dy] = out * spread(1.0 / total, eye)
    for kv, h in itertools.product(range(nkv), range(16)):
        c = (kv * 16 + h) * 128
        both = [rows[kv, dy, pl.ds(h, 8, stride=16), :] for dy in range(2)]
        o_ref[:, c : c + 128] = jnp.concatenate(both, axis=0).astype(jnp.bfloat16)


def finish(mine, theirs):
    vmem = pl.BlockSpec(memory_space=pltpu.VMEM)
    nkv = mine.shape[1] // 136
    return pl.pallas_call(
        finish_kernel,
        in_specs=[vmem, vmem],
        out_specs=vmem,
        scratch_shapes=[pltpu.VMEM((nkv, 2, 128, 128), jnp.float32)],
        compiler_params=pltpu.CompilerParams(vmem_limit_bytes=4 * MIB),
        out_shape=jax.ShapeDtypeStruct((16, nkv * 2048), jnp.bfloat16),
        name="finish",
    )(mine, theirs)


def assemble_kernel(*refs, count):
    at = 0
    for x in refs[:count]:
        refs[-1][at : at + x.shape[0]] = x[...]
        at += x.shape[0]


def assemble(pieces, *others):
    vmem = pl.BlockSpec(memory_space=pltpu.VMEM)
    rows = sum(p.shape[0] for p in pieces)
    return pl.pallas_call(
        functools.partial(assemble_kernel, count=len(pieces)),
        in_specs=[vmem] * len(pieces) + [pl.BlockSpec(memory_space=pl.ANY)] * len(others),
        out_specs=vmem,
        out_shape=jax.ShapeDtypeStruct((rows, *pieces[0].shape[1:]), pieces[0].dtype),
        compiler_params=pltpu.CompilerParams(vmem_limit_bytes=4 * MIB),
        name="assemble",
    )(*pieces, *others)


def times_weight(halves, w_ref):
    x = jnp.concatenate([h[...] for h in halves], axis=0)
    return jnp.dot(x, w_ref[...], preferred_element_type=jnp.float32)


def project_kernel(xa, xb, w_ref, o_ref):
    o_ref[...] = times_weight((xa, xb), w_ref)


def project(xa, xb, w):
    vmem = pl.BlockSpec(memory_space=pltpu.VMEM)
    rows = xa.shape[0] + xb.shape[0]
    return pl.pallas_call(
        project_kernel,
        in_specs=[vmem] * 3,
        out_specs=vmem,
        out_shape=jax.ShapeDtypeStruct((rows, w.shape[1]), jnp.float32),
        compiler_params=pltpu.CompilerParams(vmem_limit_bytes=8 * MIB),
        cost_estimate=pl.CostEstimate(flops=2 * rows * w.shape[0] * w.shape[1], bytes_accessed=MIB, transcendentals=0),
        name="project",
    )(xa, xb, w)


def place_kernel(info, y0, y1, y3, xa, xb, w_ref, o_ref):
    me = tuple(info[i] for i in range(5))
    yl, core = me[3], me[4]
    y2 = times_weight((xa, xb), w_ref)
    for db, y in ((0, y0), (1, y1), (2, y2), (3, y3)):
        for da, dy in itertools.product(range(RING), range(2)):
            z, yh, xx = source(me, da, db, dy)
            row = (((z & 1) ^ core) * 2 + ((z >> 1) ^ yl)) * 64 + yh * 32 + xx * 8
            at = da * 16 + dy * 8
            o_ref[pl.ds(pl.multiple_of(row, 8), 8), :] = y[at : at + 8, :]


def place(info, y0, y1, y3, xa, xb, w):
    vmem = pl.BlockSpec(memory_space=pltpu.VMEM)
    return pl.pallas_call(
        place_kernel,
        in_specs=[pl.BlockSpec(memory_space=pltpu.SMEM)] + [vmem] * 6,
        out_specs=vmem,
        out_shape=jax.ShapeDtypeStruct((RING * y0.shape[0], w.shape[1]), jnp.float32),
        compiler_params=pltpu.CompilerParams(vmem_limit_bytes=8 * MIB),
        name="place",
    )(info, y0, y1, y3, xa, xb, w)


def on_device(queries, keys, values, lengths, start, out_weight):
    nkv = keys.shape[1]
    me = coords(lax.axis_index("cp"), lax.axis_index("tp"))
    info = jnp.concatenate([jnp.stack(me).astype(jnp.int32), lengths, start])
    k = keys.transpose(1, 0, 2)
    v = values.transpose(1, 0, 2)
    q = queries[None]
    q = jnp.concatenate([q, moved(q, yh=1)], axis=0)
    q, k, v, info = together(q, k, v, info)
    vx, kx0, kx1, kx2, kx3 = prepare(info, k, v)
    q2, q1, q3 = (moved(q, a=d) for d in (2, 1, 3))
    q2, vx, kx0, kx1, kx2, kx3 = together(q2, vx, kx0, kx1, kx2, kx3)
    q = assemble([q, q2, q1, q3], moved(q2, core=1))

    q2, q1, q3 = (moved(q, b=d) for d in (2, 1, 3))
    kvs = tuple(range(nkv))
    own = attend(q, kx0, vx, kvs)
    q2, own = together(q2, own)
    p2 = attend(q2, kx2, vx, kvs)
    r2 = moved(p2, b=-2)
    q1, q3, p2 = together(q1, q3, p2)
    p1 = attend(q1, kx1, vx, kvs)
    r1 = moved(p1, b=-1)
    q3, p1 = together(q3, p1)
    p3a = attend(q3, kx3, vx, kvs, 0, 4)
    r3a = moved(p3a, b=-3)
    q3, p3a, r2 = together(q3, p3a, r2)
    p3b = attend(q3, kx3, vx, kvs, 4, 4)
    r3b = moved(p3b, b=-3)
    low = combine(4, (own, 0), (r1, 0), (r2, 0), (r3a, 0))
    s2 = moved(low[2:], a=-2)
    high = combine(4, (own, 4), (r1, 4), (r2, 4), (r3b, 0))
    s1, s3 = moved(high[:2], a=-1), moved(high[2:], a=-3)
    c = combine(2, (low, 0), (s1, 0), (s2, 0), (s3, 0))
    attn = finish(c, moved(c, yh=1))
    x2, x1, x3 = (moved(attn, a=d) for d in (2, 1, 3))
    low = assemble([attn, x1], moved(x2, core=1))
    high = assemble([x2, x3])
    x1a, x3b = moved(low, b=1), moved(high, b=3)
    x1b, x3a = moved(high, b=1), moved(low, b=3)
    x2a, x2b = moved(x1a, b=1), moved(x3b, b=3)
    ys = [project(xa, xb, out_weight) for xa, xb in ((low, high), (x1a, x1b), (x3a, x3b))]
    y = place(info, *ys, x2a, x2b, out_weight)
    y = y[:128] + moved(y[128:], core=1)
    y = y[:64] + moved(y[64:].astype(jnp.bfloat16), yl=1).astype(jnp.float32)
    return y.astype(jnp.bfloat16)


def solution(mesh):
    in_specs = (
        P("cp", "tp", None),
        P("cp", "tp", None),
        P("cp", "tp", None),
        P("cp"),
        P(),
        P("tp", "cp"),
    )
    return jax.shard_map(on_device, mesh=mesh, in_specs=in_specs, out_specs=P("tp", "cp"), check_vma=False)
```

```python
import functools
import itertools
import math

import jax
import jax.numpy as jnp
from jax import lax
from jax.experimental import pallas as pl
from jax.experimental.pallas import tpu as pltpu
from jax.sharding import PartitionSpec as P

NEG = -1e30
BIG = 2.0**100
RING = 4
MIB = 2**20


def coords(cp, tp):
    z, yh, x = cp // 8, (cp // 4) % 2, cp % 4
    yl, core = tp // 2, tp % 2
    return z, yh, x, yl, core


def moved(x, a=0, b=0, yh=0, yl=0, core=0):
    pairs = []
    for cp, tp in itertools.product(range(32), range(4)):
        zi, yhi, xi, yli, ci = coords(cp, tp)
        dz, dx = (a, b) if ci == 0 else (b, a)
        zo, xo = (zi + dz) % RING, (xi + dx) % RING
        yho, ylo, co = yhi ^ yh, yli ^ yl, ci ^ core
        pairs.append((cp * 4 + tp, ((zo * 2 + yho) * 4 + xo) * 4 + ylo * 2 + co))
    return lax.ppermute(x, ("cp", "tp"), pairs)


def together(*arrays):
    return lax.optimization_barrier(arrays)


def source(me, da, db, dy):
    z, yh, x, _, core = me
    dz = jnp.where(core == 0, da, db)
    dx = jnp.where(core == 0, db, da)
    return (z - dz) & (RING - 1), yh ^ dy, (x - dx) & (RING - 1)


def spread(row, eye):
    return jnp.sum(jnp.where(eye, row, 0.0), axis=1, keepdims=True)


def gathered_row(column, eye):
    return jnp.sum(jnp.where(eye, column, 0.0), axis=0, keepdims=True)


def diagonal():
    shape = (128, 128)
    return lax.broadcasted_iota(jnp.int32, shape, 0) == lax.broadcasted_iota(jnp.int32, shape, 1)


def stat_rows(m, l):
    high = l.astype(jnp.bfloat16).astype(jnp.float32)
    return jnp.concatenate([m, high, l - high, jnp.zeros((5, 128), jnp.float32)], axis=0)


def prepare_kernel(info, k_ref, v_ref, vx, *masked):
    nkv, span = k_ref.shape[:2]
    me = tuple(info[i] for i in range(5))
    length, start = info[5], info[6]
    shard = (me[0] * 2 + me[1]) * 4 + me[2]
    lane = lax.broadcasted_iota(jnp.int32, (1, 128), 1)
    da = ((lane >> 5) & 1) | ((lane >> 3) & 2)
    seen = []
    for db in range(RING):
        z, yh, x = source(me, da, db, (lane >> 3) & 1)
        count = start + z * 64 + yh * 32 + x * 8 + (lane & 7) + 1 - shard * span
        seen.append(jnp.where(lane < 64, jnp.minimum(count, length), span))
    chunk = 256

    def fill(i, _):
        at = pl.ds(pl.multiple_of(i * chunk, chunk), chunk)
        slot = i * chunk + lax.broadcasted_iota(jnp.int32, (chunk, 128), 0)
        for count, kx in zip(seen, masked):
            mask = jnp.where(slot >= count, NEG, 0.0).astype(jnp.bfloat16)
            for kv in range(nkv):
                kx[kv, at, :128] = k_ref[kv, at, :]
                kx[kv, at, 128:] = mask
        for kv in range(nkv):
            vx[kv, at, :128] = v_ref[kv, at, :]
            vx[kv, at, 128:] = jnp.ones((chunk, 128), jnp.bfloat16)
        return 0

    lax.fori_loop(0, span // chunk, fill, 0)


def prepare(info, k, v):
    vmem = pl.BlockSpec(memory_space=pltpu.VMEM)
    count = 1 + RING
    return pl.pallas_call(
        prepare_kernel,
        in_specs=[pl.BlockSpec(memory_space=pltpu.SMEM), vmem, vmem],
        out_specs=[vmem] * count,
        out_shape=[jax.ShapeDtypeStruct((*k.shape[:2], 256), jnp.bfloat16)] * count,
        compiler_params=pltpu.CompilerParams(vmem_limit_bytes=4 * MIB),
        name="prepare",
    )(info, k, v)


def attend_kernel(q_ref, kx, vx, o_ref, *, kvs, first, nb, tile, scale):
    step = pl.program_id(0)
    span = vx.shape[1]
    eye = diagonal()

    def rows_of(b, count):
        row = lax.broadcasted_iota(jnp.int32, (count * 128, 128), 0)
        lane = lax.broadcasted_iota(jnp.int32, (count * 128, 128), 1)
        token = (first + step * nb + b + (row >> 7)) * 8 + ((row >> 4) & 7)
        hot = jnp.where(lane == token, 1.0, 0.0).astype(jnp.bfloat16)
        heads = [q_ref[pl.ds(b, count), :, kv * 16 : (kv + 1) * 16, :].reshape(count * 128, 128) for kv in kvs]
        return [jnp.concatenate([h, hot], axis=1) for h in heads]

    def scores(q, kv, t):
        return lax.dot_general(
            q, kx[kv, pl.ds(t, tile), :], (((1,), (1,)), ((), ())), preferred_element_type=jnp.float32
        )

    def point(m):
        return jnp.maximum(m * scale, 0.01 * NEG).astype(jnp.bfloat16).astype(jnp.float32)

    def put(b, r, results):
        stats = []
        for i, (m, acc) in enumerate(results):
            o_ref[b, i * 128 : (i + 1) * 128, :] = acc[r, :128].astype(jnp.bfloat16)
            stats.append(stat_rows(gathered_row(m[r], eye), gathered_row(acc[r, 128:], eye)))
        o_ref[b, len(results) * 128 :, :] = jnp.concatenate(stats, axis=0).astype(jnp.bfloat16)

    ok, results = [], []
    for q, kv in zip(rows_of(0, nb), kvs):
        s0 = scores(q, kv, 0)
        m = point(jnp.max(s0, axis=1, keepdims=True))
        p = []
        for t in range(0, span, tile):
            s = s0 if t == 0 else scores(q, kv, t)
            p.append(jnp.exp2(s * scale - m).astype(jnp.bfloat16))
        acc = jnp.dot(jnp.concatenate(p, axis=1), vx[kv], preferred_element_type=jnp.float32)
        ok.append(jnp.min(jnp.where(acc[:, 128:] < BIG, 1.0, 0.0)))
        results.append((m, acc))
    for b in range(nb):
        put(b, slice(b * 128, (b + 1) * 128), results)

    @pl.when(functools.reduce(jnp.minimum, ok) < 0.5)
    def _():
        def block(b, _):
            results = []
            for q, kv in zip(rows_of(b, 1), kvs):

                def top(n, m):
                    s = scores(q, kv, pl.multiple_of(n * tile, tile))
                    return jnp.maximum(m, jnp.max(s, axis=1, keepdims=True))

                m = point(lax.fori_loop(0, span // tile, top, jnp.full((128, 1), NEG, jnp.float32)))

                def add(n, acc):
                    t = pl.multiple_of(n * tile, tile)
                    p = jnp.exp2(scores(q, kv, t) * scale - m).astype(jnp.bfloat16)
                    return acc + jnp.dot(p, vx[kv, pl.ds(t, tile), :], preferred_element_type=jnp.float32)

                results.append((m, lax.fori_loop(0, span // tile, add, jnp.zeros((128, 256), jnp.float32))))
            put(b, slice(0, 128), results)
            return 0

        lax.fori_loop(0, nb, block, 0)


def attend(q, kx, vx, kvs, first=0, blocks=8, nb=None):
    span = vx.shape[1]
    nb, tile = nb or blocks, 256
    skip = first // nb
    vmem = pl.BlockSpec(memory_space=pltpu.VMEM)
    return pl.pallas_call(
        functools.partial(
            attend_kernel, kvs=kvs, first=first, nb=nb, tile=tile, scale=math.log2(math.e) / math.sqrt(128)
        ),
        grid=(blocks // nb,),
        in_specs=[pl.BlockSpec((nb, *q.shape[1:]), lambda i: (skip + i, 0, 0, 0)), vmem, vmem],
        out_specs=pl.BlockSpec((nb, len(kvs) * 136, 128), lambda i: (i, 0, 0)),
        out_shape=jax.ShapeDtypeStruct((blocks, len(kvs) * 136, 128), jnp.bfloat16),
        compiler_params=pltpu.CompilerParams(vmem_limit_bytes=20 * MIB, dimension_semantics=("arbitrary",)),
        cost_estimate=pl.CostEstimate(
            flops=8 * blocks * len(kvs) * 128 * span * 128,
            bytes_accessed=4 * MIB,
            transcendentals=blocks * len(kvs) * 128 * span,
        ),
        name="attend_plane",
    )(q, kx, vx)


def merged(parts, kv, nkv, eye):
    stats = [p[nkv * 128 :, :].astype(jnp.float32)[kv * 8 : kv * 8 + 8] for p in parts]
    m = functools.reduce(jnp.maximum, [s[0:1] for s in stats])
    total = jnp.zeros((1, 128), jnp.float32)
    out = jnp.zeros((128, 128), jnp.float32)
    for p, s in zip(parts, stats):
        factor = jnp.exp2(s[0:1] - m)
        total = total + factor * (s[1:2] + s[2:3])
        out = out + spread(factor, eye) * p[kv * 128 : (kv + 1) * 128, :].astype(jnp.float32)
    return out, m, total


def combine_kernel(*refs, starts):
    parts, o_ref = refs[:-1], refs[-1]
    nkv = o_ref.shape[1] // 136
    eye = diagonal()
    for b in range(o_ref.shape[0]):
        here = [part.at[at + b] for part, at in zip(parts, starts)]
        stats = []
        for kv in range(nkv):
            out, m, total = merged(here, kv, nkv, eye)
            o_ref[b, kv * 128 : (kv + 1) * 128, :] = out.astype(jnp.bfloat16)
            stats.append(stat_rows(m, total))
        o_ref[b, nkv * 128 :, :] = jnp.concatenate(stats, axis=0).astype(jnp.bfloat16)


def combine(blocks, *parts):
    vmem = pl.BlockSpec(memory_space=pltpu.VMEM)
    arrays, starts = zip(*parts)
    return pl.pallas_call(
        functools.partial(combine_kernel, starts=starts),
        in_specs=[vmem] * len(arrays),
        out_specs=vmem,
        out_shape=jax.ShapeDtypeStruct((blocks, *arrays[0].shape[1:]), jnp.bfloat16),
        compiler_params=pltpu.CompilerParams(vmem_limit_bytes=8 * MIB),
        name="combine",
    )(*arrays)


def finish_kernel(mine, theirs, o_ref, rows):
    eye = diagonal()
    nkv = mine.shape[1] // 136
    for kv in range(nkv):
        for dy in range(2):
            out, _, total = merged([mine.at[dy], theirs.at[1 - dy]], kv, nkv, eye)
            rows[kv, dy] = out * spread(1.0 / total, eye)
    for kv, h in itertools.product(range(nkv), range(16)):
        c = (kv * 16 + h) * 128
        both = [rows[kv, dy, pl.ds(h, 8, stride=16), :] for dy in range(2)]
        o_ref[:, c : c + 128] = jnp.concatenate(both, axis=0).astype(jnp.bfloat16)


def finish(mine, theirs):
    vmem = pl.BlockSpec(memory_space=pltpu.VMEM)
    nkv = mine.shape[1] // 136
    return pl.pallas_call(
        finish_kernel,
        in_specs=[vmem, vmem],
        out_specs=vmem,
        scratch_shapes=[pltpu.VMEM((nkv, 2, 128, 128), jnp.float32)],
        compiler_params=pltpu.CompilerParams(vmem_limit_bytes=4 * MIB),
        out_shape=jax.ShapeDtypeStruct((16, nkv * 2048), jnp.bfloat16),
        name="finish",
    )(mine, theirs)


def assemble_kernel(*refs, count):
    at = 0
    for x in refs[:count]:
        refs[-1][at : at + x.shape[0]] = x[...]
        at += x.shape[0]


def assemble(pieces, *others):
    vmem = pl.BlockSpec(memory_space=pltpu.VMEM)
    rows = sum(p.shape[0] for p in pieces)
    return pl.pallas_call(
        functools.partial(assemble_kernel, count=len(pieces)),
        in_specs=[vmem] * len(pieces) + [pl.BlockSpec(memory_space=pl.ANY)] * len(others),
        out_specs=vmem,
        out_shape=jax.ShapeDtypeStruct((rows, *pieces[0].shape[1:]), pieces[0].dtype),
        compiler_params=pltpu.CompilerParams(vmem_limit_bytes=4 * MIB),
        name="assemble",
    )(*pieces, *others)


def times_weight(halves, w_ref):
    x = jnp.concatenate([h[...] for h in halves], axis=0)
    return jnp.dot(x, w_ref[...], preferred_element_type=jnp.float32)


def project_kernel(xa, xb, w_ref, o_ref):
    o_ref[...] = times_weight((xa, xb), w_ref)


def project(xa, xb, w):
    vmem = pl.BlockSpec(memory_space=pltpu.VMEM)
    rows = xa.shape[0] + xb.shape[0]
    return pl.pallas_call(
        project_kernel,
        in_specs=[vmem] * 3,
        out_specs=vmem,
        out_shape=jax.ShapeDtypeStruct((rows, w.shape[1]), jnp.float32),
        compiler_params=pltpu.CompilerParams(vmem_limit_bytes=8 * MIB),
        cost_estimate=pl.CostEstimate(flops=2 * rows * w.shape[0] * w.shape[1], bytes_accessed=MIB, transcendentals=0),
        name="project",
    )(xa, xb, w)


def place_kernel(info, y0, y1, y3, xa, xb, w_ref, o_ref):
    me = tuple(info[i] for i in range(5))
    yl, core = me[3], me[4]
    y2 = times_weight((xa, xb), w_ref)
    for db, y in ((0, y0), (1, y1), (2, y2), (3, y3)):
        for da, dy in itertools.product(range(RING), range(2)):
            z, yh, xx = source(me, da, db, dy)
            row = (((z & 1) ^ core) * 2 + ((z >> 1) ^ yl)) * 64 + yh * 32 + xx * 8
            at = da * 16 + dy * 8
            o_ref[pl.ds(pl.multiple_of(row, 8), 8), :] = y[at : at + 8, :]


def place(info, y0, y1, y3, xa, xb, w):
    vmem = pl.BlockSpec(memory_space=pltpu.VMEM)
    return pl.pallas_call(
        place_kernel,
        in_specs=[pl.BlockSpec(memory_space=pltpu.SMEM)] + [vmem] * 6,
        out_specs=vmem,
        out_shape=jax.ShapeDtypeStruct((RING * y0.shape[0], w.shape[1]), jnp.float32),
        compiler_params=pltpu.CompilerParams(vmem_limit_bytes=8 * MIB),
        name="place",
    )(info, y0, y1, y3, xa, xb, w)


def on_device(queries, keys, values, lengths, start, out_weight):
    nkv = keys.shape[1]
    me = coords(lax.axis_index("cp"), lax.axis_index("tp"))
    info = jnp.concatenate([jnp.stack(me).astype(jnp.int32), lengths, start])
    k = keys.transpose(1, 0, 2)
    v = values.transpose(1, 0, 2)
    q = queries[None]
    q = jnp.concatenate([q, moved(q, yh=1)], axis=0)
    q, k, v, info = together(q, k, v, info)
    vx, kx0, kx1, kx2, kx3 = prepare(info, k, v)
    q2, q1, q3 = (moved(q, a=d) for d in (2, 1, 3))
    q2, vx, kx0, kx1, kx2, kx3 = together(q2, vx, kx0, kx1, kx2, kx3)
    q = assemble([q, q2, q1, q3], moved(q2, core=1))

    q2, q1, q3 = (moved(q, b=d) for d in (2, 1, 3))
    kvs = tuple(range(nkv))
    own = attend(q, kx0, vx, kvs, nb=4)
    q2, own = together(q2, own)
    p2 = attend(q2, kx2, vx, kvs)
    r2 = moved(p2, b=-2)
    q1, q3, p2 = together(q1, q3, p2)
    p1 = attend(q1, kx1, vx, kvs)
    r1 = moved(p1, b=-1)
    q3, p1 = together(q3, p1)
    p3a = attend(q3, kx3, vx, kvs, 0, 4)
    r3a = moved(p3a, b=-3)
    q3, p3a, r2 = together(q3, p3a, r2)
    p3b = attend(q3, kx3, vx, kvs, 4, 4)
    r3b = moved(p3b, b=-3)
    low = combine(4, (own, 0), (r1, 0), (r2, 0), (r3a, 0))
    s2 = moved(low[2:], a=-2)
    high = combine(4, (own, 4), (r1, 4), (r2, 4), (r3b, 0))
    s1, s3 = moved(high[:2], a=-1), moved(high[2:], a=-3)
    c = combine(2, (low, 0), (s1, 0), (s2, 0), (s3, 0))
    attn = finish(c, moved(c, yh=1))
    x2, x1, x3 = (moved(attn, a=d) for d in (2, 1, 3))
    low = assemble([attn, x1], moved(x2, core=1))
    high = assemble([x2, x3])
    x1a, x3b = moved(low, b=1), moved(high, b=3)
    x1b, x3a = moved(high, b=1), moved(low, b=3)
    x2a, x2b = moved(x1a, b=1), moved(x3b, b=3)
    ys = [project(xa, xb, out_weight) for xa, xb in ((low, high), (x1a, x1b), (x3a, x3b))]
    y = place(info, *ys, x2a, x2b, out_weight)
    y = y[:128] + moved(y[128:], core=1)
    y = y[:64] + moved(y[64:].astype(jnp.bfloat16), yl=1).astype(jnp.float32)
    return y.astype(jnp.bfloat16)


def solution(mesh):
    in_specs = (
        P("cp", "tp", None),
        P("cp", "tp", None),
        P("cp", "tp", None),
        P("cp"),
        P(),
        P("tp", "cp"),
    )
    return jax.shard_map(on_device, mesh=mesh, in_specs=in_specs, out_specs=P("tp", "cp"), check_vma=False)
```

```python
import functools
import itertools
import math

import jax
import jax.numpy as jnp
from jax import lax
from jax.experimental import pallas as pl
from jax.experimental.pallas import tpu as pltpu
from jax.sharding import PartitionSpec as P

NEG = -1e30
BIG = 2.0**100
RING = 4
MIB = 2**20


def coords(cp, tp):
    z, yh, x = cp // 8, (cp // 4) % 2, cp % 4
    yl, core = tp // 2, tp % 2
    return z, yh, x, yl, core


def moved(x, a=0, b=0, yh=0, yl=0, core=0):
    pairs = []
    for cp, tp in itertools.product(range(32), range(4)):
        zi, yhi, xi, yli, ci = coords(cp, tp)
        dz, dx = (a, b) if ci == 0 else (b, a)
        zo, xo = (zi + dz) % RING, (xi + dx) % RING
        yho, ylo, co = yhi ^ yh, yli ^ yl, ci ^ core
        pairs.append((cp * 4 + tp, ((zo * 2 + yho) * 4 + xo) * 4 + ylo * 2 + co))
    return lax.ppermute(x, ("cp", "tp"), pairs)


def together(*arrays):
    return lax.optimization_barrier(arrays)


def source(me, da, db, dy):
    z, yh, x, _, core = me
    dz = jnp.where(core == 0, da, db)
    dx = jnp.where(core == 0, db, da)
    return (z - dz) & (RING - 1), yh ^ dy, (x - dx) & (RING - 1)


def spread(row, eye):
    return jnp.sum(jnp.where(eye, row, 0.0), axis=1, keepdims=True)


def gathered_row(column, eye):
    return jnp.sum(jnp.where(eye, column, 0.0), axis=0, keepdims=True)


def diagonal():
    shape = (128, 128)
    return lax.broadcasted_iota(jnp.int32, shape, 0) == lax.broadcasted_iota(jnp.int32, shape, 1)


def stat_rows(m, l):
    high = l.astype(jnp.bfloat16).astype(jnp.float32)
    return jnp.concatenate([m, high, l - high, jnp.zeros((5, 128), jnp.float32)], axis=0)


def prepare_kernel(info, k_ref, v_ref, vx, *masked):
    nkv, span = k_ref.shape[:2]
    me = tuple(info[i] for i in range(5))
    length, start = info[5], info[6]
    shard = (me[0] * 2 + me[1]) * 4 + me[2]
    lane = lax.broadcasted_iota(jnp.int32, (1, 128), 1)
    da = ((lane >> 5) & 1) | ((lane >> 3) & 2)
    seen = []
    for db in range(RING):
        z, yh, x = source(me, da, db, (lane >> 3) & 1)
        count = start + z * 64 + yh * 32 + x * 8 + (lane & 7) + 1 - shard * span
        seen.append(jnp.where(lane < 64, jnp.minimum(count, length), span))
    chunk = 256

    def fill(i, _):
        at = pl.ds(pl.multiple_of(i * chunk, chunk), chunk)
        slot = i * chunk + lax.broadcasted_iota(jnp.int32, (chunk, 128), 0)
        for count, kx in zip(seen, masked):
            mask = jnp.where(slot >= count, NEG, 0.0).astype(jnp.bfloat16)
            for kv in range(nkv):
                kx[kv, at, :128] = k_ref[kv, at, :]
                kx[kv, at, 128:] = mask
        for kv in range(nkv):
            vx[kv, at, :128] = v_ref[kv, at, :]
            vx[kv, at, 128:] = jnp.ones((chunk, 128), jnp.bfloat16)
        return 0

    lax.fori_loop(0, span // chunk, fill, 0)


def prepare(info, k, v):
    vmem = pl.BlockSpec(memory_space=pltpu.VMEM)
    count = 1 + RING
    return pl.pallas_call(
        prepare_kernel,
        in_specs=[pl.BlockSpec(memory_space=pltpu.SMEM), vmem, vmem],
        out_specs=[vmem] * count,
        out_shape=[jax.ShapeDtypeStruct((*k.shape[:2], 256), jnp.bfloat16)] * count,
        compiler_params=pltpu.CompilerParams(vmem_limit_bytes=4 * MIB),
        name="prepare",
    )(info, k, v)


def attend_kernel(q_ref, kx, vx, *o_refs, kvs, first, nb, tile, scale):
    step = pl.program_id(0)
    span = vx.shape[1]
    share = nb // len(o_refs)
    eye = diagonal()

    def rows_of(b, count):
        row = lax.broadcasted_iota(jnp.int32, (count * 128, 128), 0)
        lane = lax.broadcasted_iota(jnp.int32, (count * 128, 128), 1)
        token = (first + step * nb + b + (row >> 7)) * 8 + ((row >> 4) & 7)
        hot = jnp.where(lane == token, 1.0, 0.0).astype(jnp.bfloat16)
        heads = [q_ref[pl.ds(b, count), :, kv * 16 : (kv + 1) * 16, :].reshape(count * 128, 128) for kv in kvs]
        return [jnp.concatenate([h, hot], axis=1) for h in heads]

    def scores(q, kv, t):
        return lax.dot_general(
            q, kx[kv, pl.ds(t, tile), :], (((1,), (1,)), ((), ())), preferred_element_type=jnp.float32
        )

    def point(m):
        return jnp.maximum(m * scale, 0.01 * NEG).astype(jnp.bfloat16).astype(jnp.float32)

    def put(o_ref, b, r, results):
        stats = []
        for i, (m, acc) in enumerate(results):
            o_ref[b, i * 128 : (i + 1) * 128, :] = acc[r, :128].astype(jnp.bfloat16)
            stats.append(stat_rows(gathered_row(m[r], eye), gathered_row(acc[r, 128:], eye)))
        o_ref[b, len(results) * 128 :, :] = jnp.concatenate(stats, axis=0).astype(jnp.bfloat16)

    ok, results = [], []
    for q, kv in zip(rows_of(0, nb), kvs):
        s0 = scores(q, kv, 0)
        m = point(jnp.max(s0, axis=1, keepdims=True))
        p = []
        for t in range(0, span, tile):
            s = s0 if t == 0 else scores(q, kv, t)
            p.append(jnp.exp2(s * scale - m).astype(jnp.bfloat16))
        acc = jnp.dot(jnp.concatenate(p, axis=1), vx[kv], preferred_element_type=jnp.float32)
        ok.append(jnp.min(jnp.where(acc[:, 128:] < BIG, 1.0, 0.0)))
        results.append((m, acc))
    for b in range(nb):
        put(o_refs[b // share], b % share, slice(b * 128, (b + 1) * 128), results)

    @pl.when(functools.reduce(jnp.minimum, ok) < 0.5)
    def _():
        def block(o_ref, at, b, _):
            results = []
            for q, kv in zip(rows_of(at + b, 1), kvs):

                def top(n, m):
                    s = scores(q, kv, pl.multiple_of(n * tile, tile))
                    return jnp.maximum(m, jnp.max(s, axis=1, keepdims=True))

                m = point(lax.fori_loop(0, span // tile, top, jnp.full((128, 1), NEG, jnp.float32)))

                def add(n, acc):
                    t = pl.multiple_of(n * tile, tile)
                    p = jnp.exp2(scores(q, kv, t) * scale - m).astype(jnp.bfloat16)
                    return acc + jnp.dot(p, vx[kv, pl.ds(t, tile), :], preferred_element_type=jnp.float32)

                results.append((m, lax.fori_loop(0, span // tile, add, jnp.zeros((128, 256), jnp.float32))))
            put(o_ref, b, slice(0, 128), results)
            return 0

        for i, o_ref in enumerate(o_refs):
            lax.fori_loop(0, share, functools.partial(block, o_ref, i * share), 0)


def attend(q, kx, vx, kvs, first=0, blocks=8, nb=None, outs=1):
    span = vx.shape[1]
    nb, tile = nb or blocks, 256
    skip = first // nb
    vmem = pl.BlockSpec(memory_space=pltpu.VMEM)
    return pl.pallas_call(
        functools.partial(
            attend_kernel, kvs=kvs, first=first, nb=nb, tile=tile, scale=math.log2(math.e) / math.sqrt(128)
        ),
        grid=(blocks // nb,),
        in_specs=[pl.BlockSpec((nb, *q.shape[1:]), lambda i: (skip + i, 0, 0, 0)), vmem, vmem],
        out_specs=[pl.BlockSpec((nb // outs, len(kvs) * 136, 128), lambda i: (i, 0, 0))] * outs,
        out_shape=[jax.ShapeDtypeStruct((blocks // outs, len(kvs) * 136, 128), jnp.bfloat16)] * outs,
        compiler_params=pltpu.CompilerParams(vmem_limit_bytes=20 * MIB, dimension_semantics=("arbitrary",)),
        cost_estimate=pl.CostEstimate(
            flops=8 * blocks * len(kvs) * 128 * span * 128,
            bytes_accessed=4 * MIB,
            transcendentals=blocks * len(kvs) * 128 * span,
        ),
        name="attend_plane",
    )(q, kx, vx)


def merged(parts, kv, nkv, eye):
    stats = [p[nkv * 128 :, :].astype(jnp.float32)[kv * 8 : kv * 8 + 8] for p in parts]
    m = functools.reduce(jnp.maximum, [s[0:1] for s in stats])
    total = jnp.zeros((1, 128), jnp.float32)
    out = jnp.zeros((128, 128), jnp.float32)
    for p, s in zip(parts, stats):
        factor = jnp.exp2(s[0:1] - m)
        total = total + factor * (s[1:2] + s[2:3])
        out = out + spread(factor, eye) * p[kv * 128 : (kv + 1) * 128, :].astype(jnp.float32)
    return out, m, total


def combine_kernel(*refs, starts):
    parts, o_ref = refs[:-1], refs[-1]
    nkv = o_ref.shape[1] // 136
    eye = diagonal()
    for b in range(o_ref.shape[0]):
        here = [part.at[at + b] for part, at in zip(parts, starts)]
        stats = []
        for kv in range(nkv):
            out, m, total = merged(here, kv, nkv, eye)
            o_ref[b, kv * 128 : (kv + 1) * 128, :] = out.astype(jnp.bfloat16)
            stats.append(stat_rows(m, total))
        o_ref[b, nkv * 128 :, :] = jnp.concatenate(stats, axis=0).astype(jnp.bfloat16)


def combine(blocks, *parts):
    vmem = pl.BlockSpec(memory_space=pltpu.VMEM)
    arrays, starts = zip(*parts)
    return pl.pallas_call(
        functools.partial(combine_kernel, starts=starts),
        in_specs=[vmem] * len(arrays),
        out_specs=vmem,
        out_shape=jax.ShapeDtypeStruct((blocks, *arrays[0].shape[1:]), jnp.bfloat16),
        compiler_params=pltpu.CompilerParams(vmem_limit_bytes=8 * MIB),
        name="combine",
    )(*arrays)


def finish_kernel(mine, theirs, o_ref, rows):
    eye = diagonal()
    nkv = mine.shape[1] // 136
    for kv in range(nkv):
        for dy in range(2):
            out, _, total = merged([mine.at[dy], theirs.at[1 - dy]], kv, nkv, eye)
            rows[kv, dy] = out * spread(1.0 / total, eye)
    for kv, h in itertools.product(range(nkv), range(16)):
        c = (kv * 16 + h) * 128
        both = [rows[kv, dy, pl.ds(h, 8, stride=16), :] for dy in range(2)]
        o_ref[:, c : c + 128] = jnp.concatenate(both, axis=0).astype(jnp.bfloat16)


def finish(mine, theirs):
    vmem = pl.BlockSpec(memory_space=pltpu.VMEM)
    nkv = mine.shape[1] // 136
    return pl.pallas_call(
        finish_kernel,
        in_specs=[vmem, vmem],
        out_specs=vmem,
        scratch_shapes=[pltpu.VMEM((nkv, 2, 128, 128), jnp.float32)],
        compiler_params=pltpu.CompilerParams(vmem_limit_bytes=4 * MIB),
        out_shape=jax.ShapeDtypeStruct((16, nkv * 2048), jnp.bfloat16),
        name="finish",
    )(mine, theirs)


def assemble_kernel(*refs, count):
    at = 0
    for x in refs[:count]:
        refs[-1][at : at + x.shape[0]] = x[...]
        at += x.shape[0]


def assemble(pieces, *others):
    vmem = pl.BlockSpec(memory_space=pltpu.VMEM)
    rows = sum(p.shape[0] for p in pieces)
    return pl.pallas_call(
        functools.partial(assemble_kernel, count=len(pieces)),
        in_specs=[vmem] * len(pieces) + [pl.BlockSpec(memory_space=pl.ANY)] * len(others),
        out_specs=vmem,
        out_shape=jax.ShapeDtypeStruct((rows, *pieces[0].shape[1:]), pieces[0].dtype),
        compiler_params=pltpu.CompilerParams(vmem_limit_bytes=4 * MIB),
        name="assemble",
    )(*pieces, *others)


def times_weight(halves, w_ref):
    x = jnp.concatenate([h[...] for h in halves], axis=0)
    return jnp.dot(x, w_ref[...], preferred_element_type=jnp.float32)


def project_kernel(xa, xb, w_ref, o_ref):
    o_ref[...] = times_weight((xa, xb), w_ref)


def project(xa, xb, w):
    vmem = pl.BlockSpec(memory_space=pltpu.VMEM)
    rows = xa.shape[0] + xb.shape[0]
    return pl.pallas_call(
        project_kernel,
        in_specs=[vmem] * 3,
        out_specs=vmem,
        out_shape=jax.ShapeDtypeStruct((rows, w.shape[1]), jnp.float32),
        compiler_params=pltpu.CompilerParams(vmem_limit_bytes=8 * MIB),
        cost_estimate=pl.CostEstimate(flops=2 * rows * w.shape[0] * w.shape[1], bytes_accessed=MIB, transcendentals=0),
        name="project",
    )(xa, xb, w)


def place_kernel(info, y0, y1, y3, xa, xb, w_ref, o_ref):
    me = tuple(info[i] for i in range(5))
    yl, core = me[3], me[4]
    y2 = times_weight((xa, xb), w_ref)
    for db, y in ((0, y0), (1, y1), (2, y2), (3, y3)):
        for da, dy in itertools.product(range(RING), range(2)):
            z, yh, xx = source(me, da, db, dy)
            row = (((z & 1) ^ core) * 2 + ((z >> 1) ^ yl)) * 64 + yh * 32 + xx * 8
            at = da * 16 + dy * 8
            o_ref[pl.ds(pl.multiple_of(row, 8), 8), :] = y[at : at + 8, :]


def place(info, y0, y1, y3, xa, xb, w):
    vmem = pl.BlockSpec(memory_space=pltpu.VMEM)
    return pl.pallas_call(
        place_kernel,
        in_specs=[pl.BlockSpec(memory_space=pltpu.SMEM)] + [vmem] * 6,
        out_specs=vmem,
        out_shape=jax.ShapeDtypeStruct((RING * y0.shape[0], w.shape[1]), jnp.float32),
        compiler_params=pltpu.CompilerParams(vmem_limit_bytes=8 * MIB),
        name="place",
    )(info, y0, y1, y3, xa, xb, w)


def on_device(queries, keys, values, lengths, start, out_weight):
    nkv = keys.shape[1]
    me = coords(lax.axis_index("cp"), lax.axis_index("tp"))
    info = jnp.concatenate([jnp.stack(me).astype(jnp.int32), lengths, start])
    k = keys.transpose(1, 0, 2)
    v = values.transpose(1, 0, 2)
    q = queries[None]
    q = jnp.concatenate([q, moved(q, yh=1)], axis=0)
    q, k, v, info = together(q, k, v, info)
    vx, kx0, kx1, kx2, kx3 = prepare(info, k, v)
    q2, q1, q3 = (moved(q, a=d) for d in (2, 1, 3))
    q2, vx, kx0, kx1, kx2, kx3 = together(q2, vx, kx0, kx1, kx2, kx3)
    q = assemble([q, q2, q1, q3], moved(q2, core=1))

    q2, q1, q3 = (moved(q, b=d) for d in (2, 1, 3))
    kvs = tuple(range(nkv))
    own = attend(q, kx0, vx, kvs, nb=4)[0]
    q2, own = together(q2, own)
    p2 = attend(q2, kx2, vx, kvs)[0]
    r2 = moved(p2, b=-2)
    q1, q3, p2 = together(q1, q3, p2)
    p1 = attend(q1, kx1, vx, kvs)[0]
    r1 = moved(p1, b=-1)
    q3, p1 = together(q3, p1)
    p3a, p3b = attend(q3, kx3, vx, kvs, outs=2)
    r3a, r3b = moved(p3a, b=-3), moved(p3b, b=-3)
    low = combine(4, (own, 0), (r1, 0), (r2, 0), (r3a, 0))
    s2 = moved(low[2:], a=-2)
    own, low = together(own, low)
    high = combine(4, (own, 4), (r1, 4), (r2, 4), (r3b, 0))
    s1, s3 = moved(high[:2], a=-1), moved(high[2:], a=-3)
    c = combine(2, (low, 0), (s1, 0), (s2, 0), (s3, 0))
    attn = finish(c, moved(c, yh=1))
    x2, x1, x3 = (moved(attn, a=d) for d in (2, 1, 3))
    low = assemble([attn, x1], moved(x2, core=1))
    high = assemble([x2, x3])
    x1a, x3b = moved(low, b=1), moved(high, b=3)
    x1b, x3a = moved(high, b=1), moved(low, b=3)
    x2a, x2b = moved(x1a, b=1), moved(x3b, b=3)
    ys = [project(xa, xb, out_weight) for xa, xb in ((low, high), (x1a, x1b), (x3a, x3b))]
    y = place(info, *ys, x2a, x2b, out_weight)
    y = y[:128] + moved(y[128:], core=1)
    y = y[:64] + moved(y[64:].astype(jnp.bfloat16), yl=1).astype(jnp.float32)
    return y.astype(jnp.bfloat16)


def solution(mesh):
    in_specs = (
        P("cp", "tp", None),
        P("cp", "tp", None),
        P("cp", "tp", None),
        P("cp"),
        P(),
        P("tp", "cp"),
    )
    return jax.shard_map(on_device, mesh=mesh, in_specs=in_specs, out_specs=P("tp", "cp"), check_vma=False)
```

```python
import functools
import itertools
import math

import jax
import jax.numpy as jnp
from jax import lax
from jax.experimental import pallas as pl
from jax.experimental.pallas import tpu as pltpu
from jax.sharding import PartitionSpec as P

NEG = -1e30
BIG = 2.0**100
RING = 4
MIB = 2**20


def coords(cp, tp):
    z, yh, x = cp // 8, (cp // 4) % 2, cp % 4
    yl, core = tp // 2, tp % 2
    return z, yh, x, yl, core


def moved(x, a=0, b=0, yh=0, yl=0, core=0):
    pairs = []
    for cp, tp in itertools.product(range(32), range(4)):
        zi, yhi, xi, yli, ci = coords(cp, tp)
        dz, dx = (a, b) if ci == 0 else (b, a)
        zo, xo = (zi + dz) % RING, (xi + dx) % RING
        yho, ylo, co = yhi ^ yh, yli ^ yl, ci ^ core
        pairs.append((cp * 4 + tp, ((zo * 2 + yho) * 4 + xo) * 4 + ylo * 2 + co))
    return lax.ppermute(x, ("cp", "tp"), pairs)


def together(*arrays):
    return lax.optimization_barrier(arrays)


def source(me, da, db, dy):
    z, yh, x, _, core = me
    dz = jnp.where(core == 0, da, db)
    dx = jnp.where(core == 0, db, da)
    return (z - dz) & (RING - 1), yh ^ dy, (x - dx) & (RING - 1)


def spread(row, eye):
    return jnp.sum(jnp.where(eye, row, 0.0), axis=1, keepdims=True)


def gathered_row(column, eye):
    return jnp.sum(jnp.where(eye, column, 0.0), axis=0, keepdims=True)


def diagonal():
    shape = (128, 128)
    return lax.broadcasted_iota(jnp.int32, shape, 0) == lax.broadcasted_iota(jnp.int32, shape, 1)


def stat_rows(m, l):
    high = l.astype(jnp.bfloat16).astype(jnp.float32)
    return jnp.concatenate([m, high, l - high, jnp.zeros((5, 128), jnp.float32)], axis=0)


def prepare_kernel(info, k_ref, v_ref, vx, *masked):
    nkv, span = k_ref.shape[:2]
    me = tuple(info[i] for i in range(5))
    length, start = info[5], info[6]
    shard = (me[0] * 2 + me[1]) * 4 + me[2]
    lane = lax.broadcasted_iota(jnp.int32, (1, 128), 1)
    da = ((lane >> 5) & 1) | ((lane >> 3) & 2)
    seen = []
    for db in range(RING):
        z, yh, x = source(me, da, db, (lane >> 3) & 1)
        count = start + z * 64 + yh * 32 + x * 8 + (lane & 7) + 1 - shard * span
        seen.append(jnp.where(lane < 64, jnp.minimum(count, length), span))
    chunk = 256

    def fill(i, _):
        at = pl.ds(pl.multiple_of(i * chunk, chunk), chunk)
        slot = i * chunk + lax.broadcasted_iota(jnp.int32, (chunk, 128), 0)
        for count, kx in zip(seen, masked):
            mask = jnp.where(slot >= count, NEG, 0.0).astype(jnp.bfloat16)
            for kv in range(nkv):
                kx[kv, at, :128] = k_ref[kv, at, :]
                kx[kv, at, 128:] = mask
        for kv in range(nkv):
            vx[kv, at, :128] = v_ref[kv, at, :]
            vx[kv, at, 128:] = jnp.ones((chunk, 128), jnp.bfloat16)
        return 0

    lax.fori_loop(0, span // chunk, fill, 0)


def prepare(info, k, v):
    vmem = pl.BlockSpec(memory_space=pltpu.VMEM)
    count = 1 + RING
    return pl.pallas_call(
        prepare_kernel,
        in_specs=[pl.BlockSpec(memory_space=pltpu.SMEM), vmem, vmem],
        out_specs=[vmem] * count,
        out_shape=[jax.ShapeDtypeStruct((*k.shape[:2], 256), jnp.bfloat16)] * count,
        compiler_params=pltpu.CompilerParams(vmem_limit_bytes=4 * MIB),
        name="prepare",
    )(info, k, v)


def attend_kernel(q_ref, kx, vx, o_ref, *, kvs, first, nb, tile, scale):
    step = pl.program_id(0)
    span = vx.shape[1]
    eye = diagonal()

    def rows_of(b, count):
        row = lax.broadcasted_iota(jnp.int32, (count * 128, 128), 0)
        lane = lax.broadcasted_iota(jnp.int32, (count * 128, 128), 1)
        token = (first + step * nb + b + (row >> 7)) * 8 + ((row >> 4) & 7)
        hot = jnp.where(lane == token, 1.0, 0.0).astype(jnp.bfloat16)
        heads = [q_ref[pl.ds(b, count), :, kv * 16 : (kv + 1) * 16, :].reshape(count * 128, 128) for kv in kvs]
        return [jnp.concatenate([h, hot], axis=1) for h in heads]

    def scores(q, kv, t):
        return lax.dot_general(
            q, kx[kv, pl.ds(t, tile), :], (((1,), (1,)), ((), ())), preferred_element_type=jnp.float32
        )

    def point(m):
        return jnp.maximum(m * scale, 0.01 * NEG).astype(jnp.bfloat16).astype(jnp.float32)

    def put(b, r, results):
        stats = []
        for i, (m, acc) in enumerate(results):
            o_ref[b, i * 128 : (i + 1) * 128, :] = acc[r, :128].astype(jnp.bfloat16)
            stats.append(stat_rows(gathered_row(m[r], eye), gathered_row(acc[r, 128:], eye)))
        o_ref[b, len(results) * 128 :, :] = jnp.concatenate(stats, axis=0).astype(jnp.bfloat16)

    ok, results = [], []
    for q, kv in zip(rows_of(0, nb), kvs):
        s0 = scores(q, kv, 0)
        m = point(jnp.max(s0, axis=1, keepdims=True))
        p = []
        for t in range(0, span, tile):
            s = s0 if t == 0 else scores(q, kv, t)
            p.append(jnp.exp2(s * scale - m).astype(jnp.bfloat16))
        acc = jnp.dot(jnp.concatenate(p, axis=1), vx[kv], preferred_element_type=jnp.float32)
        ok.append(jnp.min(jnp.where(acc[:, 128:] < BIG, 1.0, 0.0)))
        results.append((m, acc))
    for b in range(nb):
        put(b, slice(b * 128, (b + 1) * 128), results)

    @pl.when(functools.reduce(jnp.minimum, ok) < 0.5)
    def _():
        def block(b, _):
            results = []
            for q, kv in zip(rows_of(b, 1), kvs):

                def top(n, m):
                    s = scores(q, kv, pl.multiple_of(n * tile, tile))
                    return jnp.maximum(m, jnp.max(s, axis=1, keepdims=True))

                m = point(lax.fori_loop(0, span // tile, top, jnp.full((128, 1), NEG, jnp.float32)))

                def add(n, acc):
                    t = pl.multiple_of(n * tile, tile)
                    p = jnp.exp2(scores(q, kv, t) * scale - m).astype(jnp.bfloat16)
                    return acc + jnp.dot(p, vx[kv, pl.ds(t, tile), :], preferred_element_type=jnp.float32)

                results.append((m, lax.fori_loop(0, span // tile, add, jnp.zeros((128, 256), jnp.float32))))
            put(b, slice(0, 128), results)
            return 0

        lax.fori_loop(0, nb, block, 0)


def attend(q, kx, vx, kvs, first=0, blocks=8, nb=None):
    span = vx.shape[1]
    nb, tile = nb or blocks, 256
    skip = first // nb
    vmem = pl.BlockSpec(memory_space=pltpu.VMEM)
    return pl.pallas_call(
        functools.partial(
            attend_kernel, kvs=kvs, first=first, nb=nb, tile=tile, scale=math.log2(math.e) / math.sqrt(128)
        ),
        grid=(blocks // nb,),
        in_specs=[pl.BlockSpec((nb, *q.shape[1:]), lambda i: (skip + i, 0, 0, 0)), vmem, vmem],
        out_specs=pl.BlockSpec((nb, len(kvs) * 136, 128), lambda i: (i, 0, 0)),
        out_shape=jax.ShapeDtypeStruct((blocks, len(kvs) * 136, 128), jnp.bfloat16),
        compiler_params=pltpu.CompilerParams(vmem_limit_bytes=20 * MIB, dimension_semantics=("arbitrary",)),
        cost_estimate=pl.CostEstimate(
            flops=8 * blocks * len(kvs) * 128 * span * 128,
            bytes_accessed=4 * MIB,
            transcendentals=blocks * len(kvs) * 128 * span,
        ),
        name="attend_plane",
    )(q, kx, vx)


def merged(parts, kv, nkv, eye):
    stats = [p[nkv * 128 :, :].astype(jnp.float32)[kv * 8 : kv * 8 + 8] for p in parts]
    m = functools.reduce(jnp.maximum, [s[0:1] for s in stats])
    total = jnp.zeros((1, 128), jnp.float32)
    out = jnp.zeros((128, 128), jnp.float32)
    for p, s in zip(parts, stats):
        factor = jnp.exp2(s[0:1] - m)
        total = total + factor * (s[1:2] + s[2:3])
        out = out + spread(factor, eye) * p[kv * 128 : (kv + 1) * 128, :].astype(jnp.float32)
    return out, m, total


def combine_kernel(*refs, starts):
    parts, o_ref = refs[:-1], refs[-1]
    nkv = o_ref.shape[1] // 136
    eye = diagonal()
    for b in range(o_ref.shape[0]):
        here = [part.at[at + b] for part, at in zip(parts, starts)]
        stats = []
        for kv in range(nkv):
            out, m, total = merged(here, kv, nkv, eye)
            o_ref[b, kv * 128 : (kv + 1) * 128, :] = out.astype(jnp.bfloat16)
            stats.append(stat_rows(m, total))
        o_ref[b, nkv * 128 :, :] = jnp.concatenate(stats, axis=0).astype(jnp.bfloat16)


def combine(blocks, *parts):
    vmem = pl.BlockSpec(memory_space=pltpu.VMEM)
    arrays, starts = zip(*parts)
    return pl.pallas_call(
        functools.partial(combine_kernel, starts=starts),
        in_specs=[vmem] * len(arrays),
        out_specs=vmem,
        out_shape=jax.ShapeDtypeStruct((blocks, *arrays[0].shape[1:]), jnp.bfloat16),
        compiler_params=pltpu.CompilerParams(vmem_limit_bytes=8 * MIB),
        name="combine",
    )(*arrays)


def finish_kernel(mine, theirs, o_ref, rows):
    eye = diagonal()
    nkv = mine.shape[1] // 136
    for kv in range(nkv):
        for dy in range(2):
            out, _, total = merged([mine.at[dy], theirs.at[1 - dy]], kv, nkv, eye)
            rows[kv, dy] = out * spread(1.0 / total, eye)
    for kv, h in itertools.product(range(nkv), range(16)):
        c = (kv * 16 + h) * 128
        both = [rows[kv, dy, pl.ds(h, 8, stride=16), :] for dy in range(2)]
        o_ref[:, c : c + 128] = jnp.concatenate(both, axis=0).astype(jnp.bfloat16)


def finish(mine, theirs):
    vmem = pl.BlockSpec(memory_space=pltpu.VMEM)
    nkv = mine.shape[1] // 136
    return pl.pallas_call(
        finish_kernel,
        in_specs=[vmem, vmem],
        out_specs=vmem,
        scratch_shapes=[pltpu.VMEM((nkv, 2, 128, 128), jnp.float32)],
        compiler_params=pltpu.CompilerParams(vmem_limit_bytes=4 * MIB),
        out_shape=jax.ShapeDtypeStruct((16, nkv * 2048), jnp.bfloat16),
        name="finish",
    )(mine, theirs)


def assemble_kernel(*refs, count):
    at = 0
    for x in refs[:count]:
        refs[-1][at : at + x.shape[0]] = x[...]
        at += x.shape[0]


def assemble(pieces, *others):
    vmem = pl.BlockSpec(memory_space=pltpu.VMEM)
    rows = sum(p.shape[0] for p in pieces)
    return pl.pallas_call(
        functools.partial(assemble_kernel, count=len(pieces)),
        in_specs=[vmem] * len(pieces) + [pl.BlockSpec(memory_space=pl.ANY)] * len(others),
        out_specs=vmem,
        out_shape=jax.ShapeDtypeStruct((rows, *pieces[0].shape[1:]), pieces[0].dtype),
        compiler_params=pltpu.CompilerParams(vmem_limit_bytes=4 * MIB),
        name="assemble",
    )(*pieces, *others)


def times_weight(halves, w_ref):
    x = jnp.concatenate([h[...] for h in halves], axis=0)
    return jnp.dot(x, w_ref[...], preferred_element_type=jnp.float32)


def project_kernel(xa, xb, w_ref, o_ref):
    o_ref[...] = times_weight((xa, xb), w_ref)


def project(xa, xb, w):
    vmem = pl.BlockSpec(memory_space=pltpu.VMEM)
    rows = xa.shape[0] + xb.shape[0]
    return pl.pallas_call(
        project_kernel,
        in_specs=[vmem] * 3,
        out_specs=vmem,
        out_shape=jax.ShapeDtypeStruct((rows, w.shape[1]), jnp.float32),
        compiler_params=pltpu.CompilerParams(vmem_limit_bytes=8 * MIB),
        cost_estimate=pl.CostEstimate(flops=2 * rows * w.shape[0] * w.shape[1], bytes_accessed=MIB, transcendentals=0),
        name="project",
    )(xa, xb, w)


def place_kernel(info, y0, y1, y3, xa, xb, w_ref, o_ref):
    me = tuple(info[i] for i in range(5))
    yl, core = me[3], me[4]
    y2 = times_weight((xa, xb), w_ref)
    for db, y in ((0, y0), (1, y1), (2, y2), (3, y3)):
        for da, dy in itertools.product(range(RING), range(2)):
            z, yh, xx = source(me, da, db, dy)
            row = (((z & 1) ^ core) * 2 + ((z >> 1) ^ yl)) * 64 + yh * 32 + xx * 8
            at = da * 16 + dy * 8
            o_ref[pl.ds(pl.multiple_of(row, 8), 8), :] = y[at : at + 8, :]


def place(info, y0, y1, y3, xa, xb, w):
    vmem = pl.BlockSpec(memory_space=pltpu.VMEM)
    return pl.pallas_call(
        place_kernel,
        in_specs=[pl.BlockSpec(memory_space=pltpu.SMEM)] + [vmem] * 6,
        out_specs=vmem,
        out_shape=jax.ShapeDtypeStruct((RING * y0.shape[0], w.shape[1]), jnp.float32),
        compiler_params=pltpu.CompilerParams(vmem_limit_bytes=8 * MIB),
        name="place",
    )(info, y0, y1, y3, xa, xb, w)


def on_device(queries, keys, values, lengths, start, out_weight):
    nkv = keys.shape[1]
    me = coords(lax.axis_index("cp"), lax.axis_index("tp"))
    info = jnp.concatenate([jnp.stack(me).astype(jnp.int32), lengths, start])
    k = keys.transpose(1, 0, 2)
    v = values.transpose(1, 0, 2)
    q = queries[None]
    q = jnp.concatenate([q, moved(q, yh=1)], axis=0)
    q, k, v, info = together(q, k, v, info)
    vx, kx0, kx1, kx2, kx3 = prepare(info, k, v)
    q2, q1, q3 = (moved(q, a=d) for d in (2, 1, 3))
    q2, vx, kx0, kx1, kx2, kx3 = together(q2, vx, kx0, kx1, kx2, kx3)
    q = assemble([q, q2, q1, q3], moved(q2, core=1))

    q2, q1, q3 = (moved(q, b=d) for d in (2, 1, 3))
    kvs = tuple(range(nkv))
    own = attend(q, kx0, vx, kvs, nb=4)
    q2, own = together(q2, own)
    p2 = attend(q2, kx2, vx, kvs)
    r2 = moved(p2, b=-2)
    q1, q3, p2 = together(q1, q3, p2)
    p1 = attend(q1, kx1, vx, kvs)
    r1 = moved(p1, b=-1)
    q3, p1 = together(q3, p1)
    p3a = attend(q3, kx3, vx, kvs, 0, 4)
    r3a = moved(p3a, b=-3)
    q3, p3a, r2 = together(q3, p3a, r2)
    p3b = attend(q3, kx3, vx, kvs, 4, 4)
    r3b = moved(p3b, b=-3)
    low = combine(4, (own, 0), (r1, 0), (r2, 0), (r3a, 0))
    s2 = moved(low[2:], a=-2)
    high = combine(4, (own, 4), (r1, 4), (r2, 4), (r3b, 0))
    s1, s3 = moved(high[:2], a=-1), moved(high[2:], a=-3)
    c = combine(2, (low, 0), (s1, 0), (s2, 0), (s3, 0))
    attn = finish(c, moved(c, yh=1))
    x1, x2, x3 = (moved(attn, a=d) for d in (1, 2, 3))
    low = assemble([attn, x1], moved(x1, core=1))
    high = assemble([x2, x3], low)
    x1a, x3b = moved(low, b=1), moved(high, b=3)
    x1b, x3a = moved(high, b=1), moved(low, b=3)
    x2a, x2b = moved(x1a, b=1), moved(x3b, b=3)
    ys = [project(xa, xb, out_weight) for xa, xb in ((low, high), (x1a, x1b), (x3a, x3b))]
    y = place(info, *ys, x2a, x2b, out_weight)
    y = y[:128] + moved(y[128:], core=1)
    y = y[:64] + moved(y[64:].astype(jnp.bfloat16), yl=1).astype(jnp.float32)
    return y.astype(jnp.bfloat16)


def solution(mesh):
    in_specs = (
        P("cp", "tp", None),
        P("cp", "tp", None),
        P("cp", "tp", None),
        P("cp"),
        P(),
        P("tp", "cp"),
    )
    return jax.shard_map(on_device, mesh=mesh, in_specs=in_specs, out_specs=P("tp", "cp"), check_vma=False)
```

```python
import functools
import itertools
import math

import jax
import jax.numpy as jnp
from jax import lax
from jax.experimental import pallas as pl
from jax.experimental.pallas import tpu as pltpu
from jax.sharding import PartitionSpec as P

NEG = -1e30
BIG = 2.0**100
RING = 4
MIB = 2**20


def coords(cp, tp):
    z, yh, x = cp // 8, (cp // 4) % 2, cp % 4
    yl, core = tp // 2, tp % 2
    return z, yh, x, yl, core


def moved(x, a=0, b=0, yh=0, yl=0, core=0):
    pairs = []
    for cp, tp in itertools.product(range(32), range(4)):
        zi, yhi, xi, yli, ci = coords(cp, tp)
        dz, dx = (a, b) if ci == 0 else (b, a)
        zo, xo = (zi + dz) % RING, (xi + dx) % RING
        yho, ylo, co = yhi ^ yh, yli ^ yl, ci ^ core
        pairs.append((cp * 4 + tp, ((zo * 2 + yho) * 4 + xo) * 4 + ylo * 2 + co))
    return lax.ppermute(x, ("cp", "tp"), pairs)


def together(*arrays):
    return lax.optimization_barrier(arrays)


def source(me, da, db, dy):
    z, yh, x, _, core = me
    dz = jnp.where(core == 0, da, db)
    dx = jnp.where(core == 0, db, da)
    return (z - dz) & (RING - 1), yh ^ dy, (x - dx) & (RING - 1)


def spread(row, eye):
    return jnp.sum(jnp.where(eye, row, 0.0), axis=1, keepdims=True)


def gathered_row(column, eye):
    return jnp.sum(jnp.where(eye, column, 0.0), axis=0, keepdims=True)


def diagonal():
    shape = (128, 128)
    return lax.broadcasted_iota(jnp.int32, shape, 0) == lax.broadcasted_iota(jnp.int32, shape, 1)


def stat_rows(m, l):
    high = l.astype(jnp.bfloat16).astype(jnp.float32)
    return jnp.concatenate([m, high, l - high, jnp.zeros((5, 128), jnp.float32)], axis=0)


def prepare_kernel(info, k_ref, v_ref, vx, *masked):
    nkv, span = k_ref.shape[:2]
    me = tuple(info[i] for i in range(5))
    length, start = info[5], info[6]
    shard = (me[0] * 2 + me[1]) * 4 + me[2]
    lane = lax.broadcasted_iota(jnp.int32, (1, 128), 1)
    da = ((lane >> 5) & 1) | ((lane >> 3) & 2)
    seen = []
    for db in range(RING):
        z, yh, x = source(me, da, db, (lane >> 3) & 1)
        count = start + z * 64 + yh * 32 + x * 8 + (lane & 7) + 1 - shard * span
        seen.append(jnp.where(lane < 64, jnp.minimum(count, length), span))
    chunk = 256

    def fill(i, _):
        at = pl.ds(pl.multiple_of(i * chunk, chunk), chunk)
        slot = i * chunk + lax.broadcasted_iota(jnp.int32, (chunk, 128), 0)
        for count, kx in zip(seen, masked):
            mask = jnp.where(slot >= count, NEG, 0.0).astype(jnp.bfloat16)
            for kv in range(nkv):
                kx[kv, at, :128] = k_ref[kv, at, :]
                kx[kv, at, 128:] = mask
        for kv in range(nkv):
            vx[kv, at, :128] = v_ref[kv, at, :]
            vx[kv, at, 128:] = jnp.ones((chunk, 128), jnp.bfloat16)
        return 0

    lax.fori_loop(0, span // chunk, fill, 0)


def prepare(info, k, v):
    vmem = pl.BlockSpec(memory_space=pltpu.VMEM)
    count = 1 + RING
    return pl.pallas_call(
        prepare_kernel,
        in_specs=[pl.BlockSpec(memory_space=pltpu.SMEM), vmem, vmem],
        out_specs=[vmem] * count,
        out_shape=[jax.ShapeDtypeStruct((*k.shape[:2], 256), jnp.bfloat16)] * count,
        compiler_params=pltpu.CompilerParams(vmem_limit_bytes=4 * MIB),
        name="prepare",
    )(info, k, v)


def attend_kernel(q_ref, kx, vx, o_ref, *, kvs, first, nb, tile, scale):
    step = pl.program_id(0)
    span = vx.shape[1]
    eye = diagonal()

    def rows_of(b, count):
        row = lax.broadcasted_iota(jnp.int32, (count * 128, 128), 0)
        lane = lax.broadcasted_iota(jnp.int32, (count * 128, 128), 1)
        token = (first + step * nb + b + (row >> 7)) * 8 + ((row >> 4) & 7)
        hot = jnp.where(lane == token, 1.0, 0.0).astype(jnp.bfloat16)
        heads = [q_ref[pl.ds(b, count), :, kv * 16 : (kv + 1) * 16, :].reshape(count * 128, 128) for kv in kvs]
        return [jnp.concatenate([h, hot], axis=1) for h in heads]

    def scores(q, kv, t):
        return lax.dot_general(
            q, kx[kv, pl.ds(t, tile), :], (((1,), (1,)), ((), ())), preferred_element_type=jnp.float32
        )

    def point(m):
        return jnp.maximum(m * scale, 0.01 * NEG).astype(jnp.bfloat16).astype(jnp.float32)

    def put(b, r, results):
        stats = []
        for i, (m, acc) in enumerate(results):
            o_ref[b, i * 128 : (i + 1) * 128, :] = acc[r, :128].astype(jnp.bfloat16)
            stats.append(stat_rows(gathered_row(m[r], eye), gathered_row(acc[r, 128:], eye)))
        o_ref[b, len(results) * 128 :, :] = jnp.concatenate(stats, axis=0).astype(jnp.bfloat16)

    ok, results = [], []
    for q, kv in zip(rows_of(0, nb), kvs):
        s0 = scores(q, kv, 0)
        m = point(jnp.max(s0, axis=1, keepdims=True))
        p = []
        for t in range(0, span, tile):
            s = s0 if t == 0 else scores(q, kv, t)
            p.append(jnp.exp2(s * scale - m).astype(jnp.bfloat16))
        acc = jnp.dot(jnp.concatenate(p, axis=1), vx[kv], preferred_element_type=jnp.float32)
        ok.append(jnp.min(jnp.where(acc[:, 128:] < BIG, 1.0, 0.0)))
        results.append((m, acc))
    for b in range(nb):
        put(b, slice(b * 128, (b + 1) * 128), results)

    @pl.when(functools.reduce(jnp.minimum, ok) < 0.5)
    def _():
        def block(b, _):
            results = []
            for q, kv in zip(rows_of(b, 1), kvs):

                def top(n, m):
                    s = scores(q, kv, pl.multiple_of(n * tile, tile))
                    return jnp.maximum(m, jnp.max(s, axis=1, keepdims=True))

                m = point(lax.fori_loop(0, span // tile, top, jnp.full((128, 1), NEG, jnp.float32)))

                def add(n, acc):
                    t = pl.multiple_of(n * tile, tile)
                    p = jnp.exp2(scores(q, kv, t) * scale - m).astype(jnp.bfloat16)
                    return acc + jnp.dot(p, vx[kv, pl.ds(t, tile), :], preferred_element_type=jnp.float32)

                results.append((m, lax.fori_loop(0, span // tile, add, jnp.zeros((128, 256), jnp.float32))))
            put(b, slice(0, 128), results)
            return 0

        lax.fori_loop(0, nb, block, 0)


def attend(q, kx, vx, kvs, first=0, blocks=8, nb=None):
    span = vx.shape[1]
    nb, tile = nb or blocks, 256
    skip = first // nb
    vmem = pl.BlockSpec(memory_space=pltpu.VMEM)
    return pl.pallas_call(
        functools.partial(
            attend_kernel, kvs=kvs, first=first, nb=nb, tile=tile, scale=math.log2(math.e) / math.sqrt(128)
        ),
        grid=(blocks // nb,),
        in_specs=[pl.BlockSpec((nb, *q.shape[1:]), lambda i: (skip + i, 0, 0, 0)), vmem, vmem],
        out_specs=pl.BlockSpec((nb, len(kvs) * 136, 128), lambda i: (i, 0, 0)),
        out_shape=jax.ShapeDtypeStruct((blocks, len(kvs) * 136, 128), jnp.bfloat16),
        compiler_params=pltpu.CompilerParams(vmem_limit_bytes=20 * MIB, dimension_semantics=("arbitrary",)),
        cost_estimate=pl.CostEstimate(
            flops=8 * blocks * len(kvs) * 128 * span * 128,
            bytes_accessed=4 * MIB,
            transcendentals=blocks * len(kvs) * 128 * span,
        ),
        name="attend_plane",
    )(q, kx, vx)


def merged(parts, kv, nkv, eye):
    stats = [p[nkv * 128 :, :].astype(jnp.float32)[kv * 8 : kv * 8 + 8] for p in parts]
    m = functools.reduce(jnp.maximum, [s[0:1] for s in stats])
    total = jnp.zeros((1, 128), jnp.float32)
    out = jnp.zeros((128, 128), jnp.float32)
    for p, s in zip(parts, stats):
        factor = jnp.exp2(s[0:1] - m)
        total = total + factor * (s[1:2] + s[2:3])
        out = out + spread(factor, eye) * p[kv * 128 : (kv + 1) * 128, :].astype(jnp.float32)
    return out, m, total


def combine_kernel(*refs, starts):
    parts, o_ref = refs[:-1], refs[-1]
    nkv = o_ref.shape[1] // 136
    eye = diagonal()
    for b in range(o_ref.shape[0]):
        here = [part.at[at + b] for part, at in zip(parts, starts)]
        stats = []
        for kv in range(nkv):
            out, m, total = merged(here, kv, nkv, eye)
            o_ref[b, kv * 128 : (kv + 1) * 128, :] = out.astype(jnp.bfloat16)
            stats.append(stat_rows(m, total))
        o_ref[b, nkv * 128 :, :] = jnp.concatenate(stats, axis=0).astype(jnp.bfloat16)


def combine(blocks, *parts):
    vmem = pl.BlockSpec(memory_space=pltpu.VMEM)
    arrays, starts = zip(*parts)
    return pl.pallas_call(
        functools.partial(combine_kernel, starts=starts),
        in_specs=[vmem] * len(arrays),
        out_specs=vmem,
        out_shape=jax.ShapeDtypeStruct((blocks, *arrays[0].shape[1:]), jnp.bfloat16),
        compiler_params=pltpu.CompilerParams(vmem_limit_bytes=8 * MIB),
        name="combine",
    )(*arrays)


def finish_kernel(mine, theirs, o_ref, rows):
    eye = diagonal()
    nkv = mine.shape[1] // 136
    for kv in range(nkv):
        for dy in range(2):
            out, _, total = merged([mine.at[dy], theirs.at[1 - dy]], kv, nkv, eye)
            rows[kv, dy] = out * spread(1.0 / total, eye)
    for kv, h in itertools.product(range(nkv), range(16)):
        c = (kv * 16 + h) * 128
        both = [rows[kv, dy, pl.ds(h, 8, stride=16), :] for dy in range(2)]
        o_ref[:, c : c + 128] = jnp.concatenate(both, axis=0).astype(jnp.bfloat16)


def finish(mine, theirs):
    vmem = pl.BlockSpec(memory_space=pltpu.VMEM)
    nkv = mine.shape[1] // 136
    return pl.pallas_call(
        finish_kernel,
        in_specs=[vmem, vmem],
        out_specs=vmem,
        scratch_shapes=[pltpu.VMEM((nkv, 2, 128, 128), jnp.float32)],
        compiler_params=pltpu.CompilerParams(vmem_limit_bytes=4 * MIB),
        out_shape=jax.ShapeDtypeStruct((16, nkv * 2048), jnp.bfloat16),
        name="finish",
    )(mine, theirs)


def assemble_kernel(*refs, count):
    at = 0
    for x in refs[:count]:
        refs[-1][at : at + x.shape[0]] = x[...]
        at += x.shape[0]


def assemble(pieces, *others):
    vmem = pl.BlockSpec(memory_space=pltpu.VMEM)
    rows = sum(p.shape[0] for p in pieces)
    return pl.pallas_call(
        functools.partial(assemble_kernel, count=len(pieces)),
        in_specs=[vmem] * len(pieces) + [pl.BlockSpec(memory_space=pl.ANY)] * len(others),
        out_specs=vmem,
        out_shape=jax.ShapeDtypeStruct((rows, *pieces[0].shape[1:]), pieces[0].dtype),
        compiler_params=pltpu.CompilerParams(vmem_limit_bytes=4 * MIB),
        name="assemble",
    )(*pieces, *others)


def times_weight(halves, w_ref):
    x = jnp.concatenate([h[...] for h in halves], axis=0)
    return jnp.dot(x, w_ref[...], preferred_element_type=jnp.float32)


def project_kernel(xa, xb, w_ref, o_ref):
    o_ref[...] = times_weight((xa, xb), w_ref)


def project(xa, xb, w):
    vmem = pl.BlockSpec(memory_space=pltpu.VMEM)
    rows = xa.shape[0] + xb.shape[0]
    return pl.pallas_call(
        project_kernel,
        in_specs=[vmem] * 3,
        out_specs=vmem,
        out_shape=jax.ShapeDtypeStruct((rows, w.shape[1]), jnp.float32),
        compiler_params=pltpu.CompilerParams(vmem_limit_bytes=8 * MIB),
        cost_estimate=pl.CostEstimate(flops=2 * rows * w.shape[0] * w.shape[1], bytes_accessed=MIB, transcendentals=0),
        name="project",
    )(xa, xb, w)


def place_kernel(info, y0, y1, y3, xa, xb, w_ref, o_ref):
    me = tuple(info[i] for i in range(5))
    yl, core = me[3], me[4]
    y2 = times_weight((xa, xb), w_ref)
    for db, y in ((0, y0), (1, y1), (2, y2), (3, y3)):
        for da, dy in itertools.product(range(RING), range(2)):
            z, yh, xx = source(me, da, db, dy)
            row = (((z & 1) ^ core) * 2 + ((z >> 1) ^ yl)) * 64 + yh * 32 + xx * 8
            at = da * 16 + dy * 8
            o_ref[pl.ds(pl.multiple_of(row, 8), 8), :] = y[at : at + 8, :]


def place(info, y0, y1, y3, xa, xb, w):
    vmem = pl.BlockSpec(memory_space=pltpu.VMEM)
    return pl.pallas_call(
        place_kernel,
        in_specs=[pl.BlockSpec(memory_space=pltpu.SMEM)] + [vmem] * 6,
        out_specs=vmem,
        out_shape=jax.ShapeDtypeStruct((RING * y0.shape[0], w.shape[1]), jnp.float32),
        compiler_params=pltpu.CompilerParams(vmem_limit_bytes=8 * MIB),
        name="place",
    )(info, y0, y1, y3, xa, xb, w)


def on_device(queries, keys, values, lengths, start, out_weight):
    nkv = keys.shape[1]
    me = coords(lax.axis_index("cp"), lax.axis_index("tp"))
    info = jnp.concatenate([jnp.stack(me).astype(jnp.int32), lengths, start])
    k = keys.transpose(1, 0, 2)
    v = values.transpose(1, 0, 2)
    q = queries[None]
    q = jnp.concatenate([q, moved(q, yh=1)], axis=0)
    q, k, v, info = together(q, k, v, info)
    vx, kx0, kx1, kx2, kx3 = prepare(info, k, v)
    q2, q1, q3 = (moved(q, a=d) for d in (2, 1, 3))
    q2, vx, kx0, kx1, kx2, kx3 = together(q2, vx, kx0, kx1, kx2, kx3)
    q = assemble([q, q2, q1, q3], moved(q2, core=1))

    q2, q1, q3 = (moved(q, b=d) for d in (2, 1, 3))
    kvs = tuple(range(nkv))
    own = attend(q, kx0, vx, kvs, nb=4)
    q2, own = together(q2, own)
    p2 = attend(q2, kx2, vx, kvs)
    r2 = moved(p2, b=-2)
    q1, q3, p2 = together(q1, q3, p2)
    p1 = attend(q1, kx1, vx, kvs)
    r1 = moved(p1, b=-1)
    q3, p1 = together(q3, p1)
    p3a = attend(q3, kx3, vx, kvs, 0, 4)
    r3a = moved(p3a, b=-3)
    q3, p3a, r2 = together(q3, p3a, r2)
    p3b = attend(q3, kx3, vx, kvs, 4, 4)
    r3b = moved(p3b, b=-3)
    low = combine(4, (own, 0), (r1, 0), (r2, 0), (r3a, 0))
    s2 = moved(low[2:], a=-2)
    high = combine(4, (own, 4), (r1, 4), (r2, 4), (r3b, 0))
    s1, s3 = moved(high[:2], a=-1), moved(high[2:], a=-3)
    c = combine(2, (low, 0), (s1, 0), (s2, 0), (s3, 0))
    attn = finish(c, moved(c, yh=1))
    x2, x1, x3 = (moved(attn, a=d) for d in (2, 1, 3))
    low = assemble([attn, x1], moved(x2, core=1))
    high = assemble([x2, x3])
    x1a, x3b = moved(low, b=1), moved(high, b=3)
    x1b, x3a = moved(high, b=1), moved(low, b=3)
    x2a, x2b = moved(x1a, b=1), moved(x3b, b=3)
    ys = [project(xa, xb, out_weight) for xa, xb in ((low, high), (x1a, x1b), (x3a, x3b))]
    y = place(info, *ys, x2a, x2b, out_weight)
    y = y[:128] + moved(y[128:].astype(jnp.bfloat16), core=1).astype(jnp.float32)
    y = y[:64] + moved(y[64:].astype(jnp.bfloat16), yl=1).astype(jnp.float32)
    return y.astype(jnp.bfloat16)


def solution(mesh):
    in_specs = (
        P("cp", "tp", None),
        P("cp", "tp", None),
        P("cp", "tp", None),
        P("cp"),
        P(),
        P("tp", "cp"),
    )
    return jax.shard_map(on_device, mesh=mesh, in_specs=in_specs, out_specs=P("tp", "cp"), check_vma=False)
```
